256 devices in a mesh: seq: 64 (over x, z, core), head: 4 (over y).
Axes of the slice: x: 4, y: 4, z: 8, core: 2. Of those that a mesh axis runs over, the one named last changes fastest.
Arguments:
- mla_queries: bfloat16 [2, 4096, 36864], P(None, 'seq', 'head'), may hold values from -30 to 30
- latent_keys: bfloat16 [4096, 1152], P('seq'), may hold values from -20 to 20
- index_queries: bfloat16 [2, 4096, 8192], P(None, 'seq'), may hold values from -64 to 64
- index_keys: bfloat16 [4096, 256], P('seq'), may hold values from -20 to 20
- head_weights: float32 [4096, 128], P('seq'), may hold values from -6 to 6
- block_order: int32 [128], replicated, may hold values from 0 to 127, as said below
Outputs:
- key_grad: float32 [4096, 256], P(('seq', 'head'))
The draws below stay inside these ranges and needn't reach their ends.
Inputs may be any that keep to these rules, and one draw needn't show every extreme that they name: Index d of seq holds, in each sequence, half-block block_order[2 * d] in its first 32 rows and half-block block_order[2 * d + 1] in its last 32 rows; block_order[2 * d] < 64 and block_order[2 * d] + block_order[2 * d + 1] = 127; every half-block number appears once.
All inputs are finite; a program needn't handle non-finite values.
Results may differ from the reference program's by a relative error of at most 0.002.
Values may be sent and summed in bfloat16 or wider, within the bound.
A program may use at most 128 MiB of HBM per device.

```python
import jax
import jax.numpy as jnp
from jax import lax

MLA_HEADS = 64
KD = 576
IDX_HEADS = 64
IDX_DIM = 128
SEQS = 2
TOK_DEV = 64
HALF = 32
LENGTH = 4096
HALVES = 128


def spread_scales(key, array_shape, lower_end, upper_end):
    return lower_end * jnp.exp(jax.random.uniform(key, array_shape, jnp.float32) * jnp.log(upper_end / lower_end))


def draw_mla_queries(key, part):
    key = jax.random.fold_in(key, 1)
    noise_key, scale_key = jax.random.split(key, 2)
    scales = spread_scales(scale_key, (SEQS, LENGTH, MLA_HEADS, 1), 0.1, 1.0)
    values = scales * jax.random.normal(noise_key, (SEQS, LENGTH, MLA_HEADS, KD), jnp.float32)
    return jnp.clip(values, -30.0, 30.0).reshape(SEQS, LENGTH, MLA_HEADS * KD).astype(jnp.bfloat16)


def draw_latent_keys(key, part):
    key = jax.random.fold_in(key, 2)
    noise_key, scale_key = jax.random.split(key)
    scales = spread_scales(scale_key, (LENGTH, SEQS, 1), 0.3, 3.0)
    values = scales * jax.random.normal(noise_key, (LENGTH, SEQS, KD), jnp.float32)
    return jnp.clip(values, -20.0, 20.0).reshape(LENGTH, SEQS * KD).astype(jnp.bfloat16)


def draw_index_queries(key, part):
    key = jax.random.fold_in(key, 3)
    noise_key, scale_key = jax.random.split(key, 2)
    scales = spread_scales(scale_key, (SEQS, LENGTH, IDX_HEADS, 1), 0.3, 3.0)
    values = scales * jax.random.normal(noise_key, (SEQS, LENGTH, IDX_HEADS, IDX_DIM), jnp.float32)
    return jnp.clip(values, -64.0, 64.0).reshape(SEQS, LENGTH, IDX_HEADS * IDX_DIM).astype(jnp.bfloat16)


def draw_index_keys(key, part):
    key = jax.random.fold_in(key, 4)
    noise_key, scale_key = jax.random.split(key)
    scales = spread_scales(scale_key, (LENGTH, SEQS, 1), 0.3, 3.0)
    values = scales * jax.random.normal(noise_key, (LENGTH, SEQS, IDX_DIM), jnp.float32)
    return jnp.clip(values, -20.0, 20.0).reshape(LENGTH, SEQS * IDX_DIM).astype(jnp.bfloat16)


def draw_block_order(key, part):
    key = jax.random.fold_in(key, 5)
    device_total = HALVES // 2
    earlier = jax.random.permutation(key, jnp.arange(device_total, dtype=jnp.int32))
    later = HALVES - 1 - earlier
    return jnp.stack([earlier, later], axis=1).reshape(HALVES).astype(jnp.int32)


def block_scale(rng, dims, cuts, low, largest):
    gain, own = 1.0, jax.random.fold_in(rng, 6)
    for dim, blocks in cuts:
        draws = jnp.exp(jax.random.uniform(jax.random.fold_in(own, dim), (blocks,), jnp.float32, low / len(cuts), largest / len(cuts)))
        gain = gain * jnp.repeat(draws, dims[dim] // blocks).reshape([-1 if axis == dim else 1 for axis in range(len(dims))])
    return gain


def bell_draw(own_key, extent, deviation, bound, cuts=(), kind=jnp.bfloat16):
    entries = deviation * jax.random.normal(own_key, extent, jnp.float32)
    if cuts:
        entries = entries * block_scale(own_key, extent, cuts, -0.22, 0.18)
    return jnp.clip(entries, -bound, bound).astype(kind)


def setup_inputs(seed: int = 0) -> dict:
    arg_keys = jax.random.split(jax.random.key(seed), 7)
    mla_queries = draw_mla_queries(jax.random.fold_in(arg_keys[6], 71), 0)
    latent_keys = draw_latent_keys(jax.random.fold_in(arg_keys[6], 71), 0)
    index_queries = draw_index_queries(jax.random.fold_in(arg_keys[6], 71), 0)
    index_keys = draw_index_keys(jax.random.fold_in(arg_keys[6], 71), 0)
    head_weights = bell_draw(arg_keys[4], (LENGTH, SEQS * IDX_HEADS), 1.0, 6.0, ((0, 64),), jnp.float32)
    block_order = draw_block_order(jax.random.fold_in(arg_keys[6], 71), 0)
    return dict(mla_queries=mla_queries, latent_keys=latent_keys, index_queries=index_queries, index_keys=index_keys, head_weights=head_weights, block_order=block_order)


score_scale = 192.0 ** (-0.5)
loss_scale = 1024.0

def storage_places(block_order):
    row_ids = jnp.arange(LENGTH, dtype=jnp.int32)
    slot_of = 2 * (row_ids // TOK_DEV) + row_ids % TOK_DEV // HALF
    return jnp.take(block_order, slot_of).astype(jnp.int32) * HALF + row_ids % HALF

def sequence_grad(queries, latent, index_q, index_k, weights):
    block_rows = LENGTH // 8
    index_norm = (IDX_DIM * IDX_HEADS) ** (-0.5)
    grad_coef = loss_scale * index_norm
    key_grads = jnp.zeros((LENGTH, IDX_DIM), jnp.float32)
    for block_id in range(8):
        first_row = block_id * block_rows
        seen_count = first_row + block_rows
        head_major = queries[first_row:seen_count].reshape(block_rows, MLA_HEADS, KD).transpose(1, 0, 2)
        key_rows = latent[:seen_count]
        query_pos = first_row + jnp.arange(block_rows, dtype=jnp.int32)
        visible_mask = jnp.arange(seen_count, dtype=jnp.int32)[None, :] <= query_pos[:, None]

        def add_head(prob_sum, query_rows):
            scores = score_scale * jnp.dot(query_rows, key_rows.T, preferred_element_type=jnp.float32)
            scores = jnp.where(visible_mask, scores, -jnp.inf)
            row_max = lax.optimization_barrier(jnp.max(scores, axis=1, keepdims=True))
            log_total = row_max + jnp.log(lax.optimization_barrier(jnp.sum(jnp.exp(scores - row_max), axis=1, keepdims=True)))
            return (prob_sum + jnp.exp(scores - log_total), None)
        prob_sum = lax.scan(add_head, jnp.zeros((block_rows, seen_count), jnp.float32), head_major)[0]
        target = prob_sum / MLA_HEADS
        index_rows = index_q[first_row:seen_count].reshape(block_rows, IDX_HEADS, IDX_DIM).transpose(1, 0, 2)
        index_keys = index_k[:seen_count]
        head_cols = weights[first_row:seen_count].T

        def add_logit(logit_sum, head_item):
            query_rows, head_weight = head_item
            inner_dot = jnp.dot(query_rows, index_keys.T, preferred_element_type=jnp.float32)
            return (logit_sum + head_weight[:, None] * jnp.maximum(inner_dot, 0.0), None)
        logit_sum = lax.scan(add_logit, jnp.zeros((block_rows, seen_count), jnp.float32), (index_rows, head_cols))[0]
        logits = jnp.where(visible_mask, index_norm * logit_sum, -jnp.inf)
        row_max = lax.optimization_barrier(jnp.max(logits, axis=1, keepdims=True))
        exp_logits = jnp.exp(logits - row_max)
        index_probs = exp_logits / lax.optimization_barrier(jnp.sum(exp_logits, axis=1, keepdims=True))
        scaled = grad_coef * (index_probs - target)

        def add_grad(grad_sum, head_item):
            query_rows, head_weight = head_item
            inner_dot = jnp.dot(query_rows, index_keys.T, preferred_element_type=jnp.float32)
            signal = (scaled * head_weight[:, None] * (inner_dot > 0.0)).astype(jnp.bfloat16)
            return (grad_sum + jnp.dot(signal.T, query_rows, preferred_element_type=jnp.float32), None)
        block_grad = lax.scan(add_grad, jnp.zeros((seen_count, IDX_DIM), jnp.float32), (index_rows, head_cols))[0]
        key_grads = key_grads.at[:seen_count].add(block_grad)
    return key_grads

def reference(mla_queries, latent_keys, index_queries, index_keys, head_weights, block_order):
    places = storage_places(block_order)
    seq_order = jnp.zeros((LENGTH,), jnp.int32).at[places].set(jnp.arange(LENGTH, dtype=jnp.int32))
    columns = []
    for seq_id in range(SEQS):
        key_grads = sequence_grad(mla_queries[seq_id][seq_order], latent_keys[:, seq_id * KD:(seq_id + 1) * KD][seq_order], index_queries[seq_id][seq_order], index_keys[:, seq_id * IDX_DIM:(seq_id + 1) * IDX_DIM][seq_order], head_weights[:, seq_id * IDX_HEADS:(seq_id + 1) * IDX_HEADS][seq_order])
        columns.append(key_grads[places])
    return jnp.concatenate(columns, axis=1)
```

```python
import functools
import math

import jax
import jax.numpy as jnp
from jax import lax
from jax.experimental import pallas as pl
from jax.experimental.pallas import tpu as pltpu
from jax.sharding import PartitionSpec as P

MESH = pl.DeviceIdType.MESH
NX, NZ, NY = 4, 8, 4
HEADS = 64
HEADS_DEV = 16
KD = 576
KPAD = 640
IDX_HEADS = 64
IDX_DIM = 128
TOK = 64
HALF = 32
HALVES = 128
SLOTS = 36
SCORE_SCALE = 192.0 ** (-0.5)
LOG2E = 1.4426950408889634
INDEX_NORM = (IDX_HEADS * IDX_DIM) ** (-0.5)
GRAD_COEF = 1024.0 * INDEX_NORM
NEG = -1e30
VMEM_BYTES = 60 * 1024 * 1024
F32 = jnp.float32
BF16 = jnp.bfloat16


def coords():
    s = lax.axis_index("seq")
    y = lax.axis_index("head")
    return s // (2 * NZ), (s // 2) % NZ, s % 2, y


def seq_at(x, z, c):
    return (x * NZ + z) * 2 + c


def gather_kernel(
    lat_ref, idx_ref, hw_ref, mq_ref, iq_ref,
    p_out, q_out, mqx_ref, iqx_ref, hwx_ref,
    own_p, own_q, stage_out, stage_in, idx32, idx_stage_in, idx_stage_out,
    pair_send, pair_recv, send_sem, recv_sem, local_sem,
):
    x, z, c, y = coords()
    partner = (seq_at(x, z, 1 - c), y)
    ring = {
        ("x", 1): (seq_at((x + 1) % NX, z, c), y),
        ("x", -1): (seq_at((x + NX - 1) % NX, z, c), y),
        ("z", 1): (seq_at(x, (z + 1) % NZ, c), y),
        ("z", -1): (seq_at(x, (z + NZ - 1) % NZ, c), y),
    }
    barrier = pltpu.get_barrier_semaphore()
    for target in [partner] + list(ring.values()):
        pl.semaphore_signal(barrier, inc=1, device_id=target, device_id_type=MESH)

    lat = lat_ref[...]
    stage_out[:, 0:KD] = jnp.where(c == 0, lat[:, KD:], lat[:, :KD])
    stage_out[:, KD:] = jnp.zeros((TOK, KPAD - KD), BF16)
    idx32[...] = idx_ref[...].astype(F32)
    rows = jnp.concatenate(
        [idx32[pl.ds(pl.multiple_of(y * 8, 8), 8), :], idx32[pl.ds(pl.multiple_of(HALF + y * 8, 8), 8), :]], axis=0
    )
    idx_stage_out[...] = jnp.where(c == 0, rows[:, IDX_DIM:], rows[:, :IDX_DIM]).astype(BF16)
    pl.semaphore_wait(barrier, 5)

    def pair_copy(k, src, dst):
        return pltpu.make_async_remote_copy(
            src_ref=src, dst_ref=dst, send_sem=pair_send.at[k], recv_sem=pair_recv.at[k],
            device_id=partner, device_id_type=MESH,
        )

    pair = [
        pair_copy(0, stage_out, stage_in),
        pair_copy(1, idx_stage_out, idx_stage_in),
        pair_copy(2, mq_ref.at[1 - c], mqx_ref),
        pair_copy(3, iq_ref.at[1 - c], iqx_ref),
        pair_copy(4, hw_ref, hwx_ref),
    ]
    for d in pair:
        d.start()
    mine = jnp.where(c == 0, lat[:, :KD], lat[:, KD:])
    idx_mine = jnp.where(c == 0, rows[:, :IDX_DIM], rows[:, IDX_DIM:]).astype(BF16)
    pair[0].wait_recv()
    pair[1].wait_recv()
    other = stage_in[:, :KD]
    both = jnp.concatenate([jnp.where(c == 0, mine, other), jnp.where(c == 0, other, mine)], axis=1)
    own_p[...] = both[:HALF]
    own_q[:, : 2 * KD] = both[HALF:]
    idx_other = idx_stage_in[...]
    own_q[0:16, 2 * KD :] = jnp.where(c == 0, idx_mine, idx_other)
    own_q[16:32, 2 * KD :] = jnp.where(c == 0, idx_other, idx_mine)
    keep = [
        pltpu.make_async_copy(own_p, p_out.at[x, z], local_sem.at[0]),
        pltpu.make_async_copy(own_q, q_out.at[x, z], local_sem.at[1]),
    ]
    for d in keep:
        d.start()

    counter = [0]
    live = {}

    def block(part, ox, oz, rows_from, rows_to):
        ref = p_out if part == "p" else q_out
        return ref.at[ox, oz, pl.ds(rows_from, rows_to - rows_from)]

    def send(part, axis, way, dx, dz, rows_from, rows_to):
        k = counter[0]
        counter[0] += 1
        ox, oz = (x + dx + NX) % NX, (z + dz + NZ) % NZ
        if dx == 0 and dz == 0:
            src = (own_p if part == "p" else own_q).at[pl.ds(rows_from, rows_to - rows_from)]
        else:
            src = block(part, ox, oz, rows_from, rows_to)
        out = pltpu.make_async_remote_copy(
            src_ref=src, dst_ref=block(part, ox, oz, rows_from, rows_to),
            send_sem=send_sem.at[k], recv_sem=recv_sem.at[k], device_id=ring[(axis, way)], device_id_type=MESH,
        )
        out.start()
        ix, iz = (dx - way, dz) if axis == "x" else (dx, dz - way)
        here = block(part, (x + ix + 2 * NX) % NX, (z + iz + 2 * NZ) % NZ, rows_from, rows_to)
        arrival = pltpu.make_async_remote_copy(
            src_ref=here, dst_ref=here, send_sem=send_sem.at[k], recv_sem=recv_sem.at[k],
            device_id=ring[(axis, way)], device_id_type=MESH,
        )
        live[k] = [out, arrival, False]
        return k

    def arrived(k):
        if not live[k][2]:
            live[k][1].wait_recv()
            live[k][2] = True

    last_x, last_z = NX // 2, NZ // 2

    def hop(part, axis, dx, dz, step, before):
        last = last_x if axis == "x" else last_z
        keys = []
        for way, half in ((1, (0, 16)), (-1, (16, 32))):
            if before is not None:
                arrived(before[0 if way == 1 else 1])
            away = -way * (step - 1)
            ox, oz = (away, dz) if axis == "x" else (dx, away)
            lo, hi = half if step == last else (0, 32)
            keys.append(send(part, axis, way, ox, oz, lo, hi))
        return keys

    zp = {0: {1: hop("p", "z", 0, 0, 1, None)}}
    xp = hop("p", "x", 0, 0, 1, None)
    zq = {1: hop("q", "z", 0, 0, 1, None)}
    xq = {0: {1: hop("q", "x", 0, 0, 1, None)}}

    xp2 = hop("p", "x", 0, 0, 2, xp)
    zp[-1] = {1: hop("p", "z", -1, 0, 1, None)}
    zp[1] = {1: hop("p", "z", 1, 0, 1, None)}

    def advance_p(dx, step):
        zp[dx][step] = hop("p", "z", dx, 0, step, zp[dx][step - 1])

    def advance_q(step):
        arrive = zq[step - 1]
        if step <= last_z:
            zq[step] = hop("q", "z", 0, 0, step, arrive)
        else:
            arrived(arrive[0])
            arrived(arrive[1])
        for dz in ((-(step - 1), step - 1) if step <= last_z else (last_z,)):
            xq[dz] = {1: hop("q", "x", 0, dz, 1, None)}

    def finish_q(dz):
        xq[dz][2] = hop("q", "x", 0, dz, 2, xq[dz][1])

    advance_p(0, 2)
    advance_q(2)
    finish_q(0)
    arrived(xp2[0])
    arrived(xp2[1])
    zp[2] = {1: hop("p", "z", 2, 0, 1, None)}
    advance_p(-1, 2)
    advance_p(1, 2)
    advance_p(0, 3)
    advance_q(3)
    finish_q(-1)
    finish_q(1)
    advance_p(2, 2)
    advance_p(-1, 3)
    advance_p(1, 3)
    advance_p(0, 4)
    advance_q(4)
    finish_q(-2)
    finish_q(2)
    advance_p(2, 3)
    advance_p(-1, 4)
    advance_p(1, 4)
    advance_q(5)
    finish_q(-3)
    finish_q(3)
    advance_p(2, 4)
    finish_q(last_z)

    for k in live:
        arrived(k)
    for k in live:
        live[k][0].wait_send()
    for d in keep:
        d.wait()
    for d in pair[2:]:
        d.wait_recv()
    for d in pair:
        d.wait_send()


GATHER_COPIES = 76


def gather_call(lat, idx, hw, mq, iq):
    any_spec = pl.BlockSpec(memory_space=pl.ANY)
    vmem = pl.BlockSpec(memory_space=pltpu.VMEM)
    return pl.pallas_call(
        gather_kernel,
        name="gather_keys",
        out_shape=[
            jax.ShapeDtypeStruct((NX, NZ, HALF, 2 * KD), BF16),
            jax.ShapeDtypeStruct((NX, NZ, HALF, 2 * KD + IDX_DIM), BF16),
            jax.ShapeDtypeStruct((TOK, HEADS_DEV * KD), BF16),
            jax.ShapeDtypeStruct((TOK, IDX_HEADS * IDX_DIM), BF16),
            jax.ShapeDtypeStruct((TOK, 2 * IDX_HEADS), F32),
        ],
        in_specs=[vmem, vmem, vmem, any_spec, any_spec],
        out_specs=[any_spec, any_spec, any_spec, any_spec, vmem],
        scratch_shapes=[
            pltpu.VMEM((HALF, 2 * KD), BF16),
            pltpu.VMEM((HALF, 2 * KD + IDX_DIM), BF16),
            pltpu.VMEM((TOK, KPAD), BF16),
            pltpu.VMEM((TOK, KPAD), BF16),
            pltpu.VMEM((TOK, 2 * IDX_DIM), F32),
            pltpu.VMEM((16, IDX_DIM), BF16),
            pltpu.VMEM((16, IDX_DIM), BF16),
            pltpu.SemaphoreType.DMA((5,)),
            pltpu.SemaphoreType.DMA((5,)),
            pltpu.SemaphoreType.DMA((GATHER_COPIES,)),
            pltpu.SemaphoreType.DMA((GATHER_COPIES,)),
            pltpu.SemaphoreType.DMA((2,)),
        ],
        compiler_params=pltpu.CompilerParams(
            collective_id=0, has_side_effects=True, vmem_limit_bytes=VMEM_BYTES
        ),
    )(lat, idx, hw, mq, iq)


def forward_kernel(
    info, order, p_any, q_any, mq_any, mqx_any, iq_any, iqx_any, w_ref,
    tgt_ref, logit_ref, stat_ref, idx_keys_ref, idx_q_ref,
    vp, vq, vmq, vidx, keys, queries, scores, keys32, sem,
):
    c = info[4]
    copies = [
        pltpu.make_async_copy(p_any, vp, sem.at[0]),
        pltpu.make_async_copy(q_any, vq, sem.at[1]),
        pltpu.make_async_copy(mq_any.at[c], vmq.at[0], sem.at[2]),
        pltpu.make_async_copy(mqx_any, vmq.at[1], sem.at[3]),
        pltpu.make_async_copy(iq_any.at[c], vidx.at[0], sem.at[4]),
        pltpu.make_async_copy(iqx_any, vidx.at[1], sem.at[5]),
    ]
    for d in copies:
        d.start()
    copies[0].wait()
    copies[1].wait()
    pad = jnp.zeros((HALF, KPAD - KD), BF16)

    def place_keys(chip, carry):
        cx, cz = chip // NZ, chip % NZ
        for half, ref in ((0, vp), (1, vq)):
            for core in range(2):
                place = order[4 * chip + 2 * core + half]
                keys[pl.ds(pl.multiple_of(place * HALF, HALF), HALF), :] = jnp.concatenate(
                    [ref[cx, cz, :, core * KD : (core + 1) * KD], pad], axis=1
                )
        idx_rows = vq[cx, cz, :, 2 * KD :].astype(F32)
        for core in range(2):
            for half in range(2):
                place = order[4 * chip + 2 * core + half]
                at = core * 16 + half * 8
                keys32[pl.ds(pl.multiple_of(place * 8, 8), 8), :] = idx_rows[at : at + 8]
        return carry

    lax.fori_loop(0, NX * NZ, place_keys, 0)
    idx_keys_ref[...] = keys32[...].astype(BF16)
    copies[2].wait()
    copies[3].wait()
    for g in range(4):
        rows = vmq[g // 2, g % 2 * HALF : (g % 2 + 1) * HALF, :]
        for h in range(HEADS_DEV):
            queries[g, h * HALF : (h + 1) * HALF, :] = jnp.concatenate([rows[:, h * KD : (h + 1) * KD], pad], axis=1)

    lanes = HEADS_DEV * HALF
    token = lax.broadcasted_iota(jnp.int32, (256, lanes), 1) % HALF
    key_row = lax.broadcasted_iota(jnp.int32, (256, lanes), 0)
    group_of = lax.broadcasted_iota(jnp.int32, (8, 128), 1) // HALF
    tgt_ref[:, :, SLOTS - 2 :] = jnp.zeros((NY, 2, 2, 8, 128), F32)
    blocks_before = [0, 0, 0, 0]
    for g in range(4):
        pair, half = g // 2, g % 2
        place = info[g]
        total = place // 8 + 1
        first = info[2 * pair] // 8 + 1 if half else 0

        def score_block(b):
            k = keys[pl.ds(pl.multiple_of(b * 256, 256), 256), :]
            return lax.dot_general(k, queries[g], (((1,), (1,)), ((), ())), preferred_element_type=F32)

        def at(b):
            return pl.ds(pl.multiple_of((first + b) * 256, 256), 256)

        def fill(b, top):
            s = score_block(b)
            scores[at(b), :] = s
            return jnp.maximum(top, jnp.max(s.reshape(32, 8, lanes), axis=0))

        top = lax.fori_loop(0, total - 1, fill, jnp.full((8, lanes), NEG, F32))
        last = total - 1
        s = score_block(last)
        s = jnp.where(key_row + last * 256 <= token + place * HALF, s, NEG)
        scores[at(last), :] = s
        top = jnp.maximum(top, jnp.max(s.reshape(32, 8, lanes), axis=0))
        scale = SCORE_SCALE * LOG2E
        shift = jnp.max(top, axis=0, keepdims=True) * scale

        def exponentials(b, sums):
            e = jnp.exp2(scores[at(b), :] * scale - shift)
            scores[at(b), :] = e
            return sums + jnp.sum(e.reshape(32, 8, lanes), axis=0)

        sums = lax.fori_loop(0, total, exponentials, jnp.zeros((8, lanes), F32))
        weight = 1.0 / (HEADS * jnp.sum(sums, axis=0, keepdims=True))

        def head_sum(b, carry):
            for part in range(2):
                rows = pl.ds(pl.multiple_of((first + b) * 256 + part * 128, 128), 128)
                r = scores[rows, 0:128] * weight[:, 0:128]
                for lt in range(1, lanes // 128):
                    r = r + scores[rows, lt * 128 : (lt + 1) * 128] * weight[:, lt * 128 : (lt + 1) * 128]
                r = r + pltpu.roll(r, 64, 1)
                r = r + pltpu.roll(r, 32, 1)
                for y in range(NY):
                    out = r[8 * y : 8 * y + 8]
                    for a in range(1, 4):
                        out = jnp.where(group_of == a, r[32 * a + 8 * y : 32 * a + 8 * y + 8], out)
                    tgt_ref[y, pair, 2 * (first + b) + part] = out
            return carry

        lax.fori_loop(0, total, head_sum, 0)

    y = info[5]
    copies[4].wait()
    copies[5].wait()
    for g in range(4):
        rows = vidx[g // 2, g % 2 * HALF : (g % 2 + 1) * HALF, :]
        for j in range(IDX_HEADS):
            idx_q_ref[g, j * HALF : (j + 1) * HALF, :] = rows[:, j * IDX_DIM : (j + 1) * IDX_DIM]
    row_id = lax.broadcasted_iota(jnp.int32, (128, 128), 0)
    token = lax.broadcasted_iota(jnp.int32, (128, 128), 1) % HALF
    offset = row_id // 8 * HALF + row_id % 8 + 8 * y
    for g in range(4):
        place = info[g]
        total = place // 16 + 1

        def logits(b, top):
            k = idx_keys_ref[pl.ds(pl.multiple_of(b * 128, 128), 128), :]
            acc = jnp.zeros((128, 128), F32)
            for ch in range(8):
                inner = lax.dot_general(
                    k, idx_q_ref[g, ch * 256 : (ch + 1) * 256, :], (((1,), (1,)), ((), ())),
                    preferred_element_type=F32,
                )
                part = jnp.maximum(inner, 0.0) * w_ref[g, :, ch * 256 : (ch + 1) * 256]
                acc = acc + part[:, :128] + part[:, 128:]
            acc = acc + pltpu.roll(acc, 64, 1)
            acc = acc + pltpu.roll(acc, 32, 1)
            acc = jnp.where(offset + b * 512 <= token + place * HALF, acc * INDEX_NORM, NEG)
            logit_ref[g, pl.ds(pl.multiple_of(b * 128, 128), 128), :] = acc
            return jnp.maximum(top, jnp.max(acc.reshape(16, 8, 128), axis=0))

        top = lax.fori_loop(0, total, logits, jnp.full((8, 128), NEG, F32))
        top = jnp.max(top, axis=0, keepdims=True)

        def total_exp(b, sums):
            e = jnp.exp(logit_ref[g, pl.ds(pl.multiple_of(b * 128, 128), 128), :] - top)
            return sums + jnp.sum(e.reshape(16, 8, 128), axis=0)

        sums = lax.fori_loop(0, total, total_exp, jnp.zeros((8, 128), F32))
        stat_ref[g : g + 1, :] = top
        stat_ref[4 + g : 5 + g, :] = jnp.sum(sums, axis=0, keepdims=True)


def forward_call(info, order, p, q, mq, mqx, iq, iqx, w):
    any_spec = pl.BlockSpec(memory_space=pl.ANY)
    vmem = pl.BlockSpec(memory_space=pltpu.VMEM)
    smem = pl.BlockSpec(memory_space=pltpu.SMEM)
    return pl.pallas_call(
        forward_kernel,
        name="targets_and_logits",
        out_shape=[
            jax.ShapeDtypeStruct((NY, 2, SLOTS, 8, 128), F32),
            jax.ShapeDtypeStruct((4, 1024, 128), F32),
            jax.ShapeDtypeStruct((8, 128), F32),
            jax.ShapeDtypeStruct((1024, IDX_DIM), BF16),
            jax.ShapeDtypeStruct((4, IDX_HEADS * HALF, IDX_DIM), BF16),
        ],
        in_specs=[smem, smem] + [any_spec] * 6 + [vmem],
        out_specs=[vmem] * 5,
        scratch_shapes=[
            pltpu.VMEM((NX, NZ, HALF, 2 * KD), BF16),
            pltpu.VMEM((NX, NZ, HALF, 2 * KD + IDX_DIM), BF16),
            pltpu.VMEM((2, TOK, HEADS_DEV * KD), BF16),
            pltpu.VMEM((2, TOK, IDX_HEADS * IDX_DIM), BF16),
            pltpu.VMEM((HALVES * HALF, KPAD), BF16),
            pltpu.VMEM((4, HEADS_DEV * HALF, KPAD), BF16),
            pltpu.VMEM((17 * 256, HEADS_DEV * HALF), F32),
            pltpu.VMEM((1024, IDX_DIM), F32),
            pltpu.SemaphoreType.DMA((6,)),
        ],
        compiler_params=pltpu.CompilerParams(vmem_limit_bytes=VMEM_BYTES),
    )(info, order, p, q, mq, mqx, iq, iqx, w)


def exchange_kernel(tgt_ref, stat_ref, sum_ref, stats_ref, arrive, send_sem, recv_sem, stat_send, stat_recv):
    x, z, c, y = coords()
    seq = lax.axis_index("seq")
    barrier = pltpu.get_barrier_semaphore()
    for d in range(1, NY):
        pl.semaphore_signal(barrier, inc=1, device_id=(seq, (y + d) % NY), device_id_type=MESH)
    pl.semaphore_wait(barrier, NY - 1)
    sends = []
    for d in range(1, NY):
        to = (y + d) % NY
        sends.append(
            pltpu.make_async_remote_copy(
                src_ref=tgt_ref.at[to], dst_ref=arrive.at[d - 1], send_sem=send_sem.at[d - 1],
                recv_sem=recv_sem.at[d - 1], device_id=(seq, to), device_id_type=MESH,
            )
        )
        sends.append(
            pltpu.make_async_remote_copy(
                src_ref=stat_ref, dst_ref=stats_ref.at[d], send_sem=stat_send.at[d - 1],
                recv_sem=stat_recv.at[d - 1], device_id=(seq, to), device_id_type=MESH,
            )
        )
    for d in sends:
        d.start()
    stats_ref[0] = stat_ref[...]
    for d in sends:
        d.wait_recv()
    sum_ref[...] = tgt_ref[y] + arrive[0] + arrive[1] + arrive[2]
    for d in sends:
        d.wait_send()


def exchange_call(tgt, stat):
    vmem = pl.BlockSpec(memory_space=pltpu.VMEM)
    return pl.pallas_call(
        exchange_kernel,
        name="sum_targets",
        out_shape=[
            jax.ShapeDtypeStruct((2, SLOTS, 8, 128), F32),
            jax.ShapeDtypeStruct((NY, 8, 128), F32),
        ],
        in_specs=[vmem] * 2,
        out_specs=[vmem] * 2,
        scratch_shapes=[
            pltpu.VMEM((NY - 1, 2, SLOTS, 8, 128), F32),
            pltpu.SemaphoreType.DMA((NY - 1,)),
            pltpu.SemaphoreType.DMA((NY - 1,)),
            pltpu.SemaphoreType.DMA((NY - 1,)),
            pltpu.SemaphoreType.DMA((NY - 1,)),
        ],
        compiler_params=pltpu.CompilerParams(
            collective_id=1, has_side_effects=True, vmem_limit_bytes=VMEM_BYTES
        ),
    )(tgt, stat)


def backward_kernel(info, order, sum_ref, stats_ref, logit_ref, keys_ref, idx_q_ref, w_ref, out_ref, grads):
    y = info[5]
    row_id = lax.broadcasted_iota(jnp.int32, (128, 128), 0)
    token = lax.broadcasted_iota(jnp.int32, (128, 128), 1) % HALF
    offset = row_id // 8 * HALF + row_id % 8 + 8 * y
    group_of = lax.broadcasted_iota(jnp.int32, (8, 128), 1) // HALF
    grads[...] = jnp.zeros((1024, IDX_DIM), F32)
    for g in range(4):
        pair, half = g // 2, g % 2
        place = info[g]
        total = place // 16 + 1
        first = 2 * (info[2 * pair] // 8 + 1) if half else 0
        tops = [stats_ref[d, g : g + 1, :] for d in range(NY)]
        top = jnp.maximum(jnp.maximum(tops[0], tops[1]), jnp.maximum(tops[2], tops[3]))
        norm = sum(stats_ref[d, 4 + g : 5 + g, :] * jnp.exp(tops[d] - top) for d in range(NY))
        coef = GRAD_COEF / norm

        def block(b, carry):
            rows = pl.ds(pl.multiple_of(b * 128, 128), 128)
            wide = []
            for q in range(4):
                packed = sum_ref[pair, first + 4 * b + q]
                for a in range(4):
                    v = jnp.where(group_of == a, packed, 0.0)
                    v = v + pltpu.roll(v, 64, 1)
                    wide.append(v + pltpu.roll(v, 32, 1))
            target = jnp.concatenate(wide, axis=0)
            prob = jnp.exp(logit_ref[g, rows, :] - top) * coef
            scaled = jnp.where(offset + b * 512 <= token + place * HALF, prob - GRAD_COEF * target, 0.0)
            scaled = jnp.concatenate([scaled, scaled], axis=1)
            k = keys_ref[rows, :]
            acc = grads[rows, :]
            for ch in range(8):
                q_rows = idx_q_ref[g, ch * 256 : (ch + 1) * 256, :]
                inner = lax.dot_general(k, q_rows, (((1,), (1,)), ((), ())), preferred_element_type=F32)
                signal = jnp.where(inner > 0.0, scaled * w_ref[g, :, ch * 256 : (ch + 1) * 256], 0.0).astype(BF16)
                acc = acc + jnp.dot(signal, q_rows, preferred_element_type=F32)
            grads[rows, :] = acc
            return carry

        lax.fori_loop(0, total, block, 0)

    def store(chip, carry):
        for core in range(2):
            for half in range(2):
                place = order[4 * chip + 2 * core + half]
                out_ref[chip, core * 16 + half * 8 : core * 16 + half * 8 + 8, :] = grads[
                    pl.ds(pl.multiple_of(place * 8, 8), 8), :
                ]
        return carry

    lax.fori_loop(0, NX * NZ, store, 0)


def backward_call(info, order, tsum, stats, logit, keys, idx_q, w):
    vmem = pl.BlockSpec(memory_space=pltpu.VMEM)
    smem = pl.BlockSpec(memory_space=pltpu.SMEM)
    return pl.pallas_call(
        backward_kernel,
        name="key_gradients",
        out_shape=jax.ShapeDtypeStruct((NX * NZ, 32, IDX_DIM), F32),
        in_specs=[smem, smem] + [vmem] * 6,
        out_specs=vmem,
        scratch_shapes=[pltpu.VMEM((1024, IDX_DIM), F32)],
        compiler_params=pltpu.CompilerParams(vmem_limit_bytes=VMEM_BYTES),
    )(info, order, tsum, stats, logit, keys, idx_q, w)


def scatter_kernel(
    part_ref, out_ref, xa, za, xb, zb, slab_x, slab_z, tail, pieces,
    xa_sem, za_sem, xb_sem, zb_sem, piece_sem,
):
    x, z, c, y = coords()
    barrier = pltpu.get_barrier_semaphore()
    peers_x = [(seq_at((x + d) % NX, z, c), y) for d in range(1, NX)]
    peers_z = [(seq_at(x, (z + d) % NZ, c), y) for d in range(1, NZ)]
    near = [(half, core) for half in range(2) for core in range(2)]
    targets = [(seq_at(x, z, core), y // 2 + 2 * half) for half, core in near]
    sources = [(seq_at(x, z, core), 2 * (y % 2) + odd) for odd in range(2) for core in range(2)]
    for to in peers_x + peers_z:
        pl.semaphore_signal(barrier, inc=1, device_id=to, device_id_type=MESH)
    for core in range(2):
        for other in range(NY):
            @pl.when(jnp.logical_or(core != c, other != y))
            def _(core=core, other=other):
                pl.semaphore_signal(barrier, inc=1, device_id=(seq_at(x, z, core), other), device_id_type=MESH)
    pl.semaphore_wait(barrier, NX - 1 + NZ - 1 + 2 * NY - 1)

    def remote(src, dst, sems, k, to):
        d = pltpu.make_async_remote_copy(
            src_ref=src, dst_ref=dst, send_sem=sems.at[0, k], recv_sem=sems.at[1, k],
            device_id=to, device_id_type=MESH,
        )
        d.start()
        return d

    first_z = [
        remote(part_ref.at[:, (z + d) % NZ, pl.ds(16, 16)], za.at[d - 1], za_sem, d - 1, peers_z[d - 1])
        for d in range(1, NZ)
    ]
    first_x = [
        remote(part_ref.at[(x + d) % NX, :, pl.ds(0, 16)], xa.at[d - 1], xa_sem, d - 1, peers_x[d - 1])
        for d in range(1, NX)
    ]
    for d in first_x:
        d.wait_recv()
    slab_x[...] = part_ref[x, :, 0:16, :] + xa[0] + xa[1] + xa[2]
    second_z = [
        remote(slab_x.at[(z + d) % NZ], zb.at[d - 1], zb_sem, d - 1, peers_z[d - 1]) for d in range(1, NZ)
    ]
    for d in first_z:
        d.wait_recv()
    total = part_ref[:, z, 16:32, :]
    for k in range(NZ - 1):
        total = total + za[k]
    slab_z[...] = total
    second_x = [
        remote(slab_z.at[(x + d) % NX], xb.at[d - 1], xb_sem, d - 1, peers_x[d - 1]) for d in range(1, NX)
    ]
    for d in second_z:
        d.wait_recv()
    total = slab_x[z]
    for k in range(NZ - 1):
        total = total + zb[k]
    tail[0:16] = total
    for d in second_x:
        d.wait_recv()
    tail[16:32] = slab_z[x] + xb[0] + xb[1] + xb[2]

    slot = 2 * (y % 2) + c

    for k, (half, core) in enumerate(near):
        piece = tail.at[pl.ds(16 * core + 8 * half, 8)]
        local = jnp.logical_and(core == c, y // 2 + 2 * half == y)

        @pl.when(jnp.logical_not(local))
        def _(piece=piece, k=k):
            pltpu.make_async_remote_copy(
                src_ref=piece, dst_ref=pieces.at[slot], send_sem=piece_sem.at[0, k],
                recv_sem=piece_sem.at[1, slot], device_id=targets[k], device_id_type=MESH,
            ).start()

        @pl.when(local)
        def _(piece=piece):
            pieces[slot] = piece[...]

    for k, (odd, core) in enumerate([(odd, core) for odd in range(2) for core in range(2)]):
        away = jnp.logical_not(jnp.logical_and(core == c, 2 * (y % 2) + odd == y))

        @pl.when(away)
        def _(k=k, odd=odd, core=core):
            ref = pieces.at[2 * odd + core]
            pltpu.make_async_remote_copy(
                src_ref=ref, dst_ref=ref, send_sem=piece_sem.at[0, k], recv_sem=piece_sem.at[1, 2 * odd + core],
                device_id=sources[k], device_id_type=MESH,
            ).wait_recv()

    for odd in range(2):
        for core in range(2):
            out_ref[8 * odd : 8 * odd + 8, core * IDX_DIM : (core + 1) * IDX_DIM] = pieces[2 * odd + core]
    for k, (half, core) in enumerate(near):
        away = jnp.logical_not(jnp.logical_and(core == c, y // 2 + 2 * half == y))

        @pl.when(away)
        def _(k=k, half=half, core=core):
            piece = tail.at[pl.ds(16 * core + 8 * half, 8)]
            pltpu.make_async_remote_copy(
                src_ref=piece, dst_ref=pieces.at[slot], send_sem=piece_sem.at[0, k],
                recv_sem=piece_sem.at[1, slot], device_id=targets[k], device_id_type=MESH,
            ).wait_send()

    for d in first_x + first_z + second_x + second_z:
        d.wait_send()


def scatter_call(part):
    vmem = pl.BlockSpec(memory_space=pltpu.VMEM)
    return pl.pallas_call(
        scatter_kernel,
        name="sum_gradients",
        out_shape=jax.ShapeDtypeStruct((16, 2 * IDX_DIM), F32),
        in_specs=[vmem],
        out_specs=vmem,
        scratch_shapes=[
            pltpu.VMEM((NX - 1, NZ, 16, IDX_DIM), F32),
            pltpu.VMEM((NZ - 1, NX, 16, IDX_DIM), F32),
            pltpu.VMEM((NX - 1, 16, IDX_DIM), F32),
            pltpu.VMEM((NZ - 1, 16, IDX_DIM), F32),
            pltpu.VMEM((NZ, 16, IDX_DIM), F32),
            pltpu.VMEM((NX, 16, IDX_DIM), F32),
            pltpu.VMEM((32, IDX_DIM), F32),
            pltpu.VMEM((4, 8, IDX_DIM), F32),
            pltpu.SemaphoreType.DMA((2, NX - 1)),
            pltpu.SemaphoreType.DMA((2, NZ - 1)),
            pltpu.SemaphoreType.DMA((2, NX - 1)),
            pltpu.SemaphoreType.DMA((2, NZ - 1)),
            pltpu.SemaphoreType.DMA((2, 4)),
        ],
        compiler_params=pltpu.CompilerParams(
            collective_id=2, has_side_effects=True, vmem_limit_bytes=VMEM_BYTES
        ),
    )(part)


def per_device(mla_queries, latent_keys, index_queries, index_keys, head_weights, block_order):
    s = lax.axis_index("seq")
    y = lax.axis_index("head")
    c = s % 2
    p, q, mqx, iqx, hwx = gather_call(latent_keys, index_keys, head_weights, mla_queries, index_queries)
    mine = lax.dynamic_slice(block_order, (2 * s,), (2,))
    others = lax.dynamic_slice(block_order, (2 * (s + 1 - 2 * c),), (2,))
    info = jnp.concatenate([mine, others, jnp.stack([c, y]).astype(jnp.int32)])
    w = jnp.stack([head_weights, hwx]).reshape(2, 2, HALF, 2, IDX_HEADS)
    w = lax.dynamic_index_in_dim(w, c, 3, keepdims=False)
    w = w.transpose(0, 1, 3, 2).reshape(4, 1, IDX_HEADS * HALF)
    tgt, logit, stat, keys, idx_q = forward_call(info, block_order, p, q, mla_queries, mqx, index_queries, iqx, w)
    tsum, stats = exchange_call(tgt, stat)
    part = backward_call(info, block_order, tsum, stats, logit, keys, idx_q, w)
    return scatter_call(part.reshape(NX, NZ, 32, IDX_DIM))


def solution(mesh):
    return jax.shard_map(
        per_device,
        mesh=mesh,
        in_specs=(
            P(None, "seq", "head"),
            P("seq", None),
            P(None, "seq", None),
            P("seq", None),
            P("seq", None),
            P(),
        ),
        out_specs=P(("seq", "head"), None),
        check_vma=False,
    )
```

```python
import functools
import math

import jax
import jax.numpy as jnp
from jax import lax
from jax.experimental import pallas as pl
from jax.experimental.pallas import tpu as pltpu
from jax.sharding import PartitionSpec as P

MESH = pl.DeviceIdType.MESH
NX, NZ, NY = 4, 8, 4
HEADS = 64
HEADS_DEV = 16
KD = 576
KPAD = 640
IDX_HEADS = 64
IDX_DIM = 128
TOK = 64
HALF = 32
HALVES = 128
SLOTS = 36
SCORE_SCALE = 192.0 ** (-0.5)
LOG2E = 1.4426950408889634
INDEX_NORM = (IDX_HEADS * IDX_DIM) ** (-0.5)
GRAD_COEF = 1024.0 * INDEX_NORM
NEG = -1e30
VMEM_BYTES = 60 * 1024 * 1024
F32 = jnp.float32
BF16 = jnp.bfloat16


def coords():
    s = lax.axis_index("seq")
    y = lax.axis_index("head")
    return s // (2 * NZ), (s // 2) % NZ, s % 2, y


def seq_at(x, z, c):
    return (x * NZ + z) * 2 + c


def gather_kernel(
    lat_ref, idx_ref, hw_ref, mq_ref, iq_ref,
    p_out, q_out, mqx_ref, iqx_ref, hwx_ref,
    own_p, own_q, stage_out, stage_in, idx32, idx_stage_in, idx_stage_out,
    pair_send, pair_recv, send_sem, recv_sem, local_sem,
):
    x, z, c, y = coords()
    partner = (seq_at(x, z, 1 - c), y)
    ring = {
        ("x", 1): (seq_at((x + 1) % NX, z, c), y),
        ("x", -1): (seq_at((x + NX - 1) % NX, z, c), y),
        ("z", 1): (seq_at(x, (z + 1) % NZ, c), y),
        ("z", -1): (seq_at(x, (z + NZ - 1) % NZ, c), y),
    }
    barrier = pltpu.get_barrier_semaphore()
    for target in [partner] + list(ring.values()):
        pl.semaphore_signal(barrier, inc=1, device_id=target, device_id_type=MESH)

    lat = lat_ref[...]
    stage_out[:, 0:KD] = jnp.where(c == 0, lat[:, KD:], lat[:, :KD])
    stage_out[:, KD:] = jnp.zeros((TOK, KPAD - KD), BF16)
    idx32[...] = idx_ref[...].astype(F32)
    rows = jnp.concatenate(
        [idx32[pl.ds(pl.multiple_of(y * 8, 8), 8), :], idx32[pl.ds(pl.multiple_of(HALF + y * 8, 8), 8), :]], axis=0
    )
    idx_stage_out[...] = jnp.where(c == 0, rows[:, IDX_DIM:], rows[:, :IDX_DIM]).astype(BF16)
    pl.semaphore_wait(barrier, 5)

    def pair_copy(k, src, dst):
        return pltpu.make_async_remote_copy(
            src_ref=src, dst_ref=dst, send_sem=pair_send.at[k], recv_sem=pair_recv.at[k],
            device_id=partner, device_id_type=MESH,
        )

    pair = [
        pair_copy(0, stage_out, stage_in),
        pair_copy(1, idx_stage_out, idx_stage_in),
        pair_copy(2, mq_ref.at[1 - c], mqx_ref),
        pair_copy(3, iq_ref.at[1 - c], iqx_ref),
        pair_copy(4, hw_ref, hwx_ref),
    ]
    for d in pair:
        d.start()
    mine = jnp.where(c == 0, lat[:, :KD], lat[:, KD:])
    idx_mine = jnp.where(c == 0, rows[:, :IDX_DIM], rows[:, IDX_DIM:]).astype(BF16)
    pair[0].wait_recv()
    pair[1].wait_recv()
    other = stage_in[:, :KD]
    both = jnp.concatenate([jnp.where(c == 0, mine, other), jnp.where(c == 0, other, mine)], axis=1)
    own_p[...] = both[:HALF]
    own_q[:, : 2 * KD] = both[HALF:]
    idx_other = idx_stage_in[...]
    own_q[0:16, 2 * KD :] = jnp.where(c == 0, idx_mine, idx_other)
    own_q[16:32, 2 * KD :] = jnp.where(c == 0, idx_other, idx_mine)
    keep = [
        pltpu.make_async_copy(own_p, p_out.at[x, z], local_sem.at[0]),
        pltpu.make_async_copy(own_q, q_out.at[x, z], local_sem.at[1]),
    ]
    for d in keep:
        d.start()

    counter = [0]
    live = {}

    def block(part, ox, oz, rows_from, rows_to):
        ref = p_out if part == "p" else q_out
        return ref.at[ox, oz, pl.ds(rows_from, rows_to - rows_from)]

    def send(part, axis, way, dx, dz, rows_from, rows_to):
        k = counter[0]
        counter[0] += 1
        ox, oz = (x + dx + NX) % NX, (z + dz + NZ) % NZ
        if dx == 0 and dz == 0:
            src = (own_p if part == "p" else own_q).at[pl.ds(rows_from, rows_to - rows_from)]
        else:
            src = block(part, ox, oz, rows_from, rows_to)
        out = pltpu.make_async_remote_copy(
            src_ref=src, dst_ref=block(part, ox, oz, rows_from, rows_to),
            send_sem=send_sem.at[k], recv_sem=recv_sem.at[k], device_id=ring[(axis, way)], device_id_type=MESH,
        )
        out.start()
        ix, iz = (dx - way, dz) if axis == "x" else (dx, dz - way)
        here = block(part, (x + ix + 2 * NX) % NX, (z + iz + 2 * NZ) % NZ, rows_from, rows_to)
        arrival = pltpu.make_async_remote_copy(
            src_ref=here, dst_ref=here, send_sem=send_sem.at[k], recv_sem=recv_sem.at[k],
            device_id=ring[(axis, way)], device_id_type=MESH,
        )
        live[k] = [out, arrival, False]
        return k

    def arrived(k):
        if not live[k][2]:
            live[k][1].wait_recv()
            live[k][2] = True

    last_x, last_z = NX // 2, NZ // 2

    def hop(part, axis, dx, dz, step, before):
        last = last_x if axis == "x" else last_z
        keys = []
        for way, half in ((1, (0, 16)), (-1, (16, 32))):
            if before is not None:
                arrived(before[0 if way == 1 else 1])
            away = -way * (step - 1)
            ox, oz = (away, dz) if axis == "x" else (dx, away)
            lo, hi = half if step == last else (0, 32)
            keys.append(send(part, axis, way, ox, oz, lo, hi))
        return keys

    zp = {0: {1: hop("p", "z", 0, 0, 1, None)}}
    xp = hop("p", "x", 0, 0, 1, None)
    zq = {1: hop("q", "z", 0, 0, 1, None)}
    xq = {0: {1: hop("q", "x", 0, 0, 1, None)}}

    xp2 = hop("p", "x", 0, 0, 2, xp)
    zp[-1] = {1: hop("p", "z", -1, 0, 1, None)}
    zp[1] = {1: hop("p", "z", 1, 0, 1, None)}

    def advance_p(dx, step):
        zp[dx][step] = hop("p", "z", dx, 0, step, zp[dx][step - 1])

    def advance_q(step):
        arrive = zq[step - 1]
        if step <= last_z:
            zq[step] = hop("q", "z", 0, 0, step, arrive)
        else:
            arrived(arrive[0])
            arrived(arrive[1])
        for dz in ((-(step - 1), step - 1) if step <= last_z else (last_z,)):
            xq[dz] = {1: hop("q", "x", 0, dz, 1, None)}

    def finish_q(dz):
        xq[dz][2] = hop("q", "x", 0, dz, 2, xq[dz][1])

    advance_p(0, 2)
    advance_q(2)
    finish_q(0)
    arrived(xp2[0])
    arrived(xp2[1])
    zp[2] = {1: hop("p", "z", 2, 0, 1, None)}
    advance_p(-1, 2)
    advance_p(1, 2)
    advance_p(0, 3)
    advance_q(3)
    finish_q(-1)
    finish_q(1)
    advance_p(2, 2)
    advance_p(-1, 3)
    advance_p(1, 3)
    advance_p(0, 4)
    advance_q(4)
    finish_q(-2)
    finish_q(2)
    advance_p(2, 3)
    advance_p(-1, 4)
    advance_p(1, 4)
    advance_q(5)
    finish_q(-3)
    finish_q(3)
    advance_p(2, 4)
    finish_q(last_z)

    for k in live:
        arrived(k)
    for k in live:
        live[k][0].wait_send()
    for d in keep:
        d.wait()
    for d in pair[2:]:
        d.wait_recv()
    for d in pair:
        d.wait_send()


GATHER_COPIES = 76


def gather_call(lat, idx, hw, mq, iq):
    any_spec = pl.BlockSpec(memory_space=pl.ANY)
    vmem = pl.BlockSpec(memory_space=pltpu.VMEM)
    return pl.pallas_call(
        gather_kernel,
        name="gather_keys",
        out_shape=[
            jax.ShapeDtypeStruct((NX, NZ, HALF, 2 * KD), BF16),
            jax.ShapeDtypeStruct((NX, NZ, HALF, 2 * KD + IDX_DIM), BF16),
            jax.ShapeDtypeStruct((TOK, HEADS_DEV * KD), BF16),
            jax.ShapeDtypeStruct((TOK, IDX_HEADS * IDX_DIM), BF16),
            jax.ShapeDtypeStruct((TOK, 2 * IDX_HEADS), F32),
        ],
        in_specs=[vmem, vmem, vmem, any_spec, any_spec],
        out_specs=[any_spec, any_spec, any_spec, any_spec, vmem],
        scratch_shapes=[
            pltpu.VMEM((HALF, 2 * KD), BF16),
            pltpu.VMEM((HALF, 2 * KD + IDX_DIM), BF16),
            pltpu.VMEM((TOK, KPAD), BF16),
            pltpu.VMEM((TOK, KPAD), BF16),
            pltpu.VMEM((TOK, 2 * IDX_DIM), F32),
            pltpu.VMEM((16, IDX_DIM), BF16),
            pltpu.VMEM((16, IDX_DIM), BF16),
            pltpu.SemaphoreType.DMA((5,)),
            pltpu.SemaphoreType.DMA((5,)),
            pltpu.SemaphoreType.DMA((GATHER_COPIES,)),
            pltpu.SemaphoreType.DMA((GATHER_COPIES,)),
            pltpu.SemaphoreType.DMA((2,)),
        ],
        compiler_params=pltpu.CompilerParams(
            collective_id=0, has_side_effects=True, vmem_limit_bytes=VMEM_BYTES
        ),
    )(lat, idx, hw, mq, iq)


ENTRIES = 9


def entry_table(places):
    i = jnp.arange(ENTRIES, dtype=jnp.int32)[None, :]
    k = i - 5
    flip = places[:, :1] // 16 + 1 > k
    early = (i == 0) | ((i > 5) & flip)
    block = jnp.where(i == 0, 0, jnp.where(i < 6, i - 1, jnp.where(flip, k, 8 - k)))
    group = 2 * jnp.arange(2, dtype=jnp.int32)[:, None] + jnp.where(early, 0, 1)
    limit = jnp.where(early, places[:, :1], places[:, 1:]) * HALF - block * 512
    return jnp.stack([early.astype(jnp.int32), group, block, limit]).reshape(-1)


def entry(table, pair, i):
    return [table[(field * 2 + pair) * ENTRIES + i] for field in range(4)]


def mask_of(flag, shape):
    return jnp.zeros(shape, jnp.int32) + flag > 0


def sort_keys(inverse, pq, keys, keys32):
    pad = jnp.zeros((HALF, KPAD - KD), BF16)

    def step(p, carry):
        slot = inverse[p]
        chip, core, half = slot // 4, slot // 2 % 2, slot % 2
        first, second = pq[half, chip, :, 0:KD], pq[half, chip, :, KD : 2 * KD]
        at = pl.ds(pl.multiple_of(p * HALF, HALF), HALF)
        keys[at, :] = jnp.concatenate([jnp.where(core == 0, first, second), pad], axis=1)
        idx_rows = pq[1, chip, :, 2 * KD :].astype(F32)
        idx_rows = jnp.where(core == 0, idx_rows[0:16], idx_rows[16:32])
        idx_rows = jnp.where(half == 0, idx_rows[0:8], idx_rows[8:16])
        keys32[pl.ds(pl.multiple_of(p * 8, 8), 8), :] = idx_rows
        return carry

    lax.fori_loop(0, HALVES, step, 0, unroll=2)


def split_heads(vmq, queries):
    pad = jnp.zeros((HALF, KPAD - KD), BF16)
    for g in range(4):
        rows = pl.ds(g % 2 * HALF, HALF)
        for h in range(HEADS_DEV):
            queries[g, h * HALF : (h + 1) * HALF, :] = jnp.concatenate(
                [vmq[g // 2, rows, h * KD : (h + 1) * KD], pad], axis=1
            )


LANES = HEADS_DEV * HALF
EXP_SCALE = SCORE_SCALE * LOG2E


def score_step(table, pair, i, keys, queries, scores, tops):
    early, g, block, limit = entry(table, pair, i)
    early = mask_of(early, (8, LANES))
    k = keys[pl.ds(pl.multiple_of(block * 512, 512), 512), :]
    s = lax.dot_general(k, queries[g], (((1,), (1,)), ((), ())), preferred_element_type=F32)
    row = lax.broadcasted_iota(jnp.int32, (512, LANES), 0)
    token = lax.broadcasted_iota(jnp.int32, (512, LANES), 1) % HALF
    s = jnp.where(row - token <= limit, s, NEG)
    scores[pair, pl.ds(pl.multiple_of(i * 512, 512), 512), :] = s
    m = jnp.max(s.reshape(64, 8, LANES), axis=0)
    return (
        jnp.where(early, jnp.maximum(tops[0], m), tops[0]),
        jnp.where(early, tops[1], jnp.maximum(tops[1], m)),
    )


def exp_step(table, pair, i, scores, shifts, sums):
    early = entry(table, pair, i)[0]
    row = mask_of(early, (1, LANES))
    early = mask_of(early, (8, LANES))
    at = pl.ds(pl.multiple_of(i * 512, 512), 512)
    e = jnp.exp2(scores[pair, at, :] * EXP_SCALE - jnp.where(row, shifts[0], shifts[1]))
    scores[pair, at, :] = e
    m = jnp.sum(e.reshape(64, 8, LANES), axis=0)
    return (sums[0] + jnp.where(early, m, 0.0), sums[1] + jnp.where(early, 0.0, m))


def head_step(table, pair, i, scores, weights, tgt_ref):
    early = mask_of(entry(table, pair, i)[0], (1, LANES))
    group_of = lax.broadcasted_iota(jnp.int32, (8, 128), 1) // HALF
    weight = jnp.where(early, weights[0], weights[1])
    for part in range(4):
        rows = pl.ds(pl.multiple_of(i * 512 + part * 128, 128), 128)
        r = scores[pair, rows, 0:128] * weight[:, 0:128]
        for lt in range(1, LANES // 128):
            r = r + scores[pair, rows, lt * 128 : (lt + 1) * 128] * weight[:, lt * 128 : (lt + 1) * 128]
        r = r + pltpu.roll(r, 64, 1)
        r = r + pltpu.roll(r, 32, 1)
        for y in range(NY):
            out = r[8 * y : 8 * y + 8]
            for a in range(1, 4):
                out = jnp.where(group_of == a, r[32 * a + 8 * y : 32 * a + 8 * y + 8], out)
            tgt_ref[y, pair, 4 * i + part] = out


def start_tops():
    return (jnp.full((8, LANES), NEG, F32),) * 2


def start_sums():
    return (jnp.zeros((8, LANES), F32),) * 2


def shifts_of(tops):
    return tuple(jnp.max(t, axis=0, keepdims=True) * EXP_SCALE for t in tops)


def weights_of(sums):
    return tuple(1.0 / (HEADS * jnp.sum(t, axis=0, keepdims=True)) for t in sums)


def targets(table, keys, queries, scores, tgt_ref):
    tops0 = lax.fori_loop(0, 9, lambda i, t: score_step(table, 0, i, keys, queries, scores, t), start_tops())
    shifts0 = shifts_of(tops0)

    def both(i, carry):
        tops, sums = carry
        tops = score_step(table, 1, i, keys, queries, scores, tops)
        return tops, exp_step(table, 0, i, scores, shifts0, sums)

    tops1, sums0 = lax.fori_loop(0, 9, both, (start_tops(), start_sums()))
    shifts1, weights0 = shifts_of(tops1), weights_of(sums0)

    def later(i, sums):
        head_step(table, 0, i, scores, weights0, tgt_ref)
        return exp_step(table, 1, i, scores, shifts1, sums)

    weights1 = weights_of(lax.fori_loop(0, 9, later, start_sums()))

    def last(i, carry):
        head_step(table, 1, i, scores, weights1, tgt_ref)
        return carry

    lax.fori_loop(0, 9, last, 0)


def target_kernel(
    info, table, inverse, p_any, q_any, mq_any, mqx_any, tgt_ref, idx_keys_ref, pq, vmq, keys, queries, scores, keys32, sem
):
    copies = [
        pltpu.make_async_copy(mq_any.at[info[0]], vmq.at[0], sem.at[2]),
        pltpu.make_async_copy(mqx_any, vmq.at[1], sem.at[3]),
        pltpu.make_async_copy(p_any, pq.at[0, :, :, pl.ds(0, 2 * KD)], sem.at[0]),
        pltpu.make_async_copy(q_any, pq.at[1], sem.at[1]),
    ]
    for d in copies:
        d.start()
    copies[0].wait()
    copies[1].wait()
    split_heads(vmq, queries)
    copies[2].wait()
    copies[3].wait()
    sort_keys(inverse, pq, keys, keys32)
    idx_keys_ref[...] = keys32[...].astype(BF16).reshape(8, 128, IDX_DIM)
    targets(table, keys, queries, scores, tgt_ref)


def target_call(info, table, inverse, p, q, mq, mqx):
    any_spec = pl.BlockSpec(memory_space=pl.ANY)
    vmem = pl.BlockSpec(memory_space=pltpu.VMEM)
    smem = pl.BlockSpec(memory_space=pltpu.SMEM)
    return pl.pallas_call(
        target_kernel,
        name="targets",
        out_shape=[
            jax.ShapeDtypeStruct((NY, 2, SLOTS, 8, 128), F32),
            jax.ShapeDtypeStruct((8, 128, IDX_DIM), BF16),
        ],
        in_specs=[smem, smem, smem] + [any_spec] * 4,
        out_specs=[vmem] * 2,
        scratch_shapes=[
            pltpu.VMEM((2, NX * NZ, HALF, 2 * KD + IDX_DIM), BF16),
            pltpu.VMEM((2, TOK, HEADS_DEV * KD), BF16),
            pltpu.VMEM((HALVES * HALF, KPAD), BF16),
            pltpu.VMEM((4, LANES, KPAD), BF16),
            pltpu.VMEM((2, 9 * 512, LANES), F32),
            pltpu.VMEM((1024, IDX_DIM), F32),
            pltpu.SemaphoreType.DMA((4,)),
        ],
        compiler_params=pltpu.CompilerParams(vmem_limit_bytes=VMEM_BYTES),
    )(info, table, inverse, p, q, mq, mqx)


def split_index_heads(vidx, idx_q):
    for g in range(4):
        for j in range(IDX_HEADS):
            idx_q[g, j * HALF : (j + 1) * HALF, :] = vidx[
                g // 2, g % 2 * HALF : (g % 2 + 1) * HALF, j * IDX_DIM : (j + 1) * IDX_DIM
            ]


def logit_step(table, pair, i, y, idx_keys, idx_q, w_ref, inner_ref, logit_ref, tops):
    early, g, block, limit = entry(table, pair, i)
    early = mask_of(early, (8, 128))
    k = idx_keys[block]
    acc = jnp.zeros((128, 128), F32)
    for ch in range(8):
        cut = slice(ch * 256, (ch + 1) * 256)
        inner = lax.dot_general(k, idx_q[g, cut, :], (((1,), (1,)), ((), ())), preferred_element_type=F32)
        inner_ref[pair, i, :, cut] = inner.astype(BF16)
        part = jnp.maximum(inner, 0.0) * w_ref[g, :, cut]
        acc = acc + part[:, :128] + part[:, 128:]
    acc = acc + pltpu.roll(acc, 64, 1)
    acc = acc + pltpu.roll(acc, 32, 1)
    row = lax.broadcasted_iota(jnp.int32, (128, 128), 0)
    token = lax.broadcasted_iota(jnp.int32, (128, 128), 1) % HALF
    offset = row // 8 * HALF + row % 8 - token
    acc = jnp.where(offset <= limit - 8 * y, acc * INDEX_NORM, NEG)
    logit_ref[pair, i] = acc
    m = jnp.max(acc.reshape(16, 8, 128), axis=0)
    return (
        jnp.where(early, jnp.maximum(tops[0], m), tops[0]),
        jnp.where(early, tops[1], jnp.maximum(tops[1], m)),
    )


def logit_stats(table, pair, logit_ref, stat_ref, tops):
    tops = [jnp.max(t, axis=0, keepdims=True) for t in tops]

    def step(i, sums):
        early = entry(table, pair, i)[0]
        row = mask_of(early, (1, 128))
        early = mask_of(early, (8, 128))
        e = jnp.exp(logit_ref[pair, i] - jnp.where(row, tops[0], tops[1]))
        e = jnp.sum(e.reshape(16, 8, 128), axis=0)
        return (sums[0] + jnp.where(early, e, 0.0), sums[1] + jnp.where(early, 0.0, e))

    sums = lax.fori_loop(0, 9, step, (jnp.zeros((8, 128), F32),) * 2, unroll=3)
    for half in range(2):
        g = 2 * pair + half
        stat_ref[g : g + 1, :] = tops[half]
        stat_ref[4 + g : 5 + g, :] = jnp.sum(sums[half], axis=0, keepdims=True)


def norms_of(stats_ref, g):
    tops = [stats_ref[d, g : g + 1, :] for d in range(NY)]
    top = jnp.maximum(jnp.maximum(tops[0], tops[1]), jnp.maximum(tops[2], tops[3]))
    norm = sum(stats_ref[d, 4 + g : 5 + g, :] * jnp.exp(tops[d] - top) for d in range(NY))
    return top, GRAD_COEF / norm


def gradient_step(table, pair, i, y, idx_q, w_ref, inner_ref, logit_ref, tgt_ref, arrive, norms, grad_ref):
    early, g, block, limit = entry(table, pair, i)
    early = mask_of(early, (1, 128))
    group_of = lax.broadcasted_iota(jnp.int32, (8, 128), 1) // HALF
    wide = []
    for part in range(4):
        at = 4 * i + part
        packed = tgt_ref[y, pair, at] + arrive[0, pair, at] + arrive[1, pair, at] + arrive[2, pair, at]
        for a in range(4):
            v = jnp.where(group_of == a, packed, 0.0)
            v = v + pltpu.roll(v, 64, 1)
            wide.append(v + pltpu.roll(v, 32, 1))
    target = jnp.concatenate(wide, axis=0)
    top = jnp.where(early, norms[0][0], norms[1][0])
    coef = jnp.where(early, norms[0][1], norms[1][1])
    row = lax.broadcasted_iota(jnp.int32, (128, 128), 0)
    token = lax.broadcasted_iota(jnp.int32, (128, 128), 1) % HALF
    offset = row // 8 * HALF + row % 8 - token
    seen = offset <= limit - 8 * y
    scaled = jnp.where(seen, jnp.exp(logit_ref[pair, i] - top) * coef - GRAD_COEF * target, 0.0)
    scaled = jnp.concatenate([scaled, scaled], axis=1)
    acc = jnp.zeros((128, IDX_DIM), F32)
    zero = jnp.zeros((), BF16)
    for ch in range(8):
        cut = slice(ch * 256, (ch + 1) * 256)
        signal = (scaled * w_ref[g, :, cut]).astype(BF16)
        signal = jnp.where(inner_ref[pair, i, :, cut] > zero, signal, zero)
        acc = acc + jnp.dot(signal, idx_q[g, cut, :], preferred_element_type=F32)
    grad_ref[pair, i] = acc


def collect_gradients(table, order, grad_ref, sorted_ref, part_ref):
    total = [grad_ref[0, 0] + grad_ref[1, 0] + grad_ref[0, 1] + grad_ref[1, 1]]
    total += [grad_ref[0, b + 1] + grad_ref[1, b + 1] for b in range(1, 5)] + [0.0] * 3
    for pair in range(2):
        for k in range(1, 4):
            flip = mask_of(entry(table, pair, k + 5)[0], (128, IDX_DIM))
            d = grad_ref[pair, k + 5]
            total[k] = total[k] + jnp.where(flip, d, 0.0)
            total[8 - k] = total[8 - k] + jnp.where(flip, 0.0, d)
    for b in range(8):
        sorted_ref[b * 16 : (b + 1) * 16] = total[b].reshape(16, 8, IDX_DIM)

    def store(chip, carry):
        for core in range(2):
            for half in range(2):
                place = order[4 * chip + 2 * core + half]
                rows = sorted_ref[place]
                part_ref[chip // NZ, chip % NZ, core * 16 + half * 8 : core * 16 + half * 8 + 8, :] = rows
        return carry

    lax.fori_loop(0, NX * NZ, store, 0, unroll=2)


def scatter(
    x, z, c, y, peers_x, peers_z, remote, part_ref, out_ref, xa, za, xb, zb, slab_x, slab_z, tail, pieces,
    xa_sem, za_sem, xb_sem, zb_sem, piece_sem,
):
    near = [(half, core) for half in range(2) for core in range(2)]
    targets = [(seq_at(x, z, core), y // 2 + 2 * half) for half, core in near]
    sources = [(seq_at(x, z, core), 2 * (y % 2) + odd) for odd in range(2) for core in range(2)]
    first_z = [
        remote(part_ref.at[:, (z + d) % NZ, pl.ds(16, 16)], za.at[d - 1], za_sem.at[0, d - 1], za_sem.at[1, d - 1], peers_z[d - 1])
        for d in range(1, NZ)
    ]
    first_x = [
        remote(part_ref.at[(x + d) % NX, :, pl.ds(0, 16)], xa.at[d - 1], xa_sem.at[0, d - 1], xa_sem.at[1, d - 1], peers_x[d - 1])
        for d in range(1, NX)
    ]
    for d in first_x:
        d.wait_recv()
    slab_x[...] = part_ref[x, :, 0:16, :] + xa[0] + xa[1] + xa[2]
    second_z = [
        remote(slab_x.at[(z + d) % NZ], zb.at[d - 1], zb_sem.at[0, d - 1], zb_sem.at[1, d - 1], peers_z[d - 1]) for d in range(1, NZ)
    ]
    for d in first_z:
        d.wait_recv()
    total = part_ref[:, z, 16:32, :]
    for k in range(NZ - 1):
        total = total + za[k]
    slab_z[...] = total
    second_x = [
        remote(slab_z.at[(x + d) % NX], xb.at[d - 1], xb_sem.at[0, d - 1], xb_sem.at[1, d - 1], peers_x[d - 1]) for d in range(1, NX)
    ]
    for d in second_z:
        d.wait_recv()
    total = slab_x[z]
    for k in range(NZ - 1):
        total = total + zb[k]
    tail[0:16] = total
    for d in second_x:
        d.wait_recv()
    tail[16:32] = slab_z[x] + xb[0] + xb[1] + xb[2]

    slot = 2 * (y % 2) + c

    for k, (half, core) in enumerate(near):
        piece = tail.at[pl.ds(16 * core + 8 * half, 8)]
        local = jnp.logical_and(core == c, y // 2 + 2 * half == y)

        @pl.when(jnp.logical_not(local))
        def _(piece=piece, k=k):
            pltpu.make_async_remote_copy(
                src_ref=piece, dst_ref=pieces.at[slot], send_sem=piece_sem.at[0, k],
                recv_sem=piece_sem.at[1, slot], device_id=targets[k], device_id_type=MESH,
            ).start()

        @pl.when(local)
        def _(piece=piece):
            pieces[slot] = piece[...]

    for k, (odd, core) in enumerate([(odd, core) for odd in range(2) for core in range(2)]):
        away = jnp.logical_not(jnp.logical_and(core == c, 2 * (y % 2) + odd == y))

        @pl.when(away)
        def _(k=k, odd=odd, core=core):
            ref = pieces.at[2 * odd + core]
            pltpu.make_async_remote_copy(
                src_ref=ref, dst_ref=ref, send_sem=piece_sem.at[0, k], recv_sem=piece_sem.at[1, 2 * odd + core],
                device_id=sources[k], device_id_type=MESH,
            ).wait_recv()

    for odd in range(2):
        for core in range(2):
            out_ref[8 * odd : 8 * odd + 8, core * IDX_DIM : (core + 1) * IDX_DIM] = pieces[2 * odd + core]
    for k, (half, core) in enumerate(near):
        away = jnp.logical_not(jnp.logical_and(core == c, y // 2 + 2 * half == y))

        @pl.when(away)
        def _(k=k, half=half, core=core):
            piece = tail.at[pl.ds(16 * core + 8 * half, 8)]
            pltpu.make_async_remote_copy(
                src_ref=piece, dst_ref=pieces.at[slot], send_sem=piece_sem.at[0, k],
                recv_sem=piece_sem.at[1, slot], device_id=targets[k], device_id_type=MESH,
            ).wait_send()

    for d in first_x + first_z + second_x + second_z:
        d.wait_send()


def index_kernel(
    table, order, tgt_ref, iq_any, iqx_any, idx_keys, w_ref, out_ref,
    vidx, idx_q, inner_ref, logit_ref, stat_ref, stats_ref, arrive, grad_ref, sorted_ref, part_ref,
    xa, za, xb, zb, slab_x, slab_z, tail, pieces,
    load_sem, tgt_send, tgt_recv, stat_send, stat_recv, xa_sem, za_sem, xb_sem, zb_sem, piece_sem,
):
    x, z, c, y = coords()
    seq = lax.axis_index("seq")
    barrier = pltpu.get_barrier_semaphore()
    peers_y = [(seq, (y + d) % NY) for d in range(1, NY)]
    peers_x = [(seq_at((x + d) % NX, z, c), y) for d in range(1, NX)]
    peers_z = [(seq_at(x, (z + d) % NZ, c), y) for d in range(1, NZ)]
    other = [(seq_at(x, z, 1 - c), t) for t in range(NY)]
    for to in peers_x + peers_z + peers_y + other:
        pl.semaphore_signal(barrier, inc=1, device_id=to, device_id_type=MESH)
    loads = [
        pltpu.make_async_copy(iq_any.at[c], vidx.at[0], load_sem.at[0]),
        pltpu.make_async_copy(iqx_any, vidx.at[1], load_sem.at[1]),
    ]
    for d in loads:
        d.start()
    pl.semaphore_wait(barrier, NX - 1 + NZ - 1 + 2 * NY - 1)

    def remote(src, dst, send, recv, to):
        d = pltpu.make_async_remote_copy(
            src_ref=src, dst_ref=dst, send_sem=send, recv_sem=recv, device_id=to, device_id_type=MESH
        )
        d.start()
        return d

    tgt_copies = [
        [
            remote(
                tgt_ref.at[(y + d) % NY, pair], arrive.at[d - 1, pair], tgt_send.at[pair, d - 1],
                tgt_recv.at[pair, d - 1], peers_y[d - 1],
            )
            for d in range(1, NY)
        ]
        for pair in range(2)
    ]
    for d in loads:
        d.wait()
    split_index_heads(vidx, idx_q)
    start = (jnp.full((8, 128), NEG, F32),) * 2
    for pair in range(2):
        tops = lax.fori_loop(
            0, 9,
            lambda i, t: logit_step(table, pair, i, y, idx_keys, idx_q, w_ref, inner_ref, logit_ref, t),
            start,
        )
        logit_stats(table, pair, logit_ref, stat_ref, tops)
    stat_copies = [
        remote(stat_ref, stats_ref.at[d], stat_send.at[d - 1], stat_recv.at[d - 1], peers_y[d - 1])
        for d in range(1, NY)
    ]
    stats_ref[0] = stat_ref[...]
    for d in stat_copies:
        d.wait_recv()
    for pair in range(2):
        norms = [norms_of(stats_ref, 2 * pair + half) for half in range(2)]
        for d in tgt_copies[pair]:
            d.wait_recv()

        def step(i, carry):
            gradient_step(
                table, pair, i, y, idx_q, w_ref, inner_ref, logit_ref, tgt_ref, arrive, norms, grad_ref
            )
            return carry

        lax.fori_loop(0, 9, step, 0)
    collect_gradients(table, order, grad_ref, sorted_ref, part_ref)
    scatter(
        x, z, c, y, peers_x, peers_z, remote, part_ref, out_ref, xa, za, xb, zb, slab_x, slab_z, tail, pieces,
        xa_sem, za_sem, xb_sem, zb_sem, piece_sem,
    )
    for d in stat_copies + tgt_copies[0] + tgt_copies[1]:
        d.wait_send()


def index_call(table, order, tgt, iq, iqx, idx_keys, w):
    any_spec = pl.BlockSpec(memory_space=pl.ANY)
    vmem = pl.BlockSpec(memory_space=pltpu.VMEM)
    smem = pl.BlockSpec(memory_space=pltpu.SMEM)
    dma = pltpu.SemaphoreType.DMA
    return pl.pallas_call(
        index_kernel,
        name="indexer",
        out_shape=jax.ShapeDtypeStruct((16, 2 * IDX_DIM), F32),
        in_specs=[smem, smem, vmem, any_spec, any_spec, vmem, vmem],
        out_specs=vmem,
        scratch_shapes=[
            pltpu.VMEM((2, TOK, IDX_HEADS * IDX_DIM), BF16),
            pltpu.VMEM((4, IDX_HEADS * HALF, IDX_DIM), BF16),
            pltpu.VMEM((2, 9, 128, IDX_HEADS * HALF), BF16),
            pltpu.VMEM((2, 9, 128, 128), F32),
            pltpu.VMEM((8, 128), F32),
            pltpu.VMEM((NY, 8, 128), F32),
            pltpu.VMEM((NY - 1, 2, SLOTS, 8, 128), F32),
            pltpu.VMEM((2, 9, 128, IDX_DIM), F32),
            pltpu.VMEM((HALVES, 8, IDX_DIM), F32),
            pltpu.VMEM((NX, NZ, 32, IDX_DIM), F32),
            pltpu.VMEM((NX - 1, NZ, 16, IDX_DIM), F32),
            pltpu.VMEM((NZ - 1, NX, 16, IDX_DIM), F32),
            pltpu.VMEM((NX - 1, 16, IDX_DIM), F32),
            pltpu.VMEM((NZ - 1, 16, IDX_DIM), F32),
            pltpu.VMEM((NZ, 16, IDX_DIM), F32),
            pltpu.VMEM((NX, 16, IDX_DIM), F32),
            pltpu.VMEM((32, IDX_DIM), F32),
            pltpu.VMEM((4, 8, IDX_DIM), F32),
            dma((2,)),
            dma((2, NY - 1)),
            dma((2, NY - 1)),
            dma((NY - 1,)),
            dma((NY - 1,)),
            dma((2, NX - 1)),
            dma((2, NZ - 1)),
            dma((2, NX - 1)),
            dma((2, NZ - 1)),
            dma((2, 4)),
        ],
        compiler_params=pltpu.CompilerParams(
            collective_id=1, has_side_effects=True, vmem_limit_bytes=VMEM_BYTES
        ),
    )(table, order, tgt, iq, iqx, idx_keys, w)


def per_device(mla_queries, latent_keys, index_queries, index_keys, head_weights, block_order):
    s = lax.axis_index("seq")
    y = lax.axis_index("head")
    c = s % 2
    p, q, mqx, iqx, hwx = gather_call(latent_keys, index_keys, head_weights, mla_queries, index_queries)
    mine = lax.dynamic_slice(block_order, (2 * s,), (2,))
    others = lax.dynamic_slice(block_order, (2 * (s + 1 - 2 * c),), (2,))
    table = entry_table(jnp.stack([mine, others]))
    info = jnp.stack([c, y]).astype(jnp.int32)
    w = jnp.stack([head_weights, hwx]).reshape(2, 2, HALF, 2, IDX_HEADS)
    w = lax.dynamic_index_in_dim(w, c, 3, keepdims=False)
    w = w.transpose(0, 1, 3, 2).reshape(4, 1, IDX_HEADS * HALF)
    slots = jnp.arange(HALVES, dtype=jnp.int32)
    inverse = jnp.sum(jnp.where(block_order[None, :] == slots[:, None], slots[None, :], 0), axis=1)
    p = p.reshape(NX * NZ, HALF, 2 * KD)
    q = q.reshape(NX * NZ, HALF, 2 * KD + IDX_DIM)
    tgt, idx_keys = target_call(info, table, inverse, p, q, mla_queries, mqx)
    return index_call(table, block_order, tgt, index_queries, iqx, idx_keys, w)


def solution(mesh):
    return jax.shard_map(
        per_device,
        mesh=mesh,
        in_specs=(
            P(None, "seq", "head"),
            P("seq", None),
            P(None, "seq", None),
            P("seq", None),
            P("seq", None),
            P(),
        ),
        out_specs=P(("seq", "head"), None),
        check_vma=False,
    )
```

```python
import functools

import jax
import jax.numpy as jnp
from jax import lax
from jax.experimental import pallas as pl
from jax.experimental.pallas import tpu as pltpu
from jax.sharding import PartitionSpec as P

MESH = pl.DeviceIdType.MESH
NX, NZ, NY = 4, 8, 4
HEADS = 64
HEADS_DEV = 16
KD = 576
KPAD = 640
IDX_HEADS = 64
IDX_DIM = 128
TOK = 64
HALF = 32
HALVES = 128
SLOTS = 36
SCORE_SCALE = 192.0 ** (-0.5)
LOG2E = 1.4426950408889634
INDEX_NORM = (IDX_HEADS * IDX_DIM) ** (-0.5)
GRAD_COEF = 1024.0 * INDEX_NORM
NEG = -1e30
VMEM_BYTES = 60 * 1024 * 1024
F32 = jnp.float32
BF16 = jnp.bfloat16


def coords():
    s = lax.axis_index("seq")
    y = lax.axis_index("head")
    return s // (2 * NZ), (s // 2) % NZ, s % 2, y


def seq_at(x, z, c):
    return (x * NZ + z) * 2 + c


ENTRIES = 9


def entry_table(places):
    i = jnp.arange(ENTRIES, dtype=jnp.int32)[None, :]
    k = i - 5
    flip = places[:, :1] // 16 + 1 > k
    early = (i == 0) | ((i > 5) & flip)
    block = jnp.where(i == 0, 0, jnp.where(i < 6, i - 1, jnp.where(flip, k, 8 - k)))
    group = 2 * jnp.arange(2, dtype=jnp.int32)[:, None] + jnp.where(early, 0, 1)
    limit = jnp.where(early, places[:, :1], places[:, 1:]) * HALF - block * 512
    return jnp.stack([early.astype(jnp.int32), group, block, limit]).reshape(-1)


def entry(table, pair, i):
    return [table[(field * 2 + pair) * ENTRIES + i] for field in range(4)]


def mask_of(flag, shape):
    return jnp.zeros(shape, jnp.int32) + flag > 0


def sort_keys(inverse, pq, keys):
    pad = jnp.zeros((HALF, KPAD - KD), BF16)

    def step(p, carry):
        slot = inverse[p]
        chip, core, half = slot // 4, slot // 2 % 2, slot % 2
        first, second = pq[half, chip, :, 0:KD], pq[half, chip, :, KD : 2 * KD]
        rows = pl.ds(pl.multiple_of(p % 16 * HALF, HALF), HALF)
        keys[p // 16, rows, :] = jnp.concatenate([jnp.where(core == 0, first, second), pad], axis=1)
        return carry

    lax.fori_loop(0, HALVES, step, 0, unroll=2)


def sort_index_keys(inverse, idxg, slots32, sorted32, idx_keys):
    slots32[...] = idxg[...].astype(F32).reshape(HALVES, 8, IDX_DIM)

    def step(p, carry):
        sorted32[p] = slots32[inverse[p]]
        return carry

    lax.fori_loop(0, HALVES, step, 0, unroll=8)
    idx_keys[...] = sorted32[...].reshape(8, 128, IDX_DIM).astype(BF16)


def split_heads(pair, vmq, queries):
    pad = jnp.zeros((HALF, KPAD - KD), BF16)
    for half in range(2):
        for h in range(HEADS_DEV):
            queries[2 * pair + half, h * HALF : (h + 1) * HALF, :] = jnp.concatenate(
                [vmq[pair, half * HALF : (half + 1) * HALF, h * KD : (h + 1) * KD], pad], axis=1
            )


LANES = HEADS_DEV * HALF
EXP_SCALE = SCORE_SCALE * LOG2E


def score_step(table, pair, i, keys, queries, scores, tops):
    early, g, block, limit = entry(table, pair, i)
    early = mask_of(early, (8, LANES))
    k = keys[block]
    s = lax.dot_general(k, queries[g], (((1,), (1,)), ((), ())), preferred_element_type=F32)
    row = lax.broadcasted_iota(jnp.int32, (512, LANES), 0)
    token = lax.broadcasted_iota(jnp.int32, (512, LANES), 1) % HALF
    s = jnp.where(row - token <= limit, s, NEG)
    scores[i] = s
    m = jnp.max(s.reshape(64, 8, LANES), axis=0)
    return (
        jnp.where(early, jnp.maximum(tops[0], m), tops[0]),
        jnp.where(early, tops[1], jnp.maximum(tops[1], m)),
    )


def exp_step(table, pair, i, scores, shifts, sums):
    early = entry(table, pair, i)[0]
    row = mask_of(early, (1, LANES))
    early = mask_of(early, (8, LANES))
    e = jnp.exp2(scores[i] * EXP_SCALE - jnp.where(row, shifts[0], shifts[1]))
    scores[i] = e
    m = jnp.sum(e.reshape(64, 8, LANES), axis=0)
    return (sums[0] + jnp.where(early, m, 0.0), sums[1] + jnp.where(early, 0.0, m))


def head_step(table, pair, i, scores, weights, tgt_ref):
    early = mask_of(entry(table, pair, i)[0], (1, LANES))
    group_of = lax.broadcasted_iota(jnp.int32, (8, 128), 1) // HALF
    weight = jnp.where(early, weights[0], weights[1])
    for part in range(4):
        rows = slice(part * 128, (part + 1) * 128)
        r = scores[i, rows, 0:128] * weight[:, 0:128]
        for lt in range(1, LANES // 128):
            r = r + scores[i, rows, lt * 128 : (lt + 1) * 128] * weight[:, lt * 128 : (lt + 1) * 128]
        r = r + pltpu.roll(r, 64, 1)
        r = r + pltpu.roll(r, 32, 1)
        for y in range(NY):
            out = r[8 * y : 8 * y + 8]
            for a in range(1, 4):
                out = jnp.where(group_of == a, r[32 * a + 8 * y : 32 * a + 8 * y + 8], out)
            tgt_ref[y, pair, 4 * i + part] = out


def start_tops():
    return (jnp.full((8, LANES), NEG, F32),) * 2


def start_sums():
    return (jnp.zeros((8, LANES), F32),) * 2


def shifts_of(tops):
    return tuple(jnp.max(t, axis=0, keepdims=True) * EXP_SCALE for t in tops)


def weights_of(sums):
    return tuple(1.0 / (HEADS * jnp.sum(t, axis=0, keepdims=True)) for t in sums)


def targets(table, pair, keys, queries, scores, tgt_ref):
    tops = lax.fori_loop(0, 9, lambda i, t: score_step(table, pair, i, keys, queries, scores, t), start_tops())
    shifts = shifts_of(tops)
    sums = lax.fori_loop(0, 9, lambda i, t: exp_step(table, pair, i, scores, shifts, t), start_sums())
    weights = weights_of(sums)

    def last(i, carry):
        head_step(table, pair, i, scores, weights, tgt_ref)
        return carry

    lax.fori_loop(0, 9, last, 0)


def split_index_heads(pair, vidx, idx_q):
    for half in range(2):
        for j in range(IDX_HEADS):
            idx_q[2 * pair + half, j * HALF : (j + 1) * HALF, :] = vidx[
                pair, half * HALF : (half + 1) * HALF, j * IDX_DIM : (j + 1) * IDX_DIM
            ]


def logit_step(table, pair, i, y, idx_keys, idx_q, w_ref, inner_ref, logit_ref, tops):
    early, g, block, limit = entry(table, pair, i)
    early = mask_of(early, (8, 128))
    k = idx_keys[block]
    acc = jnp.zeros((128, 128), F32)
    for ch in range(8):
        cut = slice(ch * 256, (ch + 1) * 256)
        inner = lax.dot_general(k, idx_q[g, cut, :], (((1,), (1,)), ((), ())), preferred_element_type=F32)
        inner_ref[pair, i, :, cut] = inner.astype(BF16)
        part = jnp.maximum(inner, 0.0) * w_ref[g, :, cut]
        acc = acc + part[:, :128] + part[:, 128:]
    acc = acc + pltpu.roll(acc, 64, 1)
    acc = acc + pltpu.roll(acc, 32, 1)
    row = lax.broadcasted_iota(jnp.int32, (128, 128), 0)
    token = lax.broadcasted_iota(jnp.int32, (128, 128), 1) % HALF
    offset = row // 8 * HALF + row % 8 - token
    acc = jnp.where(offset <= limit - 8 * y, acc * INDEX_NORM, NEG)
    logit_ref[pair, i] = acc
    m = jnp.max(acc.reshape(16, 8, 128), axis=0)
    return (
        jnp.where(early, jnp.maximum(tops[0], m), tops[0]),
        jnp.where(early, tops[1], jnp.maximum(tops[1], m)),
    )


def logit_stats(table, pair, logit_ref, stat_ref, tops):
    tops = [jnp.max(t, axis=0, keepdims=True) for t in tops]

    def step(i, sums):
        early = entry(table, pair, i)[0]
        row = mask_of(early, (1, 128))
        early = mask_of(early, (8, 128))
        e = jnp.exp(logit_ref[pair, i] - jnp.where(row, tops[0], tops[1]))
        e = jnp.sum(e.reshape(16, 8, 128), axis=0)
        return (sums[0] + jnp.where(early, e, 0.0), sums[1] + jnp.where(early, 0.0, e))

    sums = lax.fori_loop(0, 9, step, (jnp.zeros((8, 128), F32),) * 2, unroll=3)
    for half in range(2):
        g = 2 * pair + half
        stat_ref[g : g + 1, :] = tops[half]
        stat_ref[4 + g : 5 + g, :] = jnp.sum(sums[half], axis=0, keepdims=True)


def norms_of(stats_ref, g):
    tops = [stats_ref[d, g : g + 1, :] for d in range(NY)]
    top = jnp.maximum(jnp.maximum(tops[0], tops[1]), jnp.maximum(tops[2], tops[3]))
    norm = sum(stats_ref[d, 4 + g : 5 + g, :] * jnp.exp(tops[d] - top) for d in range(NY))
    return top, GRAD_COEF / norm


def gradient_step(table, pair, i, y, idx_q, w_ref, inner_ref, logit_ref, tgt_ref, arrive, norms, grad_ref):
    early, g, block, limit = entry(table, pair, i)
    early = mask_of(early, (1, 128))
    group_of = lax.broadcasted_iota(jnp.int32, (8, 128), 1) // HALF
    wide = []
    for part in range(4):
        at = 4 * i + part
        packed = tgt_ref[y, pair, at] + arrive[0, pair, at] + arrive[1, pair, at] + arrive[2, pair, at]
        for a in range(4):
            v = jnp.where(group_of == a, packed, 0.0)
            v = v + pltpu.roll(v, 64, 1)
            wide.append(v + pltpu.roll(v, 32, 1))
    target = jnp.concatenate(wide, axis=0)
    top = jnp.where(early, norms[0][0], norms[1][0])
    coef = jnp.where(early, norms[0][1], norms[1][1])
    row = lax.broadcasted_iota(jnp.int32, (128, 128), 0)
    token = lax.broadcasted_iota(jnp.int32, (128, 128), 1) % HALF
    offset = row // 8 * HALF + row % 8 - token
    seen = offset <= limit - 8 * y
    scaled = jnp.where(seen, jnp.exp(logit_ref[pair, i] - top) * coef - GRAD_COEF * target, 0.0)
    scaled = jnp.concatenate([scaled, scaled], axis=1)
    acc = jnp.zeros((128, IDX_DIM), F32)
    zero = jnp.zeros((), BF16)
    for ch in range(8):
        cut = slice(ch * 256, (ch + 1) * 256)
        signal = (scaled * w_ref[g, :, cut]).astype(BF16)
        signal = jnp.where(inner_ref[pair, i, :, cut] > zero, signal, zero)
        acc = acc + jnp.dot(signal, idx_q[g, cut, :], preferred_element_type=F32)
    grad_ref[pair, i] = acc


def collect_gradients(table, order, grad_ref, sorted_ref, part_ref):
    total = [grad_ref[0, 0] + grad_ref[1, 0] + grad_ref[0, 1] + grad_ref[1, 1]]
    total += [grad_ref[0, b + 1] + grad_ref[1, b + 1] for b in range(1, 5)] + [0.0] * 3
    for pair in range(2):
        for k in range(1, 4):
            flip = mask_of(entry(table, pair, k + 5)[0], (128, IDX_DIM))
            d = grad_ref[pair, k + 5]
            total[k] = total[k] + jnp.where(flip, d, 0.0)
            total[8 - k] = total[8 - k] + jnp.where(flip, 0.0, d)
    for b in range(8):
        sorted_ref[b * 16 : (b + 1) * 16] = total[b].reshape(16, 8, IDX_DIM)

    def store(chip, carry):
        for core in range(2):
            for half in range(2):
                place = order[4 * chip + 2 * core + half]
                rows = sorted_ref[place]
                part_ref[chip // NZ, chip % NZ, core * 16 + half * 8 : core * 16 + half * 8 + 8, :] = rows
        return carry

    lax.fori_loop(0, NX * NZ, store, 0, unroll=2)


def scatter(
    x, z, c, y, peers_x, peers_z, remote, part_ref, out_ref, xa, za, xb, zb, slab_x, slab_z, tail, pieces,
    xa_sem, za_sem, xb_sem, zb_sem, piece_sem,
):
    near = [(half, core) for half in range(2) for core in range(2)]
    targets = [(seq_at(x, z, core), y // 2 + 2 * half) for half, core in near]
    sources = [(seq_at(x, z, core), 2 * (y % 2) + odd) for odd in range(2) for core in range(2)]
    first_z = [
        remote(part_ref.at[:, (z + d) % NZ, pl.ds(16, 16)], za.at[d - 1], za_sem.at[0, d - 1], za_sem.at[1, d - 1], peers_z[d - 1])
        for d in range(1, NZ)
    ]
    first_x = [
        remote(part_ref.at[(x + d) % NX, :, pl.ds(0, 16)], xa.at[d - 1], xa_sem.at[0, d - 1], xa_sem.at[1, d - 1], peers_x[d - 1])
        for d in range(1, NX)
    ]
    for d in first_x:
        d.wait_recv()
    slab_x[...] = part_ref[x, :, 0:16, :] + xa[0] + xa[1] + xa[2]
    second_z = [
        remote(slab_x.at[(z + d) % NZ], zb.at[d - 1], zb_sem.at[0, d - 1], zb_sem.at[1, d - 1], peers_z[d - 1]) for d in range(1, NZ)
    ]
    for d in first_z:
        d.wait_recv()
    total = part_ref[:, z, 16:32, :]
    for k in range(NZ - 1):
        total = total + za[k]
    slab_z[...] = total
    second_x = [
        remote(slab_z.at[(x + d) % NX], xb.at[d - 1], xb_sem.at[0, d - 1], xb_sem.at[1, d - 1], peers_x[d - 1]) for d in range(1, NX)
    ]
    for d in second_z:
        d.wait_recv()
    total = slab_x[z]
    for k in range(NZ - 1):
        total = total + zb[k]
    tail[0:16] = total
    for d in second_x:
        d.wait_recv()
    tail[16:32] = slab_z[x] + xb[0] + xb[1] + xb[2]

    slot = 2 * (y % 2) + c

    for k, (half, core) in enumerate(near):
        piece = tail.at[pl.ds(16 * core + 8 * half, 8)]
        local = jnp.logical_and(core == c, y // 2 + 2 * half == y)

        @pl.when(jnp.logical_not(local))
        def _(piece=piece, k=k):
            pltpu.make_async_remote_copy(
                src_ref=piece, dst_ref=pieces.at[slot], send_sem=piece_sem.at[0, k],
                recv_sem=piece_sem.at[1, slot], device_id=targets[k], device_id_type=MESH,
            ).start()

        @pl.when(local)
        def _(piece=piece):
            pieces[slot] = piece[...]

    for k, (odd, core) in enumerate([(odd, core) for odd in range(2) for core in range(2)]):
        away = jnp.logical_not(jnp.logical_and(core == c, 2 * (y % 2) + odd == y))

        @pl.when(away)
        def _(k=k, odd=odd, core=core):
            ref = pieces.at[2 * odd + core]
            pltpu.make_async_remote_copy(
                src_ref=ref, dst_ref=ref, send_sem=piece_sem.at[0, k], recv_sem=piece_sem.at[1, 2 * odd + core],
                device_id=sources[k], device_id_type=MESH,
            ).wait_recv()

    for odd in range(2):
        for core in range(2):
            out_ref[8 * odd : 8 * odd + 8, core * IDX_DIM : (core + 1) * IDX_DIM] = pieces[2 * odd + core]
    for k, (half, core) in enumerate(near):
        away = jnp.logical_not(jnp.logical_and(core == c, y // 2 + 2 * half == y))

        @pl.when(away)
        def _(k=k, half=half, core=core):
            piece = tail.at[pl.ds(16 * core + 8 * half, 8)]
            pltpu.make_async_remote_copy(
                src_ref=piece, dst_ref=pieces.at[slot], send_sem=piece_sem.at[0, k],
                recv_sem=piece_sem.at[1, slot], device_id=targets[k], device_id_type=MESH,
            ).wait_send()

    for d in first_x + first_z + second_x + second_z:
        d.wait_send()


def whole_kernel(
    table, order, inverse, lat_ref, idx_ref, w_all, mq_any, iq_any, out_ref,
    pq, stage_out, stage_in, idx32, idx_stage_out, idx_stage_in, idxg, slots32, sorted32, idx_keys,
    vmq, queries, keys, scores, tgt_ref, vidx, idx_q, w_ref, inner_ref, logit_ref, stat_ref, stats_ref, arrive,
    grad_ref, part_ref, xa, za, xb, zb, slab_x, slab_z, tail, pieces,
    load_sem, pair_send, pair_recv, ring_send, ring_recv, idx_z_sem, idx_x_sem,
    tgt_send, tgt_recv, stat_send, stat_recv, xa_sem, za_sem, xb_sem, zb_sem, piece_sem,
):
    x, z, c, y = coords()
    seq = lax.axis_index("seq")
    me = x * NZ + z
    barrier = pltpu.get_barrier_semaphore()
    partner = (seq_at(x, z, 1 - c), y)
    peers_y = [(seq, (y + d) % NY) for d in range(1, NY)]
    peers_x = [(seq_at((x + d) % NX, z, c), y) for d in range(1, NX)]
    peers_z = [(seq_at(x, (z + d) % NZ, c), y) for d in range(1, NZ)]
    other = [(seq_at(x, z, 1 - c), t) for t in range(NY)]
    ring = {("x", 1): peers_x[0], ("x", -1): peers_x[-1], ("z", 1): peers_z[0], ("z", -1): peers_z[-1]}
    for to in peers_x + peers_z + peers_y + other:
        pl.semaphore_signal(barrier, inc=1, device_id=to, device_id_type=MESH)
    loads = [
        pltpu.make_async_copy(mq_any.at[c], vmq.at[0], load_sem.at[0]),
        pltpu.make_async_copy(iq_any.at[c], vidx.at[0], load_sem.at[1]),
    ]
    for d in loads:
        d.start()

    lat = lat_ref[...]
    stage_out[:, 0:KD] = jnp.where(c == 0, lat[:, KD:], lat[:, :KD])
    stage_out[:, KD:] = jnp.zeros((TOK, KPAD - KD), BF16)
    idx32[...] = idx_ref[...].astype(F32)
    rows = jnp.concatenate(
        [idx32[pl.ds(pl.multiple_of(y * 8, 8), 8), :], idx32[pl.ds(pl.multiple_of(HALF + y * 8, 8), 8), :]], axis=0
    )
    idx_stage_out[...] = jnp.where(c == 0, rows[:, IDX_DIM:], rows[:, :IDX_DIM]).astype(BF16)
    pl.semaphore_wait(barrier, NX - 1 + NZ - 1 + 2 * NY - 1)

    def remote(src, dst, send, recv, to):
        d = pltpu.make_async_remote_copy(
            src_ref=src, dst_ref=dst, send_sem=send, recv_sem=recv, device_id=to, device_id_type=MESH
        )
        d.start()
        return d

    def to_partner(k, src, dst):
        return remote(src, dst, pair_send.at[k], pair_recv.at[k], partner)

    pair_copies = [
        to_partner(0, stage_out, stage_in),
        to_partner(1, idx_stage_out, idx_stage_in),
        to_partner(2, iq_any.at[1 - c], vidx.at[1]),
        to_partner(3, mq_any.at[1 - c], vmq.at[1]),
        to_partner(4, w_all.at[1 - c], w_ref.at[pl.ds(2, 2)]),
    ]
    mine = jnp.where(c == 0, lat[:, :KD], lat[:, KD:])
    idx_mine = jnp.where(c == 0, rows[:, :IDX_DIM], rows[:, IDX_DIM:]).astype(BF16)
    w_ref[0:2] = w_all[c]
    pair_copies[0].wait_recv()
    pair_copies[1].wait_recv()
    from_partner = stage_in[:, :KD]
    both = jnp.concatenate([jnp.where(c == 0, mine, from_partner), jnp.where(c == 0, from_partner, mine)], axis=1)
    pq[0, me] = both[:HALF]
    pq[1, me] = both[HALF:]
    idx_other = idx_stage_in[...]
    idxg[x, z, 0:16] = jnp.where(c == 0, idx_mine, idx_other)
    idxg[x, z, 16:32] = jnp.where(c == 0, idx_other, idx_mine)

    counter = [0]
    live = {}

    def send(part, axis, way, dx, dz, lo, hi):
        k = counter[0]
        counter[0] += 1

        def block(ox, oz):
            return pq.at[part, (x + ox + 2 * NX) % NX * NZ + (z + oz + 2 * NZ) % NZ, pl.ds(lo, hi - lo)]

        out = remote(block(dx, dz), block(dx, dz), ring_send.at[k], ring_recv.at[k], ring[(axis, way)])
        here = block(dx - way, dz) if axis == "x" else block(dx, dz - way)
        arrival = pltpu.make_async_remote_copy(
            src_ref=here, dst_ref=here, send_sem=ring_send.at[k], recv_sem=ring_recv.at[k],
            device_id=ring[(axis, way)], device_id_type=MESH,
        )
        live[k] = [out, arrival, False]
        return k

    def arrived(k):
        if not live[k][2]:
            live[k][1].wait_recv()
            live[k][2] = True

    last_x, last_z = NX // 2, NZ // 2

    def hop(part, axis, dx, dz, step, before):
        last = last_x if axis == "x" else last_z
        ks = []
        for way, half in ((1, (0, 16)), (-1, (16, 32))):
            if before is not None:
                arrived(before[0 if way == 1 else 1])
            away = -way * (step - 1)
            ox, oz = (away, dz) if axis == "x" else (dx, away)
            lo, hi = half if step == last else (0, 32)
            ks.append(send(part, axis, way, ox, oz, lo, hi))
        return ks

    zp, xq, zq = {}, {}, {}

    def start_p(dx):
        zp[dx] = {1: hop(0, "z", dx, 0, 1, None)}

    def advance_p(dx, step):
        zp[dx][step] = hop(0, "z", dx, 0, step, zp[dx][step - 1])

    def advance_q(step):
        before = zq[step - 1]
        if step <= last_z:
            zq[step] = hop(1, "z", 0, 0, step, before)
        else:
            arrived(before[0])
            arrived(before[1])
        for dz in (-(step - 1), step - 1) if step <= last_z else (last_z,):
            xq[dz] = {1: hop(1, "x", 0, dz, 1, None)}

    def finish_q(dz):
        xq[dz][2] = hop(1, "x", 0, dz, 2, xq[dz][1])

    idx_z = [
        remote(idxg.at[x, z], idxg.at[x, z], idx_z_sem.at[0, d - 1], idx_z_sem.at[1, d - 1], peers_z[d - 1])
        for d in range(1, NZ)
    ]
    idx_x = []

    def spread_index():
        for d in range(1, NZ):
            ref = idxg.at[x, (z - d + NZ) % NZ]
            pltpu.make_async_remote_copy(
                src_ref=ref, dst_ref=ref, send_sem=idx_z_sem.at[0, d - 1], recv_sem=idx_z_sem.at[1, d - 1],
                device_id=peers_z[d - 1], device_id_type=MESH,
            ).wait_recv()
        for d in range(1, NX):
            idx_x.append(
                remote(idxg.at[x], idxg.at[x], idx_x_sem.at[0, d - 1], idx_x_sem.at[1, d - 1], peers_x[d - 1])
            )

    def have_index():
        for d in range(1, NX):
            ref = idxg.at[(x - d + NX) % NX]
            pltpu.make_async_remote_copy(
                src_ref=ref, dst_ref=ref, send_sem=idx_x_sem.at[0, d - 1], recv_sem=idx_x_sem.at[1, d - 1],
                device_id=peers_x[d - 1], device_id_type=MESH,
            ).wait_recv()
        sort_index_keys(inverse, idxg, slots32, sorted32, idx_keys)

    logit_tops = [(jnp.full((8, 128), NEG, F32),) * 2 for _ in range(2)]
    stat_copies = []

    def logits(pair, first, last):
        logit_tops[pair] = lax.fori_loop(
            first, last,
            lambda i, t: logit_step(table, pair, i, y, idx_keys, idx_q, w_ref, inner_ref, logit_ref, t),
            logit_tops[pair],
        )
        if last == ENTRIES:
            logit_stats(table, pair, logit_ref, stat_ref, logit_tops[pair])

    def send_stats():
        for d in range(1, NY):
            stat_copies.append(
                remote(stat_ref, stats_ref.at[d], stat_send.at[d - 1], stat_recv.at[d - 1], peers_y[d - 1])
            )
        stats_ref[0] = stat_ref[...]

    def own_queries():
        loads[0].wait()
        split_heads(0, vmq, queries)

    def own_index_queries():
        loads[1].wait()
        pair_copies[4].wait_recv()
        split_index_heads(0, vidx, idx_q)

    def other_index_queries():
        pair_copies[2].wait_recv()
        split_index_heads(1, vidx, idx_q)

    def other_queries():
        pair_copies[3].wait_recv()
        split_heads(1, vmq, queries)

    work = [own_index_queries, spread_index, own_queries, have_index]
    work += [functools.partial(logits, 0, k, k + 3) for k in (0, 3, 6)]
    work += [other_index_queries]
    work += [functools.partial(logits, 1, k, k + 3) for k in (0, 3, 6)]
    work += [send_stats, other_queries]

    def between():
        if work:
            work.pop(0)()

    start_p(0)
    xp = hop(0, "x", 0, 0, 1, None)
    zq[1] = hop(1, "z", 0, 0, 1, None)
    xq[0] = {1: hop(1, "x", 0, 0, 1, None)}
    between()
    xp2 = hop(0, "x", 0, 0, 2, xp)
    start_p(-1)
    start_p(1)
    between()
    advance_p(0, 2)
    advance_q(2)
    finish_q(0)
    between()
    arrived(xp2[0])
    arrived(xp2[1])
    start_p(2)
    between()
    advance_p(-1, 2)
    advance_p(1, 2)
    between()
    advance_p(0, 3)
    advance_q(3)
    between()
    finish_q(-1)
    finish_q(1)
    advance_p(2, 2)
    between()
    advance_p(-1, 3)
    advance_p(1, 3)
    between()
    advance_p(0, 4)
    advance_q(4)
    between()
    finish_q(-2)
    finish_q(2)
    advance_p(2, 3)
    between()
    advance_p(-1, 4)
    advance_p(1, 4)
    between()
    advance_q(5)
    finish_q(-3)
    finish_q(3)
    between()
    advance_p(2, 4)
    finish_q(last_z)
    while work:
        between()
    for k in live:
        arrived(k)
    sort_keys(inverse, pq, keys)

    tgt_copies = []
    for pair in range(2):
        targets(table, pair, keys, queries, scores, tgt_ref)
        tgt_copies.append(
            [
                remote(
                    tgt_ref.at[(y + d) % NY, pair], arrive.at[d - 1, pair], tgt_send.at[pair, d - 1],
                    tgt_recv.at[pair, d - 1], peers_y[d - 1],
                )
                for d in range(1, NY)
            ]
        )
    for d in stat_copies:
        d.wait_recv()
    for pair in range(2):
        norms = [norms_of(stats_ref, 2 * pair + half) for half in range(2)]
        for d in tgt_copies[pair]:
            d.wait_recv()

        def step(i, carry):
            gradient_step(
                table, pair, i, y, idx_q, w_ref, inner_ref, logit_ref, tgt_ref, arrive, norms, grad_ref
            )
            return carry

        lax.fori_loop(0, 9, step, 0)
    collect_gradients(table, order, grad_ref, sorted32, part_ref)
    scatter(
        x, z, c, y, peers_x, peers_z, remote, part_ref, out_ref, xa, za, xb, zb, slab_x, slab_z, tail, pieces,
        xa_sem, za_sem, xb_sem, zb_sem, piece_sem,
    )
    for k in live:
        live[k][0].wait_send()
    for d in pair_copies + idx_z + idx_x + stat_copies + tgt_copies[0] + tgt_copies[1]:
        d.wait_send()


RING_COPIES = 76


def whole_call(table, order, inverse, lat, idx, w_all, mq, iq):
    any_spec = pl.BlockSpec(memory_space=pl.ANY)
    vmem = pl.BlockSpec(memory_space=pltpu.VMEM)
    smem = pl.BlockSpec(memory_space=pltpu.SMEM)
    dma = pltpu.SemaphoreType.DMA
    return pl.pallas_call(
        whole_kernel,
        name="indexer_key_gradient",
        out_shape=jax.ShapeDtypeStruct((16, 2 * IDX_DIM), F32),
        in_specs=[smem] * 3 + [vmem] * 3 + [any_spec] * 2,
        out_specs=vmem,
        scratch_shapes=[
            pltpu.VMEM((2, NX * NZ, HALF, 2 * KD), BF16),
            pltpu.VMEM((TOK, KPAD), BF16),
            pltpu.VMEM((TOK, KPAD), BF16),
            pltpu.VMEM((TOK, 2 * IDX_DIM), F32),
            pltpu.VMEM((16, IDX_DIM), BF16),
            pltpu.VMEM((16, IDX_DIM), BF16),
            pltpu.VMEM((NX, NZ, 32, IDX_DIM), BF16),
            pltpu.VMEM((HALVES, 8, IDX_DIM), F32),
            pltpu.VMEM((HALVES, 8, IDX_DIM), F32),
            pltpu.VMEM((8, 128, IDX_DIM), BF16),
            pltpu.VMEM((2, TOK, HEADS_DEV * KD), BF16),
            pltpu.VMEM((4, LANES, KPAD), BF16),
            pltpu.VMEM((8, 512, KPAD), BF16),
            pltpu.VMEM((ENTRIES, 512, LANES), F32),
            pltpu.VMEM((NY, 2, SLOTS, 8, 128), F32),
            pltpu.VMEM((2, TOK, IDX_HEADS * IDX_DIM), BF16),
            pltpu.VMEM((4, IDX_HEADS * HALF, IDX_DIM), BF16),
            pltpu.VMEM((4, 1, IDX_HEADS * HALF), F32),
            pltpu.VMEM((2, ENTRIES, 128, IDX_HEADS * HALF), BF16),
            pltpu.VMEM((2, ENTRIES, 128, 128), F32),
            pltpu.VMEM((8, 128), F32),
            pltpu.VMEM((NY, 8, 128), F32),
            pltpu.VMEM((NY - 1, 2, SLOTS, 8, 128), F32),
            pltpu.VMEM((2, ENTRIES, 128, IDX_DIM), F32),
            pltpu.VMEM((NX, NZ, 32, IDX_DIM), F32),
            pltpu.VMEM((NX - 1, NZ, 16, IDX_DIM), F32),
            pltpu.VMEM((NZ - 1, NX, 16, IDX_DIM), F32),
            pltpu.VMEM((NX - 1, 16, IDX_DIM), F32),
            pltpu.VMEM((NZ - 1, 16, IDX_DIM), F32),
            pltpu.VMEM((NZ, 16, IDX_DIM), F32),
            pltpu.VMEM((NX, 16, IDX_DIM), F32),
            pltpu.VMEM((32, IDX_DIM), F32),
            pltpu.VMEM((4, 8, IDX_DIM), F32),
            dma((2,)),
            dma((5,)),
            dma((5,)),
            dma((RING_COPIES,)),
            dma((RING_COPIES,)),
            dma((2, NZ - 1)),
            dma((2, NX - 1)),
            dma((2, NY - 1)),
            dma((2, NY - 1)),
            dma((NY - 1,)),
            dma((NY - 1,)),
            dma((2, NX - 1)),
            dma((2, NZ - 1)),
            dma((2, NX - 1)),
            dma((2, NZ - 1)),
            dma((2, 4)),
        ],
        compiler_params=pltpu.CompilerParams(
            collective_id=0, has_side_effects=True, vmem_limit_bytes=VMEM_BYTES
        ),
    )(table, order, inverse, lat, idx, w_all, mq, iq)


def per_device(mla_queries, latent_keys, index_queries, index_keys, head_weights, block_order):
    s = lax.axis_index("seq")
    mine = lax.dynamic_slice(block_order, (2 * s,), (2,))
    others = lax.dynamic_slice(block_order, (2 * (s + 1 - 2 * (s % 2)),), (2,))
    table = entry_table(jnp.stack([mine, others]))
    slots = jnp.arange(HALVES, dtype=jnp.int32)
    inverse = jnp.sum(jnp.where(block_order[None, :] == slots[:, None], slots[None, :], 0), axis=1)
    w_all = head_weights.reshape(2, HALF, 2, IDX_HEADS).transpose(2, 0, 3, 1).reshape(2, 2, 1, IDX_HEADS * HALF)
    return whole_call(table, block_order, inverse, latent_keys, index_keys, w_all, mla_queries, index_queries)


def solution(mesh):
    return jax.shard_map(
        per_device,
        mesh=mesh,
        in_specs=(
            P(None, "seq", "head"),
            P("seq", None),
            P(None, "seq", None),
            P("seq", None),
            P("seq", None),
            P(),
        ),
        out_specs=P(("seq", "head"), None),
        check_vma=False,
    )
```

```python
import functools

import jax
import jax.numpy as jnp
from jax import lax
from jax.experimental import pallas as pl
from jax.experimental.pallas import tpu as pltpu
from jax.sharding import PartitionSpec as P

MESH = pl.DeviceIdType.MESH
NX, NZ, NY = 4, 8, 4
HEADS = 64
HEADS_DEV = 16
KD = 576
KPAD = 640
IDX_HEADS = 64
IDX_DIM = 128
TOK = 64
HALF = 32
HALVES = 128
SLOTS = 36
SCORE_SCALE = 192.0 ** (-0.5)
LOG2E = 1.4426950408889634
INDEX_NORM = (IDX_HEADS * IDX_DIM) ** (-0.5)
GRAD_COEF = 1024.0 * INDEX_NORM
NEG = -1e30
VMEM_BYTES = 60 * 1024 * 1024
F32 = jnp.float32
BF16 = jnp.bfloat16


def coords():
    s = lax.axis_index("seq")
    y = lax.axis_index("head")
    return s // (2 * NZ), (s // 2) % NZ, s % 2, y


def seq_at(x, z, c):
    return (x * NZ + z) * 2 + c


ENTRIES = 9


def fill_table(order, seq, table):
    for pair in range(2):
        device = seq if pair == 0 else seq + 1 - 2 * (seq % 2)
        early_place, late_place = order[2 * device], order[2 * device + 1]
        for i in range(ENTRIES):
            k = i - 5
            flip = jnp.where(early_place // 16 >= k, 1, 0)
            early = 1 if i == 0 else 0 if i < 6 else flip
            block = 0 if i == 0 else i - 1 if i < 6 else flip * k + (1 - flip) * (8 - k)
            place = early * early_place + (1 - early) * late_place
            fields = (early, 2 * pair + 1 - early, block, place * HALF - block * 512)
            for field, value in enumerate(fields):
                table[(field * 2 + pair) * ENTRIES + i] = jnp.int32(value)


def entry(table, pair, i):
    return [table[(field * 2 + pair) * ENTRIES + i] for field in range(4)]


def mask_of(flag, shape):
    return jnp.zeros(shape, jnp.int32) + flag > 0


def split_cores(pq, slots, part, chip, lo, hi):
    pad = jnp.zeros((hi - lo, KPAD - KD), BF16)
    for core in range(2):
        rows = pq[part, chip, lo:hi, core * KD : (core + 1) * KD]
        slots[4 * chip + 2 * core + part, lo:hi, :] = jnp.concatenate([rows, pad], axis=1)


def sort_keys(first, slots, keys):
    def step(p, carry):
        slot = first[p]
        low, high = p, HALVES - 1 - p
        keys[low // 16, pl.ds(pl.multiple_of(low % 16 * HALF, HALF), HALF), :] = slots[slot]
        keys[high // 16, pl.ds(pl.multiple_of(high % 16 * HALF, HALF), HALF), :] = slots[slot + 1]
        return carry

    lax.fori_loop(0, HALVES // 2, step, 0, unroll=4)


def sort_index_keys(first, idxg, slots32, sorted32, idx_keys):
    slots32[...] = idxg[...].astype(F32).reshape(HALVES, 8, IDX_DIM)

    def step(p, carry):
        slot = first[p]
        sorted32[p] = slots32[slot]
        sorted32[HALVES - 1 - p] = slots32[slot + 1]
        return carry

    lax.fori_loop(0, HALVES // 2, step, 0, unroll=4)
    idx_keys[...] = sorted32[...].reshape(8, 128, IDX_DIM).astype(BF16)


def split_heads(pair, vmq, queries):
    pad = jnp.zeros((HALF, KPAD - KD), BF16)
    for half in range(2):
        for h in range(HEADS_DEV):
            queries[2 * pair + half, h * HALF : (h + 1) * HALF, :] = jnp.concatenate(
                [vmq[pair, half * HALF : (half + 1) * HALF, h * KD : (h + 1) * KD], pad], axis=1
            )


LANES = HEADS_DEV * HALF
EXP_SCALE = SCORE_SCALE * LOG2E


def score_step(table, pair, i, keys, queries, scores, tops):
    early, g, block, limit = entry(table, pair, i)
    early = mask_of(early, (8, LANES))
    k = keys[block]
    s = lax.dot_general(k, queries[g], (((1,), (1,)), ((), ())), preferred_element_type=F32)
    row = lax.broadcasted_iota(jnp.int32, (512, LANES), 0)
    token = lax.broadcasted_iota(jnp.int32, (512, LANES), 1) % HALF
    s = jnp.where(row - token <= limit, s, NEG)
    scores[i] = s
    m = jnp.max(s.reshape(64, 8, LANES), axis=0)
    return (
        jnp.where(early, jnp.maximum(tops[0], m), tops[0]),
        jnp.where(early, tops[1], jnp.maximum(tops[1], m)),
    )


def exp_step(table, pair, i, scores, shifts, sums):
    early = entry(table, pair, i)[0]
    row = mask_of(early, (1, LANES))
    early = mask_of(early, (8, LANES))
    e = jnp.exp2(scores[i] * EXP_SCALE - jnp.where(row, shifts[0], shifts[1]))
    scores[i] = e
    m = jnp.sum(e.reshape(64, 8, LANES), axis=0)
    return (sums[0] + jnp.where(early, m, 0.0), sums[1] + jnp.where(early, 0.0, m))


def head_step(table, pair, i, scores, weights, tgt_ref):
    early = mask_of(entry(table, pair, i)[0], (1, LANES))
    group_of = lax.broadcasted_iota(jnp.int32, (8, 128), 1) // HALF
    weight = jnp.where(early, weights[0], weights[1])
    for part in range(4):
        rows = slice(part * 128, (part + 1) * 128)
        r = scores[i, rows, 0:128] * weight[:, 0:128]
        for lt in range(1, LANES // 128):
            r = r + scores[i, rows, lt * 128 : (lt + 1) * 128] * weight[:, lt * 128 : (lt + 1) * 128]
        r = r + pltpu.roll(r, 64, 1)
        r = r + pltpu.roll(r, 32, 1)
        for y in range(NY):
            out = r[8 * y : 8 * y + 8]
            for a in range(1, 4):
                out = jnp.where(group_of == a, r[32 * a + 8 * y : 32 * a + 8 * y + 8], out)
            tgt_ref[y, pair, 4 * i + part] = out


def start_tops():
    return (jnp.full((8, LANES), NEG, F32),) * 2


def start_sums():
    return (jnp.zeros((8, LANES), F32),) * 2


def shifts_of(tops):
    return tuple(jnp.max(t, axis=0, keepdims=True) * EXP_SCALE for t in tops)


def weights_of(sums):
    return tuple(1.0 / (HEADS * jnp.sum(t, axis=0, keepdims=True)) for t in sums)


def targets(table, pair, keys, queries, scores, tgt_ref):
    tops = lax.fori_loop(0, 9, lambda i, t: score_step(table, pair, i, keys, queries, scores, t), start_tops())
    shifts = shifts_of(tops)
    sums = lax.fori_loop(0, 9, lambda i, t: exp_step(table, pair, i, scores, shifts, t), start_sums())
    weights = weights_of(sums)

    def last(i, carry):
        head_step(table, pair, i, scores, weights, tgt_ref)
        return carry

    lax.fori_loop(0, 9, last, 0)


def split_index_heads(pair, vidx, idx_q):
    for half in range(2):
        for j in range(IDX_HEADS):
            at = (j % 16 * 4 + j // 16) * HALF
            idx_q[2 * pair + half, at : at + HALF, :] = vidx[
                pair, half * HALF : (half + 1) * HALF, j * IDX_DIM : (j + 1) * IDX_DIM
            ]


def weight_rows(hw):
    turned = jnp.concatenate([hw, hw], axis=0).T
    return [
        [
            jnp.concatenate(
                [
                    turned[q * IDX_HEADS + a * 16 : q * IDX_HEADS + a * 16 + 16, half * HALF : (half + 1) * HALF]
                    for a in range(4)
                ],
                axis=1,
            )
            for half in range(2)
        ]
        for q in range(2)
    ]


def weight_cut(w_ref, g, ch):
    return jnp.concatenate([w_ref[g, 2 * ch : 2 * ch + 1, :], w_ref[g, 2 * ch + 1 : 2 * ch + 2, :]], axis=1)


def logit_step(table, pair, i, y, idx_keys, idx_q, w_ref, inner_ref, logit_ref, tops):
    early, g, block, limit = entry(table, pair, i)
    early = mask_of(early, (8, 128))
    k = idx_keys[block]
    acc = jnp.zeros((128, 128), F32)
    for ch in range(8):
        cut = slice(ch * 256, (ch + 1) * 256)
        inner = lax.dot_general(k, idx_q[g, cut, :], (((1,), (1,)), ((), ())), preferred_element_type=F32)
        inner_ref[pair, i, :, cut] = inner.astype(BF16)
        part = jnp.maximum(inner, 0.0) * weight_cut(w_ref, g, ch)
        acc = acc + part[:, :128] + part[:, 128:]
    acc = acc + pltpu.roll(acc, 64, 1)
    acc = acc + pltpu.roll(acc, 32, 1)
    row = lax.broadcasted_iota(jnp.int32, (128, 128), 0)
    token = lax.broadcasted_iota(jnp.int32, (128, 128), 1) % HALF
    offset = row // 8 * HALF + row % 8 - token
    acc = jnp.where(offset <= limit - 8 * y, acc * INDEX_NORM, NEG)
    logit_ref[pair, i] = acc
    m = jnp.max(acc.reshape(16, 8, 128), axis=0)
    return (
        jnp.where(early, jnp.maximum(tops[0], m), tops[0]),
        jnp.where(early, tops[1], jnp.maximum(tops[1], m)),
    )


def logit_stats(table, pair, logit_ref, stat_ref, tops):
    tops = [jnp.max(t, axis=0, keepdims=True) for t in tops]

    def step(i, sums):
        early = entry(table, pair, i)[0]
        row = mask_of(early, (1, 128))
        early = mask_of(early, (8, 128))
        e = jnp.exp(logit_ref[pair, i] - jnp.where(row, tops[0], tops[1]))
        e = jnp.sum(e.reshape(16, 8, 128), axis=0)
        return (sums[0] + jnp.where(early, e, 0.0), sums[1] + jnp.where(early, 0.0, e))

    sums = lax.fori_loop(0, 9, step, (jnp.zeros((8, 128), F32),) * 2, unroll=3)
    for half in range(2):
        g = 2 * pair + half
        stat_ref[g : g + 1, :] = tops[half]
        stat_ref[4 + g : 5 + g, :] = jnp.sum(sums[half], axis=0, keepdims=True)


def norms_of(stats_ref, g):
    tops = [stats_ref[d, g : g + 1, :] for d in range(NY)]
    top = jnp.maximum(jnp.maximum(tops[0], tops[1]), jnp.maximum(tops[2], tops[3]))
    norm = sum(stats_ref[d, 4 + g : 5 + g, :] * jnp.exp(tops[d] - top) for d in range(NY))
    return top, GRAD_COEF / norm


def gradient_step(table, pair, i, y, idx_q, w_ref, inner_ref, logit_ref, tgt_ref, arrive, norms, grad_ref):
    early, g, block, limit = entry(table, pair, i)
    early = mask_of(early, (1, 128))
    group_of = lax.broadcasted_iota(jnp.int32, (8, 128), 1) // HALF
    wide = []
    for part in range(4):
        at = 4 * i + part
        packed = tgt_ref[y, pair, at] + arrive[0, pair, at] + arrive[1, pair, at] + arrive[2, pair, at]
        for a in range(4):
            v = jnp.where(group_of == a, packed, 0.0)
            v = v + pltpu.roll(v, 64, 1)
            wide.append(v + pltpu.roll(v, 32, 1))
    target = jnp.concatenate(wide, axis=0)
    top = jnp.where(early, norms[0][0], norms[1][0])
    coef = jnp.where(early, norms[0][1], norms[1][1])
    row = lax.broadcasted_iota(jnp.int32, (128, 128), 0)
    token = lax.broadcasted_iota(jnp.int32, (128, 128), 1) % HALF
    offset = row // 8 * HALF + row % 8 - token
    seen = offset <= limit - 8 * y
    scaled = jnp.where(seen, jnp.exp(logit_ref[pair, i] - top) * coef - GRAD_COEF * target, 0.0)
    scaled = jnp.concatenate([scaled, scaled], axis=1)
    acc = jnp.zeros((128, IDX_DIM), F32)
    zero = jnp.zeros((), BF16)
    for ch in range(8):
        cut = slice(ch * 256, (ch + 1) * 256)
        signal = (scaled * weight_cut(w_ref, g, ch)).astype(BF16)
        signal = jnp.where(inner_ref[pair, i, :, cut] > zero, signal, zero)
        acc = acc + jnp.dot(signal, idx_q[g, cut, :], preferred_element_type=F32)
    grad_ref[pair, i] = acc


def collect_gradients(table, order, grad_ref, sorted_ref, part_ref):
    total = [grad_ref[0, 0] + grad_ref[1, 0] + grad_ref[0, 1] + grad_ref[1, 1]]
    total += [grad_ref[0, b + 1] + grad_ref[1, b + 1] for b in range(1, 5)] + [0.0] * 3
    for pair in range(2):
        for k in range(1, 4):
            flip = mask_of(entry(table, pair, k + 5)[0], (128, IDX_DIM))
            d = grad_ref[pair, k + 5]
            total[k] = total[k] + jnp.where(flip, d, 0.0)
            total[8 - k] = total[8 - k] + jnp.where(flip, 0.0, d)
    for b in range(8):
        sorted_ref[b * 16 : (b + 1) * 16] = total[b].reshape(16, 8, IDX_DIM)

    def store(chip, carry):
        for core in range(2):
            for half in range(2):
                place = order[4 * chip + 2 * core + half]
                rows = sorted_ref[place]
                part_ref[chip // NZ, chip % NZ, core * 16 + half * 8 : core * 16 + half * 8 + 8, :] = rows
        return carry

    lax.fori_loop(0, NX * NZ, store, 0, unroll=2)


def final_targets(x, z, c, y):
    return [
        (core, d, half, (seq_at(x, (z + d) % NZ, 0) if core == 0 else seq_at((x + d) % NX, z, 1), y // 2 + 2 * half))
        for core in range(2)
        for d in range(NZ if core == 0 else NX)
        for half in range(2)
    ]


def final_sources(x, z, core, y):
    return [
        (
            d,
            2 * odd + c,
            (seq_at(x, (z - d + NZ) % NZ, c) if core == 0 else seq_at((x - d + NX) % NX, z, c), 2 * (y % 2) + odd),
            d == 0 and c == core,
        )
        for d in range(NZ if core == 0 else NX)
        for odd in range(2)
        for c in range(2)
    ]


def scatter(
    x, z, c, y, peers_x, peers_z, remote, part_ref, out_ref, xa, za, slab_x, slab_z, final,
    xa_sem, za_sem, final_send, final_recv,
):
    first_z = [
        remote(
            part_ref.at[:, (z + d) % NZ, pl.ds(16, 16)], za.at[d - 1], za_sem.at[0, d - 1], za_sem.at[1, d - 1],
            peers_z[d - 1],
        )
        for d in range(1, NZ)
    ]
    first_x = [
        remote(
            part_ref.at[(x + d) % NX, :, pl.ds(0, 16)], xa.at[d - 1], xa_sem.at[0, d - 1], xa_sem.at[1, d - 1],
            peers_x[d - 1],
        )
        for d in range(1, NX)
    ]
    slot = 2 * (y % 2) + c
    ends = final_targets(x, z, c, y)

    def piece(core, d, half):
        if core == 0:
            return slab_x.at[(z + d) % NZ, pl.ds(8 * half, 8)]
        return slab_z.at[(x + d) % NX, pl.ds(8 * half, 8)]

    def last_copy(k):
        core, d, half, to = ends[k]
        return pltpu.make_async_remote_copy(
            src_ref=piece(core, d, half), dst_ref=final.at[d, slot], send_sem=final_send.at[k],
            recv_sem=final_recv.at[d, slot], device_id=to, device_id_type=MESH,
        )

    def here(k):
        core, d, half, _ = ends[k]
        return jnp.logical_and(c == core, y // 2 + 2 * half == y) if d == 0 else None

    def send_last(wanted):
        for k, (core, d, half, _) in enumerate(ends):
            if core != wanted:
                continue
            if d > 0:
                last_copy(k).start()
                continue

            @pl.when(jnp.logical_not(here(k)))
            def _(k=k):
                last_copy(k).start()

            @pl.when(here(k))
            def _(core=core, d=d, half=half):
                final[0, slot] = piece(core, d, half)[...]

    for d in first_x:
        d.wait_recv()
    slab_x[...] = part_ref[x, :, 0:16, :] + xa[0] + xa[1] + xa[2]
    send_last(0)
    for d in first_z:
        d.wait_recv()
    total = part_ref[:, z, 16:32, :]
    for k in range(NZ - 1):
        total = total + za[k]
    slab_z[...] = total
    send_last(1)
    for core in range(2):

        @pl.when(c == core)
        def _(core=core):
            for d, at, source, maybe_here in final_sources(x, z, core, y):
                ref = final.at[d, at]
                arrival = pltpu.make_async_remote_copy(
                    src_ref=ref, dst_ref=ref, send_sem=final_send.at[0], recv_sem=final_recv.at[d, at],
                    device_id=source, device_id_type=MESH,
                )
                if maybe_here:
                    pl.when(source[1] != y)(arrival.wait_recv)
                else:
                    arrival.wait_recv()
            for at in range(4):
                total = final[0, at]
                for d in range(1, NZ if core == 0 else NX):
                    total = total + final[d, at]
                out_ref[at // 2 * 8 : at // 2 * 8 + 8, at % 2 * IDX_DIM : (at % 2 + 1) * IDX_DIM] = total

    for k, (core, d, half, _) in enumerate(ends):
        if d > 0:
            last_copy(k).wait_send()
        else:
            pl.when(jnp.logical_not(here(k)))(last_copy(k).wait_send)
    for d in first_x + first_z:
        d.wait_send()


def whole_kernel(
    order, first, lat_any, idx_any, hw_any, mq_any, iq_any, out_ref,
    table, lat_ref, idx_ref, hw_ref, w_other, pq, slots, stage_out, stage_in, idx32, idx_stage_out, idx_stage_in, idxg, slots32, sorted32, idx_keys,
    vmq, queries, keys, scores, tgt_ref, vidx, idx_q, w_ref, inner_ref, logit_ref, stat_ref, stats_ref, arrive,
    grad_ref, part_ref, xa, za, slab_x, slab_z, final,
    load_sem, pair_send, pair_recv, ring_send, ring_recv, idx_z_sem, idx_x_sem,
    tgt_send, tgt_recv, stat_send, stat_recv, xa_sem, za_sem, final_send, final_recv,
):
    x, z, c, y = coords()
    seq = lax.axis_index("seq")
    me = x * NZ + z
    barrier = pltpu.get_barrier_semaphore()
    partner = (seq_at(x, z, 1 - c), y)
    peers_y = [(seq, (y + d) % NY) for d in range(1, NY)]
    peers_x = [(seq_at((x + d) % NX, z, c), y) for d in range(1, NX)]
    peers_z = [(seq_at(x, (z + d) % NZ, c), y) for d in range(1, NZ)]
    ring = {("x", 1): peers_x[0], ("x", -1): peers_x[-1], ("z", 1): peers_z[0], ("z", -1): peers_z[-1]}

    def tell(to):
        pl.semaphore_signal(barrier, inc=1, device_id=to, device_id_type=MESH)

    for to in peers_x + peers_z + peers_y + [partner]:
        tell(to)
    loads = [
        pltpu.make_async_copy(src, dst, load_sem.at[k])
        for k, (src, dst) in enumerate(
            [
                (lat_any, lat_ref), (idx_any, idx_ref), (hw_any, hw_ref), (iq_any.at[c], vidx.at[0]),
                (mq_any.at[c], vmq.at[0]),
            ]
        )
    ]
    for d in loads:
        d.start()
    for core in range(2):

        @pl.when(c == core)
        def _(core=core):
            for _, _, source, maybe_here in final_sources(x, z, core, y):
                if maybe_here:
                    pl.when(source[1] != y)(functools.partial(tell, source))
                else:
                    tell(source)

    fill_table(order, seq, table)
    for d in loads[:3]:
        d.wait()
    weights = weight_rows(hw_ref[...])
    for half in range(2):
        w_other[half] = jnp.where(c == 0, weights[1][half], weights[0][half])
        w_ref[half] = jnp.where(c == 0, weights[0][half], weights[1][half])
    lat = lat_ref[...]
    stage_out[:, 0:KD] = jnp.where(c == 0, lat[:, KD:], lat[:, :KD])
    stage_out[:, KD:] = jnp.zeros((TOK, KPAD - KD), BF16)
    idx32[...] = idx_ref[...].astype(F32)
    rows = jnp.concatenate(
        [idx32[pl.ds(pl.multiple_of(y * 8, 8), 8), :], idx32[pl.ds(pl.multiple_of(HALF + y * 8, 8), 8), :]], axis=0
    )
    idx_stage_out[...] = jnp.where(c == 0, rows[:, IDX_DIM:], rows[:, :IDX_DIM]).astype(BF16)
    own = jnp.where(jnp.logical_or(y == 0, y == NY - 1), 1, 0)
    pl.semaphore_wait(barrier, NX - 1 + NZ - 1 + NY - 1 + 1 + 2 * (NZ + NX) - own)

    def remote(src, dst, send, recv, to):
        d = pltpu.make_async_remote_copy(
            src_ref=src, dst_ref=dst, send_sem=send, recv_sem=recv, device_id=to, device_id_type=MESH
        )
        d.start()
        return d

    def to_partner(k, src, dst):
        return remote(src, dst, pair_send.at[k], pair_recv.at[k], partner)

    pair_copies = [
        to_partner(0, stage_out, stage_in),
        to_partner(1, idx_stage_out, idx_stage_in),
        to_partner(2, iq_any.at[1 - c], vidx.at[1]),
        to_partner(3, mq_any.at[1 - c], vmq.at[1]),
        to_partner(4, w_other, w_ref.at[pl.ds(2, 2)]),
    ]
    mine = jnp.where(c == 0, lat[:, :KD], lat[:, KD:])
    idx_mine = jnp.where(c == 0, rows[:, :IDX_DIM], rows[:, IDX_DIM:]).astype(BF16)
    pair_copies[0].wait_recv()
    pair_copies[1].wait_recv()
    from_partner = stage_in[:, :KD]
    both = jnp.concatenate([jnp.where(c == 0, mine, from_partner), jnp.where(c == 0, from_partner, mine)], axis=1)
    pq[0, me] = both[:HALF]
    pq[1, me] = both[HALF:]
    idx_other = idx_stage_in[...]
    idxg[x, z, 0:16] = jnp.where(c == 0, idx_mine, idx_other)
    idxg[x, z, 16:32] = jnp.where(c == 0, idx_other, idx_mine)

    counter = [0]
    live, origin = {}, {}
    landed = [(0, me, 0, HALF), (1, me, 0, HALF)]

    def send(part, axis, way, dx, dz, lo, hi):
        k = counter[0]
        counter[0] += 1

        def block(ox, oz):
            return pq.at[part, (x + ox + 2 * NX) % NX * NZ + (z + oz + 2 * NZ) % NZ, pl.ds(lo, hi - lo)]

        out = remote(block(dx, dz), block(dx, dz), ring_send.at[k], ring_recv.at[k], ring[(axis, way)])
        here = block(dx - way, dz) if axis == "x" else block(dx, dz - way)
        arrival = pltpu.make_async_remote_copy(
            src_ref=here, dst_ref=here, send_sem=ring_send.at[k], recv_sem=ring_recv.at[k],
            device_id=ring[(axis, way)], device_id_type=MESH,
        )
        live[k] = [out, arrival, False]
        ix, iz = (dx - way, dz) if axis == "x" else (dx, dz - way)
        origin[k] = (part, (x + ix + 2 * NX) % NX * NZ + (z + iz + 2 * NZ) % NZ, lo, hi)
        return k

    def arrived(k):
        if not live[k][2]:
            live[k][1].wait_recv()
            live[k][2] = True
            landed.append(origin[k])

    last_x, last_z = NX // 2, NZ // 2

    def hop(part, axis, dx, dz, step, before):
        last = last_x if axis == "x" else last_z
        ks = []
        for way, half in ((1, (0, 16)), (-1, (16, 32))):
            if before is not None:
                arrived(before[0 if way == 1 else 1])
            away = -way * (step - 1)
            ox, oz = (away, dz) if axis == "x" else (dx, away)
            lo, hi = half if step == last else (0, 32)
            ks.append(send(part, axis, way, ox, oz, lo, hi))
        return ks

    zp, xq, zq = {}, {}, {}

    def start_p(dx):
        zp[dx] = {1: hop(0, "z", dx, 0, 1, None)}

    def advance_p(dx, step):
        zp[dx][step] = hop(0, "z", dx, 0, step, zp[dx][step - 1])

    def advance_q(step):
        before = zq[step - 1]
        if step <= last_z:
            zq[step] = hop(1, "z", 0, 0, step, before)
        else:
            arrived(before[0])
            arrived(before[1])
        for dz in (-(step - 1), step - 1) if step <= last_z else (last_z,):
            xq[dz] = {1: hop(1, "x", 0, dz, 1, None)}

    def finish_q(dz):
        xq[dz][2] = hop(1, "x", 0, dz, 2, xq[dz][1])

    idx_z = [
        remote(idxg.at[x, z], idxg.at[x, z], idx_z_sem.at[0, d - 1], idx_z_sem.at[1, d - 1], peers_z[d - 1])
        for d in range(1, NZ)
    ]
    idx_x = []

    def spread_index():
        for d in range(1, NZ):
            ref = idxg.at[x, (z - d + NZ) % NZ]
            pltpu.make_async_remote_copy(
                src_ref=ref, dst_ref=ref, send_sem=idx_z_sem.at[0, d - 1], recv_sem=idx_z_sem.at[1, d - 1],
                device_id=peers_z[d - 1], device_id_type=MESH,
            ).wait_recv()
        for d in range(1, NX):
            idx_x.append(
                remote(idxg.at[x], idxg.at[x], idx_x_sem.at[0, d - 1], idx_x_sem.at[1, d - 1], peers_x[d - 1])
            )

    def have_index():
        for d in range(1, NX):
            ref = idxg.at[(x - d + NX) % NX]
            pltpu.make_async_remote_copy(
                src_ref=ref, dst_ref=ref, send_sem=idx_x_sem.at[0, d - 1], recv_sem=idx_x_sem.at[1, d - 1],
                device_id=peers_x[d - 1], device_id_type=MESH,
            ).wait_recv()
        sort_index_keys(first, idxg, slots32, sorted32, idx_keys)

    logit_tops = [(jnp.full((8, 128), NEG, F32),) * 2 for _ in range(2)]
    stat_copies = []

    def logits(pair, first, last):
        logit_tops[pair] = lax.fori_loop(
            first, last,
            lambda i, t: logit_step(table, pair, i, y, idx_keys, idx_q, w_ref, inner_ref, logit_ref, t),
            logit_tops[pair],
        )
        if last == ENTRIES:
            logit_stats(table, pair, logit_ref, stat_ref, logit_tops[pair])

    def send_stats():
        for d in range(1, NY):
            stat_copies.append(
                remote(stat_ref, stats_ref.at[d], stat_send.at[d - 1], stat_recv.at[d - 1], peers_y[d - 1])
            )
        stats_ref[0] = stat_ref[...]

    def own_queries():
        loads[4].wait()
        split_heads(0, vmq, queries)

    def own_index_queries():
        loads[3].wait()
        pair_copies[4].wait_recv()
        split_index_heads(0, vidx, idx_q)

    def other_index_queries():
        pair_copies[2].wait_recv()
        split_index_heads(1, vidx, idx_q)

    def other_queries():
        pair_copies[3].wait_recv()
        split_heads(1, vmq, queries)

    work = [own_index_queries, spread_index, own_queries, have_index]
    work += [functools.partial(logits, 0, k, k + 3) for k in (0, 3, 6)]
    work += [other_index_queries]
    work += [functools.partial(logits, 1, k, k + 3) for k in (0, 3, 6)]
    work += [send_stats, other_queries]

    def between():
        if work:
            work.pop(0)()
        for _ in range(min(4, len(landed))):
            split_cores(pq, slots, *landed.pop(0))

    start_p(0)
    xp = hop(0, "x", 0, 0, 1, None)
    zq[1] = hop(1, "z", 0, 0, 1, None)
    xq[0] = {1: hop(1, "x", 0, 0, 1, None)}
    between()
    xp2 = hop(0, "x", 0, 0, 2, xp)
    start_p(-1)
    start_p(1)
    between()
    advance_p(0, 2)
    advance_q(2)
    finish_q(0)
    between()
    arrived(xp2[0])
    arrived(xp2[1])
    start_p(2)
    between()
    advance_p(-1, 2)
    advance_p(1, 2)
    between()
    advance_p(0, 3)
    advance_q(3)
    between()
    finish_q(-1)
    finish_q(1)
    advance_p(2, 2)
    between()
    advance_p(-1, 3)
    advance_p(1, 3)
    between()
    advance_p(0, 4)
    advance_q(4)
    between()
    finish_q(-2)
    finish_q(2)
    advance_p(2, 3)
    between()
    advance_p(-1, 4)
    advance_p(1, 4)
    between()
    advance_q(5)
    finish_q(-3)
    finish_q(3)
    between()
    advance_p(2, 4)
    finish_q(last_z)
    while work:
        between()
    for k in live:
        arrived(k)
        while landed:
            split_cores(pq, slots, *landed.pop(0))
    sort_keys(first, slots, keys)

    tgt_copies = []
    for pair in range(2):
        targets(table, pair, keys, queries, scores, tgt_ref)
        tgt_copies.append(
            [
                remote(
                    tgt_ref.at[(y + d) % NY, pair], arrive.at[d - 1, pair], tgt_send.at[pair, d - 1],
                    tgt_recv.at[pair, d - 1], peers_y[d - 1],
                )
                for d in range(1, NY)
            ]
        )
    for d in stat_copies:
        d.wait_recv()
    for pair in range(2):
        norms = [norms_of(stats_ref, 2 * pair + half) for half in range(2)]
        for d in tgt_copies[pair]:
            d.wait_recv()

        def step(i, carry):
            gradient_step(
                table, pair, i, y, idx_q, w_ref, inner_ref, logit_ref, tgt_ref, arrive, norms, grad_ref
            )
            return carry

        lax.fori_loop(0, 9, step, 0)
    collect_gradients(table, order, grad_ref, sorted32, part_ref)
    scatter(
        x, z, c, y, peers_x, peers_z, remote, part_ref, out_ref, xa, za, slab_x, slab_z, final,
        xa_sem, za_sem, final_send, final_recv,
    )
    for k in live:
        live[k][0].wait_send()
    for d in pair_copies + idx_z + idx_x + stat_copies + tgt_copies[0] + tgt_copies[1]:
        d.wait_send()


RING_COPIES = 76


def whole_call(order, first, lat, idx, hw, mq, iq):
    any_spec = pl.BlockSpec(memory_space=pl.ANY)
    vmem = pl.BlockSpec(memory_space=pltpu.VMEM)
    smem = pl.BlockSpec(memory_space=pltpu.SMEM)
    dma = pltpu.SemaphoreType.DMA
    return pl.pallas_call(
        whole_kernel,
        name="indexer_key_gradient",
        out_shape=jax.ShapeDtypeStruct((16, 2 * IDX_DIM), F32),
        in_specs=[smem] * 2 + [any_spec] * 5,
        out_specs=vmem,
        scratch_shapes=[
            pltpu.SMEM((8 * ENTRIES,), jnp.int32),
            pltpu.VMEM((TOK, 2 * KD), BF16),
            pltpu.VMEM((TOK, 2 * IDX_DIM), BF16),
            pltpu.VMEM((TOK, 2 * IDX_HEADS), F32),
            pltpu.VMEM((2, 16, 128), F32),
            pltpu.VMEM((2, NX * NZ, HALF, 2 * KD), BF16),
            pltpu.VMEM((HALVES, HALF, KPAD), BF16),
            pltpu.VMEM((TOK, KPAD), BF16),
            pltpu.VMEM((TOK, KPAD), BF16),
            pltpu.VMEM((TOK, 2 * IDX_DIM), F32),
            pltpu.VMEM((16, IDX_DIM), BF16),
            pltpu.VMEM((16, IDX_DIM), BF16),
            pltpu.VMEM((NX, NZ, 32, IDX_DIM), BF16),
            pltpu.VMEM((HALVES, 8, IDX_DIM), F32),
            pltpu.VMEM((HALVES, 8, IDX_DIM), F32),
            pltpu.VMEM((8, 128, IDX_DIM), BF16),
            pltpu.VMEM((2, TOK, HEADS_DEV * KD), BF16),
            pltpu.VMEM((4, LANES, KPAD), BF16),
            pltpu.VMEM((8, 512, KPAD), BF16),
            pltpu.VMEM((ENTRIES, 512, LANES), F32),
            pltpu.VMEM((NY, 2, SLOTS, 8, 128), F32),
            pltpu.VMEM((2, TOK, IDX_HEADS * IDX_DIM), BF16),
            pltpu.VMEM((4, IDX_HEADS * HALF, IDX_DIM), BF16),
            pltpu.VMEM((4, 16, 128), F32),
            pltpu.VMEM((2, ENTRIES, 128, IDX_HEADS * HALF), BF16),
            pltpu.VMEM((2, ENTRIES, 128, 128), F32),
            pltpu.VMEM((8, 128), F32),
            pltpu.VMEM((NY, 8, 128), F32),
            pltpu.VMEM((NY - 1, 2, SLOTS, 8, 128), F32),
            pltpu.VMEM((2, ENTRIES, 128, IDX_DIM), F32),
            pltpu.VMEM((NX, NZ, 32, IDX_DIM), F32),
            pltpu.VMEM((NX - 1, NZ, 16, IDX_DIM), F32),
            pltpu.VMEM((NZ - 1, NX, 16, IDX_DIM), F32),
            pltpu.VMEM((NZ, 16, IDX_DIM), F32),
            pltpu.VMEM((NX, 16, IDX_DIM), F32),
            pltpu.VMEM((NZ, 4, 8, IDX_DIM), F32),
            dma((5,)),
            dma((5,)),
            dma((5,)),
            dma((RING_COPIES,)),
            dma((RING_COPIES,)),
            dma((2, NZ - 1)),
            dma((2, NX - 1)),
            dma((2, NY - 1)),
            dma((2, NY - 1)),
            dma((NY - 1,)),
            dma((NY - 1,)),
            dma((2, NX - 1)),
            dma((2, NZ - 1)),
            dma((2 * (NX + NZ),)),
            dma((NZ, 4)),
        ],
        compiler_params=pltpu.CompilerParams(
            collective_id=0, has_side_effects=True, vmem_limit_bytes=VMEM_BYTES
        ),
    )(order, first, lat, idx, hw, mq, iq)


def per_device(mla_queries, latent_keys, index_queries, index_keys, head_weights, block_order):
    early = block_order.reshape(HALVES // 2, 2)[:, 0]
    ids = jnp.arange(HALVES // 2, dtype=jnp.int32)
    first = jnp.sum(jnp.where(early[None, :] == ids[:, None], 2 * ids[None, :], 0), axis=1)
    return whole_call(block_order, first, latent_keys, index_keys, head_weights, mla_queries, index_queries)


def solution(mesh):
    return jax.shard_map(
        per_device,
        mesh=mesh,
        in_specs=(
            P(None, "seq", "head"),
            P("seq", None),
            P(None, "seq", None),
            P("seq", None),
            P("seq", None),
            P(),
        ),
        out_specs=P(("seq", "head"), None),
        check_vma=False,
    )
```

```python
import functools

import jax
import jax.numpy as jnp
from jax import lax
from jax.experimental import pallas as pl
from jax.experimental.pallas import tpu as pltpu
from jax.sharding import PartitionSpec as P

MESH = pl.DeviceIdType.MESH
NX, NZ, NY = 4, 8, 4
HEADS = 64
HEADS_DEV = 16
KD = 576
KPAD = 640
IDX_HEADS = 64
IDX_DIM = 128
TOK = 64
HALF = 32
HALVES = 128
SLOTS = 36
SCORE_SCALE = 192.0 ** (-0.5)
LOG2E = 1.4426950408889634
INDEX_NORM = (IDX_HEADS * IDX_DIM) ** (-0.5)
GRAD_COEF = 1024.0 * INDEX_NORM
NEG = -1e30
VMEM_BYTES = 60 * 1024 * 1024
F32 = jnp.float32
BF16 = jnp.bfloat16


def coords():
    s = lax.axis_index("seq")
    y = lax.axis_index("head")
    return s // (2 * NZ), (s // 2) % NZ, s % 2, y


def seq_at(x, z, c):
    return (x * NZ + z) * 2 + c


ENTRIES = 9


def fill_table(order, seq, table):
    for pair in range(2):
        device = seq if pair == 0 else seq + 1 - 2 * (seq % 2)
        early_place, late_place = order[2 * device], order[2 * device + 1]
        for i in range(ENTRIES):
            k = i - 5
            flip = jnp.where(early_place // 16 >= k, 1, 0)
            early = 1 if i == 0 else 0 if i < 6 else flip
            block = 0 if i == 0 else i - 1 if i < 6 else flip * k + (1 - flip) * (8 - k)
            place = early * early_place + (1 - early) * late_place
            fields = (early, 2 * pair + 1 - early, block, place * HALF - block * 512)
            for field, value in enumerate(fields):
                table[(field * 2 + pair) * ENTRIES + i] = jnp.int32(value)


def entry(table, pair, i):
    return [table[(field * 2 + pair) * ENTRIES + i] for field in range(4)]


def mask_of(flag, shape):
    return jnp.zeros(shape, jnp.int32) + flag > 0


P_LANES = 7 * 128
Q_LANES = 4 * KD - P_LANES


def split_cores(p_ref, q_ref, slots, part, chip, lo, hi):
    pad = jnp.zeros((hi - lo, KPAD - KD), BF16)

    def padded(rows):
        return jnp.concatenate([rows, pad], axis=1)

    if part == 0:
        slots[4 * chip, lo:hi, :] = padded(p_ref[chip, lo:hi, :KD])
        slots[4 * chip + 2, lo:hi, : P_LANES - KD] = p_ref[chip, lo:hi, KD:]
    else:
        slots[4 * chip + 1, lo:hi, :] = padded(q_ref[chip, lo:hi, :KD])
        slots[4 * chip + 3, lo:hi, :] = padded(q_ref[chip, lo:hi, KD : 2 * KD])
        slots[4 * chip + 2, lo:hi, P_LANES - KD :] = padded(q_ref[chip, lo:hi, 2 * KD :])


def sort_keys(first, slots, keys):
    def step(p, carry):
        slot = first[p]
        low, high = p, HALVES - 1 - p
        keys[low // 16, pl.ds(pl.multiple_of(low % 16 * HALF, HALF), HALF), :] = slots[slot]
        keys[high // 16, pl.ds(pl.multiple_of(high % 16 * HALF, HALF), HALF), :] = slots[slot + 1]
        return carry

    lax.fori_loop(0, HALVES // 2, step, 0, unroll=4)


def sort_index_keys(first, idxg, slots32, sorted32, idx_keys):
    slots32[...] = idxg[...].astype(F32).reshape(HALVES, 8, IDX_DIM)

    def step(p, carry):
        slot = first[p]
        sorted32[p] = slots32[slot]
        sorted32[HALVES - 1 - p] = slots32[slot + 1]
        return carry

    lax.fori_loop(0, HALVES // 2, step, 0, unroll=4)
    idx_keys[...] = sorted32[...].reshape(8, 128, IDX_DIM).astype(BF16)


def split_heads(pair, vmq, queries):
    pad = jnp.zeros((HALF, KPAD - KD), BF16)
    for half in range(2):
        for h in range(HEADS_DEV):
            queries[2 * pair + half, h * HALF : (h + 1) * HALF, :] = jnp.concatenate(
                [vmq[pair, half * HALF : (half + 1) * HALF, h * KD : (h + 1) * KD], pad], axis=1
            )


LANES = HEADS_DEV * HALF
EXP_SCALE = SCORE_SCALE * LOG2E


def score_step(table, pair, i, keys, queries, scores, tops):
    early, g, block, limit = entry(table, pair, i)
    early = mask_of(early, (8, LANES))
    k = keys[block]
    s = lax.dot_general(k, queries[g], (((1,), (1,)), ((), ())), preferred_element_type=F32)
    row = lax.broadcasted_iota(jnp.int32, (512, LANES), 0)
    token = lax.broadcasted_iota(jnp.int32, (512, LANES), 1) % HALF
    s = jnp.where(row - token <= limit, s, NEG)
    scores[i] = s
    m = jnp.max(s.reshape(64, 8, LANES), axis=0)
    return (
        jnp.where(early, jnp.maximum(tops[0], m), tops[0]),
        jnp.where(early, tops[1], jnp.maximum(tops[1], m)),
    )


def exp_step(table, pair, i, scores, shifts, sums):
    early = entry(table, pair, i)[0]
    row = mask_of(early, (1, LANES))
    early = mask_of(early, (8, LANES))
    e = jnp.exp2(scores[i] * EXP_SCALE - jnp.where(row, shifts[0], shifts[1]))
    scores[i] = e
    m = jnp.sum(e.reshape(64, 8, LANES), axis=0)
    return (sums[0] + jnp.where(early, m, 0.0), sums[1] + jnp.where(early, 0.0, m))


def head_step(table, pair, i, scores, weights, tgt_ref):
    early = mask_of(entry(table, pair, i)[0], (1, LANES))
    group_of = lax.broadcasted_iota(jnp.int32, (8, 128), 1) // HALF
    weight = jnp.broadcast_to(jnp.where(early, weights[0], weights[1]), (8, LANES))
    low, even = group_of < 2, group_of % 2 == 0

    def heads(first):
        tiles = [slice(lt * 128, (lt + 1) * 128) for lt in range(LANES // 128)]
        terms = [scores[i, first : first + 8, cut] * weight[:, cut] for cut in tiles]
        return (terms[0] + terms[1]) + (terms[2] + terms[3])

    for part in range(4):
        for y in range(NY):
            v = [heads(part * 128 + 32 * a + 8 * y) for a in range(4)]
            t02 = jnp.where(low, v[0], v[2]) + pltpu.roll(jnp.where(low, v[2], v[0]), 64, 1)
            t13 = jnp.where(low, v[1], v[3]) + pltpu.roll(jnp.where(low, v[3], v[1]), 64, 1)
            swap = jnp.where(even, t13, t02)
            swap = jnp.where(even, pltpu.roll(swap, 96, 1), pltpu.roll(swap, 32, 1))
            tgt_ref[y, pair, 4 * i + part] = jnp.where(even, t02, t13) + swap


def start_tops():
    return (jnp.full((8, LANES), NEG, F32),) * 2


def start_sums():
    return (jnp.zeros((8, LANES), F32),) * 2


def shifts_of(tops):
    return tuple(jnp.max(t, axis=0, keepdims=True) * EXP_SCALE for t in tops)


def weights_of(sums):
    return tuple(1.0 / (HEADS * jnp.sum(t, axis=0, keepdims=True)) for t in sums)


def targets(table, pair, keys, queries, scores, tgt_ref, send):
    tops = lax.fori_loop(0, 9, lambda i, t: score_step(table, pair, i, keys, queries, scores, t), start_tops(), unroll=3)
    shifts = shifts_of(tops)
    sums = lax.fori_loop(0, 9, lambda i, t: exp_step(table, pair, i, scores, shifts, t), start_sums())
    weights = weights_of(sums)

    def last(i, carry):
        head_step(table, pair, i, scores, weights, tgt_ref)
        return carry

    for first in range(0, ENTRIES, 3):
        lax.fori_loop(first, first + 3, last, 0)
        send(pair, first)


def split_index_heads(pair, vidx, idx_q):
    for half in range(2):
        for j in range(IDX_HEADS):
            at = (j % 16 * 4 + j // 16) * HALF
            idx_q[2 * pair + half, at : at + HALF, :] = vidx[
                pair, half * HALF : (half + 1) * HALF, j * IDX_DIM : (j + 1) * IDX_DIM
            ]


def weight_rows(hw):
    turned = jnp.concatenate([hw, hw], axis=0).T
    return [
        [
            jnp.concatenate(
                [
                    turned[q * IDX_HEADS + a * 16 : q * IDX_HEADS + a * 16 + 16, half * HALF : (half + 1) * HALF]
                    for a in range(4)
                ],
                axis=1,
            )
            for half in range(2)
        ]
        for q in range(2)
    ]


def weight_cut(w_ref, g, ch):
    return jnp.concatenate([w_ref[g, 2 * ch : 2 * ch + 1, :], w_ref[g, 2 * ch + 1 : 2 * ch + 2, :]], axis=1)


def logit_step(table, pair, i, y, idx_keys, idx_q, w_ref, inner_ref, logit_ref, tops):
    early, g, block, limit = entry(table, pair, i)
    early = mask_of(early, (8, 128))
    k = idx_keys[block]
    acc = jnp.zeros((128, 128), F32)
    for ch in range(8):
        cut = slice(ch * 256, (ch + 1) * 256)
        inner = lax.dot_general(k, idx_q[g, cut, :], (((1,), (1,)), ((), ())), preferred_element_type=F32)
        inner_ref[pair, i, :, cut] = inner.astype(BF16)
        part = jnp.maximum(inner, 0.0) * weight_cut(w_ref, g, ch)
        acc = acc + part[:, :128] + part[:, 128:]
    acc = acc + pltpu.roll(acc, 64, 1)
    acc = acc + pltpu.roll(acc, 32, 1)
    row = lax.broadcasted_iota(jnp.int32, (128, 128), 0)
    token = lax.broadcasted_iota(jnp.int32, (128, 128), 1) % HALF
    offset = row // 8 * HALF + row % 8 - token
    acc = jnp.where(offset <= limit - 8 * y, acc * INDEX_NORM, NEG)
    logit_ref[pair, i] = acc
    m = jnp.max(acc.reshape(16, 8, 128), axis=0)
    return (
        jnp.where(early, jnp.maximum(tops[0], m), tops[0]),
        jnp.where(early, tops[1], jnp.maximum(tops[1], m)),
    )


def logit_stats(table, pair, logit_ref, stat_ref, tops):
    tops = [jnp.max(t, axis=0, keepdims=True) for t in tops]

    def step(i, sums):
        early = entry(table, pair, i)[0]
        row = mask_of(early, (1, 128))
        early = mask_of(early, (8, 128))
        e = jnp.exp(logit_ref[pair, i] - jnp.where(row, tops[0], tops[1]))
        e = jnp.sum(e.reshape(16, 8, 128), axis=0)
        return (sums[0] + jnp.where(early, e, 0.0), sums[1] + jnp.where(early, 0.0, e))

    sums = lax.fori_loop(0, 9, step, (jnp.zeros((8, 128), F32),) * 2, unroll=3)
    for half in range(2):
        g = 2 * pair + half
        stat_ref[g : g + 1, :] = tops[half]
        stat_ref[4 + g : 5 + g, :] = jnp.sum(sums[half], axis=0, keepdims=True)


def norms_of(stats_ref, g):
    tops = [stats_ref[d, g : g + 1, :] for d in range(NY)]
    top = jnp.maximum(jnp.maximum(tops[0], tops[1]), jnp.maximum(tops[2], tops[3]))
    norm = sum(stats_ref[d, 4 + g : 5 + g, :] * jnp.exp(tops[d] - top) for d in range(NY))
    return top, GRAD_COEF / norm


def gradient_step(table, pair, i, y, idx_q, w_ref, inner_ref, logit_ref, tgt_ref, arrive, norms, grad_ref):
    early, g, block, limit = entry(table, pair, i)
    early = mask_of(early, (1, 128))
    group_of = lax.broadcasted_iota(jnp.int32, (8, 128), 1) // HALF
    wide = []
    for part in range(4):
        at = 4 * i + part
        packed = tgt_ref[y, pair, at] + arrive[0, pair, at] + arrive[1, pair, at] + arrive[2, pair, at]
        for a in range(4):
            v = jnp.where(group_of == a, packed, 0.0)
            v = v + pltpu.roll(v, 64, 1)
            wide.append(v + pltpu.roll(v, 32, 1))
    target = jnp.concatenate(wide, axis=0)
    top = jnp.where(early, norms[0][0], norms[1][0])
    coef = jnp.where(early, norms[0][1], norms[1][1])
    row = lax.broadcasted_iota(jnp.int32, (128, 128), 0)
    token = lax.broadcasted_iota(jnp.int32, (128, 128), 1) % HALF
    offset = row // 8 * HALF + row % 8 - token
    seen = offset <= limit - 8 * y
    scaled = jnp.where(seen, jnp.exp(logit_ref[pair, i] - top) * coef - GRAD_COEF * target, 0.0)
    scaled = jnp.concatenate([scaled, scaled], axis=1)
    acc = jnp.zeros((128, IDX_DIM), F32)
    zero = jnp.zeros((), BF16)
    for ch in range(8):
        cut = slice(ch * 256, (ch + 1) * 256)
        signal = (scaled * weight_cut(w_ref, g, ch)).astype(BF16)
        signal = jnp.where(inner_ref[pair, i, :, cut] > zero, signal, zero)
        acc = acc + jnp.dot(signal, idx_q[g, cut, :], preferred_element_type=F32)
    grad_ref[pair, i] = acc


def collect_gradients(table, order, grad_ref, sorted_ref, part_ref):
    total = [grad_ref[0, 0] + grad_ref[1, 0] + grad_ref[0, 1] + grad_ref[1, 1]]
    total += [grad_ref[0, b + 1] + grad_ref[1, b + 1] for b in range(1, 5)] + [0.0] * 3
    for pair in range(2):
        for k in range(1, 4):
            flip = mask_of(entry(table, pair, k + 5)[0], (128, IDX_DIM))
            d = grad_ref[pair, k + 5]
            total[k] = total[k] + jnp.where(flip, d, 0.0)
            total[8 - k] = total[8 - k] + jnp.where(flip, 0.0, d)
    for b in range(8):
        sorted_ref[b * 16 : (b + 1) * 16] = total[b].reshape(16, 8, IDX_DIM)

    def store(chip, carry):
        for core in range(2):
            for half in range(2):
                place = order[4 * chip + 2 * core + half]
                rows = sorted_ref[place]
                part_ref[chip // NZ, chip % NZ, core * 16 + half * 8 : core * 16 + half * 8 + 8, :] = rows
        return carry

    lax.fori_loop(0, NX * NZ, store, 0, unroll=2)


X_ROWS = 24
PIECES = [(core, half) for core in range(2) for half in range(2)]


def along_x(core, half):
    return (core, half) != (1, 1)


def final_targets(x, z, y):
    return [
        (
            core, half, d,
            (seq_at(x, (z + d) % NZ, core) if along_x(core, half) else seq_at((x + d) % NX, z, core), y // 2 + 2 * half),
        )
        for core, half in PIECES
        for d in range(NZ if along_x(core, half) else NX)
    ]


def final_sources(x, z, y, summed_x):
    return [
        (
            d, 2 * odd + core,
            (seq_at(x, (z - d + NZ) % NZ, core) if summed_x else seq_at((x - d + NX) % NX, z, core), 2 * (y % 2) + odd),
            core,
        )
        for d in range(NZ if summed_x else NX)
        for odd in range(2)
        for core in range(2)
    ]


def scatter(
    x, z, c, y, peers_x, peers_z, remote, part_ref, out_ref, xa, za, slab_x, slab_z, final,
    xa_sem, za_sem, final_send, final_recv,
):
    first_x = [
        remote(
            part_ref.at[(x + d) % NX, :, pl.ds(0, X_ROWS)], xa.at[d - 1], xa_sem.at[0, d - 1], xa_sem.at[1, d - 1],
            peers_x[d - 1],
        )
        for d in range(1, NX)
    ]
    first_z = [
        remote(
            part_ref.at[:, (z + d) % NZ, pl.ds(X_ROWS, 32 - X_ROWS)], za.at[d - 1], za_sem.at[0, d - 1],
            za_sem.at[1, d - 1], peers_z[d - 1],
        )
        for d in range(1, NZ)
    ]
    slot = 2 * (y % 2) + c
    ends = final_targets(x, z, y)

    def piece(k):
        core, half, d, _ = ends[k]
        if along_x(core, half):
            return slab_x.at[(z + d) % NZ, pl.ds(16 * core + 8 * half, 8)]
        return slab_z.at[(x + d) % NX]

    def last_copy(k):
        d, to = ends[k][2:]
        return pltpu.make_async_remote_copy(
            src_ref=piece(k), dst_ref=final.at[d, slot], send_sem=final_send.at[k],
            recv_sem=final_recv.at[d, slot], device_id=to, device_id_type=MESH,
        )

    def here(k):
        core, half, _, _ = ends[k]
        return jnp.logical_and(c == core, y // 2 + 2 * half == y)

    def send_last(summed_x):
        for k, (core, half, d, _) in enumerate(ends):
            if along_x(core, half) != summed_x:
                continue
            if d > 0:
                last_copy(k).start()
                continue

            @pl.when(jnp.logical_not(here(k)))
            def _(k=k):
                last_copy(k).start()

            @pl.when(here(k))
            def _(k=k):
                final[0, slot] = piece(k)[...]

    for d in first_x:
        d.wait_recv()
    slab_x[...] = part_ref[x, :, 0:X_ROWS, :] + xa[0] + xa[1] + xa[2]
    send_last(True)
    for d in first_z:
        d.wait_recv()
    total = part_ref[:, z, X_ROWS:32, :]
    for k in range(NZ - 1):
        total = total + za[k]
    slab_z[...] = total
    send_last(False)
    for summed_x in (True, False):

        @pl.when(by_x(c, y) if summed_x else jnp.logical_not(by_x(c, y)))
        def _(summed_x=summed_x):
            for d, at, source, core in final_sources(x, z, y, summed_x):
                ref = final.at[d, at]
                arrival = pltpu.make_async_remote_copy(
                    src_ref=ref, dst_ref=ref, send_sem=final_send.at[0], recv_sem=final_recv.at[d, at],
                    device_id=source, device_id_type=MESH,
                )
                if d == 0:
                    pl.when(jnp.logical_or(core != c, source[1] != y))(arrival.wait_recv)
                else:
                    arrival.wait_recv()
            for at in range(4):
                total = final[0, at]
                for d in range(1, NZ if summed_x else NX):
                    total = total + final[d, at]
                out_ref[at // 2 * 8 : at // 2 * 8 + 8, at % 2 * IDX_DIM : (at % 2 + 1) * IDX_DIM] = total

    for k, (core, half, d, _) in enumerate(ends):
        if d > 0:
            last_copy(k).wait_send()
        else:
            pl.when(jnp.logical_not(here(k)))(last_copy(k).wait_send)
    for d in first_x + first_z:
        d.wait_send()


def by_x(c, y):
    return jnp.logical_or(c == 0, y < 2)


def whole_kernel(
    order, first, lat_any, idx_any, hw_any, mq_any, iq_any, out_ref,
    table, lat_ref, idx_ref, hw_ref, w_other, p_ref, q_ref, slots, stage_out, stage_in, idx32, idx_stage_out, idx_stage_in, idxg, slots32, sorted32, idx_keys,
    vmq, queries, keys, scores, tgt_ref, vidx, idx_q, w_ref, inner_ref, logit_ref, stat_ref, stats_ref, arrive,
    grad_ref, part_ref, xa, za, slab_x, slab_z, final,
    load_sem, pair_send, pair_recv, ring_send, ring_recv, idx_z_sem, idx_x_sem,
    tgt_send, tgt_recv, stat_send, stat_recv, xa_sem, za_sem, final_send, final_recv,
):
    x, z, c, y = coords()
    seq = lax.axis_index("seq")
    me = x * NZ + z
    barrier = pltpu.get_barrier_semaphore()
    partner = (seq_at(x, z, 1 - c), y)
    peers_y = [(seq, (y + d) % NY) for d in range(1, NY)]
    peers_x = [(seq_at((x + d) % NX, z, c), y) for d in range(1, NX)]
    peers_z = [(seq_at(x, (z + d) % NZ, c), y) for d in range(1, NZ)]
    ring = {("x", 1): peers_x[0], ("x", -1): peers_x[-1], ("z", 1): peers_z[0], ("z", -1): peers_z[-1]}

    def tell(to):
        pl.semaphore_signal(barrier, inc=1, device_id=to, device_id_type=MESH)

    for to in peers_x + peers_z + peers_y + [partner]:
        tell(to)
    loads = [
        pltpu.make_async_copy(src, dst, load_sem.at[k])
        for k, (src, dst) in enumerate(
            [
                (lat_any, lat_ref), (idx_any, idx_ref), (hw_any, hw_ref), (iq_any.at[c], vidx.at[0]),
                (mq_any.at[c], vmq.at[0]),
            ]
        )
    ]
    for d in loads:
        d.start()
    for summed_x in (True, False):

        @pl.when(by_x(c, y) if summed_x else jnp.logical_not(by_x(c, y)))
        def _(summed_x=summed_x):
            for d, _, source, core in final_sources(x, z, y, summed_x):
                if d == 0:
                    pl.when(jnp.logical_or(core != c, source[1] != y))(functools.partial(tell, source))
                else:
                    tell(source)

    fill_table(order, seq, table)
    for d in loads[:3]:
        d.wait()
    weights = weight_rows(hw_ref[...])
    for half in range(2):
        w_other[half] = jnp.where(c == 0, weights[1][half], weights[0][half])
        w_ref[half] = jnp.where(c == 0, weights[0][half], weights[1][half])
    lat = lat_ref[...]
    stage_out[:, 0:KD] = jnp.where(c == 0, lat[:, KD:], lat[:, :KD])
    stage_out[:, KD:] = jnp.zeros((TOK, KPAD - KD), BF16)
    idx32[...] = idx_ref[...].astype(F32)
    rows = jnp.concatenate(
        [idx32[pl.ds(pl.multiple_of(y * 8, 8), 8), :], idx32[pl.ds(pl.multiple_of(HALF + y * 8, 8), 8), :]], axis=0
    )
    idx_stage_out[...] = jnp.where(c == 0, rows[:, IDX_DIM:], rows[:, :IDX_DIM]).astype(BF16)
    own = jnp.where(jnp.logical_or(y == 0, y == NY - 1), 1, 0)
    pl.semaphore_wait(barrier, NX - 1 + NZ - 1 + NY - 1 + 1 + 3 * NZ + NX - own)

    def remote(src, dst, send, recv, to):
        d = pltpu.make_async_remote_copy(
            src_ref=src, dst_ref=dst, send_sem=send, recv_sem=recv, device_id=to, device_id_type=MESH
        )
        d.start()
        return d

    def to_partner(k, src, dst):
        return remote(src, dst, pair_send.at[k], pair_recv.at[k], partner)

    pair_copies = [
        to_partner(0, stage_out, stage_in),
        to_partner(1, idx_stage_out, idx_stage_in),
        to_partner(2, iq_any.at[1 - c], vidx.at[1]),
        to_partner(3, mq_any.at[1 - c], vmq.at[1]),
        to_partner(4, w_other, w_ref.at[pl.ds(2, 2)]),
    ]
    mine = jnp.where(c == 0, lat[:, :KD], lat[:, KD:])
    idx_mine = jnp.where(c == 0, rows[:, :IDX_DIM], rows[:, IDX_DIM:]).astype(BF16)
    pair_copies[0].wait_recv()
    pair_copies[1].wait_recv()
    from_partner = stage_in[:, :KD]
    both = jnp.concatenate([jnp.where(c == 0, mine, from_partner), jnp.where(c == 0, from_partner, mine)], axis=1)
    p_ref[me] = both[:HALF, :P_LANES]
    q_ref[me] = jnp.concatenate([both[HALF:], both[:HALF, P_LANES:]], axis=1)
    idx_other = idx_stage_in[...]
    idxg[x, z, 0:16] = jnp.where(c == 0, idx_mine, idx_other)
    idxg[x, z, 16:32] = jnp.where(c == 0, idx_other, idx_mine)

    counter = [0]
    live, origin = {}, {}
    landed = [(0, me, 0, HALF), (1, me, 0, HALF)]

    def send(part, axis, way, dx, dz, lo, hi):
        k = counter[0]
        counter[0] += 1

        def block(ox, oz):
            ref = q_ref if part else p_ref
            return ref.at[(x + ox + 2 * NX) % NX * NZ + (z + oz + 2 * NZ) % NZ, pl.ds(lo, hi - lo)]

        out = remote(block(dx, dz), block(dx, dz), ring_send.at[k], ring_recv.at[k], ring[(axis, way)])
        here = block(dx - way, dz) if axis == "x" else block(dx, dz - way)
        arrival = pltpu.make_async_remote_copy(
            src_ref=here, dst_ref=here, send_sem=ring_send.at[k], recv_sem=ring_recv.at[k],
            device_id=ring[(axis, way)], device_id_type=MESH,
        )
        live[k] = [out, arrival, False]
        ix, iz = (dx - way, dz) if axis == "x" else (dx, dz - way)
        origin[k] = (part, (x + ix + 2 * NX) % NX * NZ + (z + iz + 2 * NZ) % NZ, lo, hi)
        return k

    def arrived(k):
        if not live[k][2]:
            live[k][1].wait_recv()
            live[k][2] = True
            landed.append(origin[k])

    gone = set()

    def left(ks):
        for k in ks:
            if k not in gone:
                live[k][0].wait_send()
                gone.add(k)

    last_x, last_z = NX // 2, NZ // 2

    def hop(part, axis, dx, dz, step, before):
        last = last_x if axis == "x" else last_z
        ks = []
        for way, half in ((1, (0, 16)), (-1, (16, 32))):
            if before is not None:
                arrived(before[0 if way == 1 else 1])
            away = -way * (step - 1)
            ox, oz = (away, dz) if axis == "x" else (dx, away)
            lo, hi = half if step == last else (0, 32)
            ks.append(send(part, axis, way, ox, oz, lo, hi))
        return ks

    zp, xq, zq = {}, {}, {}

    def start_p(dx):
        zp[dx] = {1: hop(0, "z", dx, 0, 1, None)}

    def advance_p(dx, step):
        zp[dx][step] = hop(0, "z", dx, 0, step, zp[dx][step - 1])

    def advance_q(step):
        before = zq[step - 1]
        if step <= last_z:
            zq[step] = hop(1, "z", 0, 0, step, before)
        else:
            arrived(before[0])
            arrived(before[1])
        for dz in (-(step - 1), step - 1) if step <= last_z else (last_z,):
            xq[dz] = {1: hop(1, "x", 0, dz, 1, None)}

    def finish_q(dz):
        xq[dz][2] = hop(1, "x", 0, dz, 2, xq[dz][1])

    idx_z = []

    def start_index():
        for d in range(1, NZ):
            ref = idxg.at[x, z]
            idx_z.append(remote(ref, ref, idx_z_sem.at[0, d - 1], idx_z_sem.at[1, d - 1], peers_z[d - 1]))

    idx_x = []

    def spread_index():
        for d in range(1, NZ):
            ref = idxg.at[x, (z - d + NZ) % NZ]
            pltpu.make_async_remote_copy(
                src_ref=ref, dst_ref=ref, send_sem=idx_z_sem.at[0, d - 1], recv_sem=idx_z_sem.at[1, d - 1],
                device_id=peers_z[d - 1], device_id_type=MESH,
            ).wait_recv()
        for d in range(1, NX):
            idx_x.append(
                remote(idxg.at[x], idxg.at[x], idx_x_sem.at[0, d - 1], idx_x_sem.at[1, d - 1], peers_x[d - 1])
            )

    def have_index():
        for d in range(1, NX):
            ref = idxg.at[(x - d + NX) % NX]
            pltpu.make_async_remote_copy(
                src_ref=ref, dst_ref=ref, send_sem=idx_x_sem.at[0, d - 1], recv_sem=idx_x_sem.at[1, d - 1],
                device_id=peers_x[d - 1], device_id_type=MESH,
            ).wait_recv()
        sort_index_keys(first, idxg, slots32, sorted32, idx_keys)

    logit_tops = [(jnp.full((8, 128), NEG, F32),) * 2 for _ in range(2)]
    stat_copies = []

    def logits(pair, first, last):
        logit_tops[pair] = lax.fori_loop(
            first, last,
            lambda i, t: logit_step(table, pair, i, y, idx_keys, idx_q, w_ref, inner_ref, logit_ref, t),
            logit_tops[pair],
        )
        if last == ENTRIES:
            logit_stats(table, pair, logit_ref, stat_ref, logit_tops[pair])

    def send_stats():
        for d in range(1, NY):
            stat_copies.append(
                remote(stat_ref, stats_ref.at[d], stat_send.at[d - 1], stat_recv.at[d - 1], peers_y[d - 1])
            )
        stats_ref[0] = stat_ref[...]

    def own_queries():
        loads[4].wait()
        split_heads(0, vmq, queries)

    def own_index_queries():
        loads[3].wait()
        pair_copies[4].wait_recv()
        split_index_heads(0, vidx, idx_q)

    def other_index_queries():
        pair_copies[2].wait_recv()
        split_index_heads(1, vidx, idx_q)

    def other_queries():
        pair_copies[3].wait_recv()
        split_heads(1, vmq, queries)

    work = [own_index_queries, spread_index, own_queries, have_index]
    work += [functools.partial(logits, 0, k, k + 3) for k in (0, 3, 6)]
    work += [other_index_queries]
    work += [functools.partial(logits, 1, k, k + 3) for k in (0, 3, 6)]
    work += [send_stats, other_queries]

    def between():
        if work:
            work.pop(0)()
        for _ in range(min(4, len(landed))):
            split_cores(p_ref, q_ref, slots, *landed.pop(0))

    zq[1] = hop(1, "z", 0, 0, 1, None)
    xp = hop(0, "x", 0, 0, 1, None)
    left(zq[1])
    start_p(0)
    left(xp)
    xq[0] = {1: hop(1, "x", 0, 0, 1, None)}
    start_index()
    between()
    advance_q(2)
    xp2 = hop(0, "x", 0, 0, 2, xp)
    start_p(-1)
    start_p(1)
    between()
    advance_p(0, 2)
    finish_q(0)
    advance_q(3)
    arrived(xp2[0])
    arrived(xp2[1])
    start_p(2)
    between()
    advance_p(-1, 2)
    advance_p(1, 2)
    between()
    advance_p(0, 3)
    advance_q(4)
    finish_q(-1)
    finish_q(1)
    between()
    advance_p(2, 2)
    between()
    advance_p(-1, 3)
    advance_p(1, 3)
    advance_q(5)
    between()
    finish_q(-2)
    finish_q(2)
    advance_p(0, 4)
    between()
    advance_p(2, 3)
    between()
    advance_p(-1, 4)
    advance_p(1, 4)
    finish_q(-3)
    finish_q(3)
    between()
    advance_p(2, 4)
    finish_q(last_z)
    while work:
        between()
    for k in live:
        arrived(k)
        while landed:
            split_cores(p_ref, q_ref, slots, *landed.pop(0))
    sort_keys(first, slots, keys)

    tgt_copies = {}

    def send_targets(pair, at):
        cut = pl.ds(4 * at, 12)
        tgt_copies[pair, at] = [
            remote(
                tgt_ref.at[(y + d) % NY, pair, cut], arrive.at[d - 1, pair, cut], tgt_send.at[pair, at // 3, d - 1],
                tgt_recv.at[pair, at // 3, d - 1], peers_y[d - 1],
            )
            for d in range(1, NY)
        ]

    for pair in range(2):
        targets(table, pair, keys, queries, scores, tgt_ref, send_targets)
    for d in stat_copies:
        d.wait_recv()
    for pair in range(2):
        norms = [norms_of(stats_ref, 2 * pair + half) for half in range(2)]

        def step(i, carry):
            gradient_step(
                table, pair, i, y, idx_q, w_ref, inner_ref, logit_ref, tgt_ref, arrive, norms, grad_ref
            )
            return carry

        for at in range(0, ENTRIES, 3):
            for d in tgt_copies[pair, at]:
                d.wait_recv()
            lax.fori_loop(at, at + 3, step, 0)
    collect_gradients(table, order, grad_ref, sorted32, part_ref)
    scatter(
        x, z, c, y, peers_x, peers_z, remote, part_ref, out_ref, xa, za, slab_x, slab_z, final,
        xa_sem, za_sem, final_send, final_recv,
    )
    left(live)
    for d in pair_copies + idx_z + idx_x + stat_copies + sum(tgt_copies.values(), []):
        d.wait_send()


RING_COPIES = 76


def whole_call(order, first, lat, idx, hw, mq, iq):
    any_spec = pl.BlockSpec(memory_space=pl.ANY)
    vmem = pl.BlockSpec(memory_space=pltpu.VMEM)
    smem = pl.BlockSpec(memory_space=pltpu.SMEM)
    dma = pltpu.SemaphoreType.DMA
    return pl.pallas_call(
        whole_kernel,
        name="indexer_key_gradient",
        out_shape=jax.ShapeDtypeStruct((16, 2 * IDX_DIM), F32),
        in_specs=[smem] * 2 + [any_spec] * 5,
        out_specs=vmem,
        scratch_shapes=[
            pltpu.SMEM((8 * ENTRIES,), jnp.int32),
            pltpu.VMEM((TOK, 2 * KD), BF16),
            pltpu.VMEM((TOK, 2 * IDX_DIM), BF16),
            pltpu.VMEM((TOK, 2 * IDX_HEADS), F32),
            pltpu.VMEM((2, 16, 128), F32),
            pltpu.VMEM((NX * NZ, HALF, P_LANES), BF16),
            pltpu.VMEM((NX * NZ, HALF, Q_LANES), BF16),
            pltpu.VMEM((HALVES, HALF, KPAD), BF16),
            pltpu.VMEM((TOK, KPAD), BF16),
            pltpu.VMEM((TOK, KPAD), BF16),
            pltpu.VMEM((TOK, 2 * IDX_DIM), F32),
            pltpu.VMEM((16, IDX_DIM), BF16),
            pltpu.VMEM((16, IDX_DIM), BF16),
            pltpu.VMEM((NX, NZ, 32, IDX_DIM), BF16),
            pltpu.VMEM((HALVES, 8, IDX_DIM), F32),
            pltpu.VMEM((HALVES, 8, IDX_DIM), F32),
            pltpu.VMEM((8, 128, IDX_DIM), BF16),
            pltpu.VMEM((2, TOK, HEADS_DEV * KD), BF16),
            pltpu.VMEM((4, LANES, KPAD), BF16),
            pltpu.VMEM((8, 512, KPAD), BF16),
            pltpu.VMEM((ENTRIES, 512, LANES), F32),
            pltpu.VMEM((NY, 2, SLOTS, 8, 128), F32),
            pltpu.VMEM((2, TOK, IDX_HEADS * IDX_DIM), BF16),
            pltpu.VMEM((4, IDX_HEADS * HALF, IDX_DIM), BF16),
            pltpu.VMEM((4, 16, 128), F32),
            pltpu.VMEM((2, ENTRIES, 128, IDX_HEADS * HALF), BF16),
            pltpu.VMEM((2, ENTRIES, 128, 128), F32),
            pltpu.VMEM((8, 128), F32),
            pltpu.VMEM((NY, 8, 128), F32),
            pltpu.VMEM((NY - 1, 2, SLOTS, 8, 128), F32),
            pltpu.VMEM((2, ENTRIES, 128, IDX_DIM), F32),
            pltpu.VMEM((NX, NZ, 32, IDX_DIM), F32),
            pltpu.VMEM((NX - 1, NZ, X_ROWS, IDX_DIM), F32),
            pltpu.VMEM((NZ - 1, NX, 32 - X_ROWS, IDX_DIM), F32),
            pltpu.VMEM((NZ, X_ROWS, IDX_DIM), F32),
            pltpu.VMEM((NX, 32 - X_ROWS, IDX_DIM), F32),
            pltpu.VMEM((NZ, 4, 8, IDX_DIM), F32),
            dma((5,)),
            dma((5,)),
            dma((5,)),
            dma((RING_COPIES,)),
            dma((RING_COPIES,)),
            dma((2, NZ - 1)),
            dma((2, NX - 1)),
            dma((2, 3, NY - 1)),
            dma((2, 3, NY - 1)),
            dma((NY - 1,)),
            dma((NY - 1,)),
            dma((2, NX - 1)),
            dma((2, NZ - 1)),
            dma((3 * NZ + NX,)),
            dma((NZ, 4)),
        ],
        compiler_params=pltpu.CompilerParams(
            collective_id=0, has_side_effects=True, vmem_limit_bytes=VMEM_BYTES
        ),
    )(order, first, lat, idx, hw, mq, iq)


def per_device(mla_queries, latent_keys, index_queries, index_keys, head_weights, block_order):
    places = jnp.arange(HALVES // 2, dtype=jnp.int32)[:, None]
    slots = jnp.arange(HALVES, dtype=jnp.int32)[None, :]
    first = jnp.sum(jnp.where(block_order[None, :] == places, slots, 0), axis=1)
    return whole_call(block_order, first, latent_keys, index_keys, head_weights, mla_queries, index_queries)


def solution(mesh):
    return jax.shard_map(
        per_device,
        mesh=mesh,
        in_specs=(
            P(None, "seq", "head"),
            P("seq", None),
            P(None, "seq", None),
            P("seq", None),
            P("seq", None),
            P(),
        ),
        out_specs=P(("seq", "head"), None),
        check_vma=False,
    )
```

```python
import functools

import jax
import jax.numpy as jnp
from jax import lax
from jax.experimental import pallas as pl
from jax.experimental.pallas import tpu as pltpu
from jax.sharding import PartitionSpec as P

MESH = pl.DeviceIdType.MESH
NX, NZ, NY = 4, 8, 4
HEADS = 64
HEADS_DEV = 16
KD = 576
KPAD = 640
IDX_HEADS = 64
IDX_DIM = 128
TOK = 64
HALF = 32
HALVES = 128
SLOTS = 36
SCORE_SCALE = 192.0 ** (-0.5)
LOG2E = 1.4426950408889634
INDEX_NORM = (IDX_HEADS * IDX_DIM) ** (-0.5)
GRAD_COEF = 1024.0 * INDEX_NORM
NEG = -1e30
VMEM_BYTES = 60 * 1024 * 1024
F32 = jnp.float32
BF16 = jnp.bfloat16


def coords():
    s = lax.axis_index("seq")
    y = lax.axis_index("head")
    return s // (2 * NZ), (s // 2) % NZ, s % 2, y


def seq_at(x, z, c):
    return (x * NZ + z) * 2 + c


ENTRIES = 9


def fill_table(order, seq, table):
    for pair in range(2):
        device = seq if pair == 0 else seq + 1 - 2 * (seq % 2)
        early_place, late_place = order[2 * device], order[2 * device + 1]
        for i in range(ENTRIES):
            k = i - 5
            flip = jnp.where(early_place // 16 >= k, 1, 0)
            early = 1 if i == 0 else 0 if i < 6 else flip
            block = 0 if i == 0 else i - 1 if i < 6 else flip * k + (1 - flip) * (8 - k)
            place = early * early_place + (1 - early) * late_place
            fields = (early, 2 * pair + 1 - early, block, place * HALF - block * 512)
            for field, value in enumerate(fields):
                table[(field * 2 + pair) * ENTRIES + i] = jnp.int32(value)


def slots_of(row):
    slot = lax.broadcasted_iota(jnp.int32, (HALVES, HALVES), 0)
    lane = lax.broadcasted_iota(jnp.int32, (HALVES, HALVES), 1)
    column = jnp.sum(jnp.where(slot == lane, row, 0), axis=1, keepdims=True)
    return jnp.max(jnp.where(column == lane, slot - slot % 2, 0), axis=0, keepdims=True)


def entry(table, pair, i):
    return [table[(field * 2 + pair) * ENTRIES + i] for field in range(4)]


def mask_of(flag, shape):
    return jnp.zeros(shape, jnp.int32) + flag > 0


P_LANES = 7 * 128
Q_LANES = 4 * KD - P_LANES


def split_cores(p_ref, q_ref, slots, part, chip, lo, hi):
    pad = jnp.zeros((hi - lo, KPAD - KD), BF16)

    def padded(rows):
        return jnp.concatenate([rows, pad], axis=1)

    if part == 0:
        slots[4 * chip, lo:hi, :] = padded(p_ref[chip, lo:hi, :KD])
        slots[4 * chip + 2, lo:hi, : P_LANES - KD] = p_ref[chip, lo:hi, KD:]
    else:
        slots[4 * chip + 1, lo:hi, :] = padded(q_ref[chip, lo:hi, :KD])
        slots[4 * chip + 3, lo:hi, :] = padded(q_ref[chip, lo:hi, KD : 2 * KD])
        slots[4 * chip + 2, lo:hi, P_LANES - KD :] = padded(q_ref[chip, lo:hi, 2 * KD :])


def sort_keys(first, slots, keys):
    def step(p, carry):
        slot = first[0, p]
        low, high = p, HALVES - 1 - p
        keys[low // 16, pl.ds(pl.multiple_of(low % 16 * HALF, HALF), HALF), :] = slots[slot]
        keys[high // 16, pl.ds(pl.multiple_of(high % 16 * HALF, HALF), HALF), :] = slots[slot + 1]
        return carry

    lax.fori_loop(0, HALVES // 2, step, 0, unroll=4)


def sort_index_keys(first, idxg, slots32, sorted32, idx_keys):
    slots32[...] = idxg[...].astype(F32).reshape(HALVES, 8, IDX_DIM)

    def step(p, carry):
        slot = first[0, p]
        sorted32[p] = slots32[slot]
        sorted32[HALVES - 1 - p] = slots32[slot + 1]
        return carry

    lax.fori_loop(0, HALVES // 2, step, 0, unroll=4)
    idx_keys[...] = sorted32[...].reshape(8, 128, IDX_DIM).astype(BF16)


def split_heads(pair, vmq, queries):
    pad = jnp.zeros((HALF, KPAD - KD), BF16)
    for half in range(2):
        for h in range(HEADS_DEV):
            queries[2 * pair + half, h * HALF : (h + 1) * HALF, :] = jnp.concatenate(
                [vmq[pair, half * HALF : (half + 1) * HALF, h * KD : (h + 1) * KD], pad], axis=1
            )


LANES = HEADS_DEV * HALF
EXP_SCALE = SCORE_SCALE * LOG2E


def score_step(table, pair, i, keys, queries, scores, tops):
    early, g, block, limit = entry(table, pair, i)
    early = mask_of(early, (8, LANES))
    k = keys[block]
    s = lax.dot_general(k, queries[g], (((1,), (1,)), ((), ())), preferred_element_type=F32)
    row = lax.broadcasted_iota(jnp.int32, (512, LANES), 0)
    token = lax.broadcasted_iota(jnp.int32, (512, LANES), 1) % HALF
    s = jnp.where(row - token <= limit, s, NEG)
    scores[i] = s
    m = jnp.max(s.reshape(64, 8, LANES), axis=0)
    return (
        jnp.where(early, jnp.maximum(tops[0], m), tops[0]),
        jnp.where(early, tops[1], jnp.maximum(tops[1], m)),
    )


def exp_step(table, pair, i, scores, shifts, sums):
    early = entry(table, pair, i)[0]
    row = mask_of(early, (1, LANES))
    early = mask_of(early, (8, LANES))
    e = jnp.exp2(scores[i] * EXP_SCALE - jnp.where(row, shifts[0], shifts[1]))
    scores[i] = e
    m = jnp.sum(e.reshape(64, 8, LANES), axis=0)
    return (sums[0] + jnp.where(early, m, 0.0), sums[1] + jnp.where(early, 0.0, m))


def head_step(table, pair, i, scores, weights, tgt_ref):
    early = mask_of(entry(table, pair, i)[0], (1, LANES))
    group_of = lax.broadcasted_iota(jnp.int32, (8, 128), 1) // HALF
    weight = jnp.broadcast_to(jnp.where(early, weights[0], weights[1]), (8, LANES))
    low, even = group_of < 2, group_of % 2 == 0

    def heads(first):
        tiles = [slice(lt * 128, (lt + 1) * 128) for lt in range(LANES // 128)]
        terms = [scores[i, first : first + 8, cut] * weight[:, cut] for cut in tiles]
        return (terms[0] + terms[1]) + (terms[2] + terms[3])

    for part in range(4):
        for y in range(NY):
            v = [heads(part * 128 + 32 * a + 8 * y) for a in range(4)]
            t02 = jnp.where(low, v[0], v[2]) + pltpu.roll(jnp.where(low, v[2], v[0]), 64, 1)
            t13 = jnp.where(low, v[1], v[3]) + pltpu.roll(jnp.where(low, v[3], v[1]), 64, 1)
            swap = jnp.where(even, t13, t02)
            swap = jnp.where(even, pltpu.roll(swap, 96, 1), pltpu.roll(swap, 32, 1))
            tgt_ref[y, pair, 4 * i + part] = jnp.where(even, t02, t13) + swap


def start_tops():
    return (jnp.full((8, LANES), NEG, F32),) * 2


def start_sums():
    return (jnp.zeros((8, LANES), F32),) * 2


def shifts_of(tops):
    return tuple(jnp.max(t, axis=0, keepdims=True) * EXP_SCALE for t in tops)


def weights_of(sums):
    return tuple(1.0 / (HEADS * jnp.sum(t, axis=0, keepdims=True)) for t in sums)


def targets(table, pair, keys, queries, scores, tgt_ref, send):
    tops = lax.fori_loop(0, 9, lambda i, t: score_step(table, pair, i, keys, queries, scores, t), start_tops(), unroll=3)
    shifts = shifts_of(tops)
    sums = lax.fori_loop(0, 9, lambda i, t: exp_step(table, pair, i, scores, shifts, t), start_sums())
    weights = weights_of(sums)

    def last(i, carry):
        head_step(table, pair, i, scores, weights, tgt_ref)
        return carry

    for first in range(0, ENTRIES, 3):
        lax.fori_loop(first, first + 3, last, 0)
        send(pair, first)


def split_index_heads(pair, vidx, idx_q):
    for half in range(2):
        for j in range(IDX_HEADS):
            at = (j % 16 * 4 + j // 16) * HALF
            idx_q[2 * pair + half, at : at + HALF, :] = vidx[
                pair, half * HALF : (half + 1) * HALF, j * IDX_DIM : (j + 1) * IDX_DIM
            ]


def weight_rows(hw):
    turned = jnp.concatenate([hw, hw], axis=0).T
    return [
        [
            jnp.concatenate(
                [
                    turned[q * IDX_HEADS + a * 16 : q * IDX_HEADS + a * 16 + 16, half * HALF : (half + 1) * HALF]
                    for a in range(4)
                ],
                axis=1,
            )
            for half in range(2)
        ]
        for q in range(2)
    ]


def weight_cut(w_ref, g, ch):
    return jnp.concatenate([w_ref[g, 2 * ch : 2 * ch + 1, :], w_ref[g, 2 * ch + 1 : 2 * ch + 2, :]], axis=1)


def logit_step(table, pair, i, y, idx_keys, idx_q, w_ref, inner_ref, logit_ref, tops):
    early, g, block, limit = entry(table, pair, i)
    early = mask_of(early, (8, 128))
    k = idx_keys[block]
    acc = jnp.zeros((128, 128), F32)
    for ch in range(8):
        cut = slice(ch * 256, (ch + 1) * 256)
        inner = lax.dot_general(k, idx_q[g, cut, :], (((1,), (1,)), ((), ())), preferred_element_type=F32)
        inner_ref[pair, i, :, cut] = inner.astype(BF16)
        part = jnp.maximum(inner, 0.0) * weight_cut(w_ref, g, ch)
        acc = acc + part[:, :128] + part[:, 128:]
    acc = acc + pltpu.roll(acc, 64, 1)
    acc = acc + pltpu.roll(acc, 32, 1)
    row = lax.broadcasted_iota(jnp.int32, (128, 128), 0)
    token = lax.broadcasted_iota(jnp.int32, (128, 128), 1) % HALF
    offset = row // 8 * HALF + row % 8 - token
    acc = jnp.where(offset <= limit - 8 * y, acc * INDEX_NORM, NEG)
    logit_ref[pair, i] = acc
    m = jnp.max(acc.reshape(16, 8, 128), axis=0)
    return (
        jnp.where(early, jnp.maximum(tops[0], m), tops[0]),
        jnp.where(early, tops[1], jnp.maximum(tops[1], m)),
    )


def logit_stats(table, pair, logit_ref, stat_ref, tops):
    tops = [jnp.max(t, axis=0, keepdims=True) for t in tops]

    def step(i, sums):
        early = entry(table, pair, i)[0]
        row = mask_of(early, (1, 128))
        early = mask_of(early, (8, 128))
        e = jnp.exp(logit_ref[pair, i] - jnp.where(row, tops[0], tops[1]))
        e = jnp.sum(e.reshape(16, 8, 128), axis=0)
        return (sums[0] + jnp.where(early, e, 0.0), sums[1] + jnp.where(early, 0.0, e))

    sums = lax.fori_loop(0, 9, step, (jnp.zeros((8, 128), F32),) * 2, unroll=3)
    for half in range(2):
        g = 2 * pair + half
        stat_ref[g : g + 1, :] = tops[half]
        stat_ref[4 + g : 5 + g, :] = jnp.sum(sums[half], axis=0, keepdims=True)


def norms_of(stats_ref, g):
    tops = [stats_ref[d, g : g + 1, :] for d in range(NY)]
    top = jnp.maximum(jnp.maximum(tops[0], tops[1]), jnp.maximum(tops[2], tops[3]))
    norm = sum(stats_ref[d, 4 + g : 5 + g, :] * jnp.exp(tops[d] - top) for d in range(NY))
    return top, GRAD_COEF / norm


def gradient_step(table, pair, i, y, idx_q, w_ref, inner_ref, logit_ref, tgt_ref, arrive, norms, grad_ref):
    early, g, block, limit = entry(table, pair, i)
    early = mask_of(early, (1, 128))
    group_of = lax.broadcasted_iota(jnp.int32, (8, 128), 1) // HALF
    wide = []
    for part in range(4):
        at = 4 * i + part
        packed = tgt_ref[y, pair, at] + arrive[0, pair, at] + arrive[1, pair, at] + arrive[2, pair, at]
        for a in range(4):
            v = jnp.where(group_of == a, packed, 0.0)
            v = v + pltpu.roll(v, 64, 1)
            wide.append(v + pltpu.roll(v, 32, 1))
    target = jnp.concatenate(wide, axis=0)
    top = jnp.where(early, norms[0][0], norms[1][0])
    coef = jnp.where(early, norms[0][1], norms[1][1])
    row = lax.broadcasted_iota(jnp.int32, (128, 128), 0)
    token = lax.broadcasted_iota(jnp.int32, (128, 128), 1) % HALF
    offset = row // 8 * HALF + row % 8 - token
    seen = offset <= limit - 8 * y
    scaled = jnp.where(seen, jnp.exp(logit_ref[pair, i] - top) * coef - GRAD_COEF * target, 0.0)
    scaled = jnp.concatenate([scaled, scaled], axis=1)
    acc = jnp.zeros((128, IDX_DIM), F32)
    zero = jnp.zeros((), BF16)
    for ch in range(8):
        cut = slice(ch * 256, (ch + 1) * 256)
        signal = (scaled * weight_cut(w_ref, g, ch)).astype(BF16)
        signal = jnp.where(inner_ref[pair, i, :, cut] > zero, signal, zero)
        acc = acc + jnp.dot(signal, idx_q[g, cut, :], preferred_element_type=F32)
    grad_ref[pair, i] = acc


def collect_gradients(table, order, grad_ref, sorted_ref, part_ref):
    total = [grad_ref[0, 0] + grad_ref[1, 0] + grad_ref[0, 1] + grad_ref[1, 1]]
    total += [grad_ref[0, b + 1] + grad_ref[1, b + 1] for b in range(1, 5)] + [0.0] * 3
    for pair in range(2):
        for k in range(1, 4):
            flip = mask_of(entry(table, pair, k + 5)[0], (128, IDX_DIM))
            d = grad_ref[pair, k + 5]
            total[k] = total[k] + jnp.where(flip, d, 0.0)
            total[8 - k] = total[8 - k] + jnp.where(flip, 0.0, d)
    for b in range(8):
        sorted_ref[b * 16 : (b + 1) * 16] = total[b].reshape(16, 8, IDX_DIM)

    def store(chip, carry):
        for core in range(2):
            for half in range(2):
                place = order[4 * chip + 2 * core + half]
                rows = sorted_ref[place]
                part_ref[chip // NZ, chip % NZ, core * 16 + half * 8 : core * 16 + half * 8 + 8, :] = rows
        return carry

    lax.fori_loop(0, NX * NZ, store, 0, unroll=2)


X_ROWS = 24
PIECES = [(core, half) for core in range(2) for half in range(2)]


def along_x(core, half):
    return (core, half) != (1, 1)


def final_targets(x, z, y):
    return [
        (
            core, half, d,
            (seq_at(x, (z + d) % NZ, core) if along_x(core, half) else seq_at((x + d) % NX, z, core), y // 2 + 2 * half),
        )
        for core, half in PIECES
        for d in range(NZ if along_x(core, half) else NX)
    ]


def final_sources(x, z, y, summed_x):
    return [
        (
            d, 2 * odd + core,
            (seq_at(x, (z - d + NZ) % NZ, core) if summed_x else seq_at((x - d + NX) % NX, z, core), 2 * (y % 2) + odd),
            core,
        )
        for d in range(NZ if summed_x else NX)
        for odd in range(2)
        for core in range(2)
    ]


def await_bytes(ref, sem):
    pltpu.make_async_copy(ref, ref, sem).wait()


def scatter(
    x, z, c, y, peers_x, peers_z, remote, part_ref, out_ref, xa, za, slab_x, slab_z, final,
    xa_sem, za_sem, final_sem, meanwhile,
):
    for d in range(1, NX):
        remote(
            part_ref.at[(x + d) % NX, :, pl.ds(0, X_ROWS)], xa.at[d - 1], xa_sem.at[0], xa_sem.at[1], peers_x[d - 1],
        )
    for d in range(1, NZ):
        remote(
            part_ref.at[:, (z + d) % NZ, pl.ds(X_ROWS, 32 - X_ROWS)], za.at[d - 1], za_sem.at[0], za_sem.at[1],
            peers_z[d - 1],
        )
    slot = 2 * (y % 2) + c
    ends = final_targets(x, z, y)

    def piece(k):
        core, half, d, _ = ends[k]
        if along_x(core, half):
            return slab_x.at[(z + d) % NZ, pl.ds(16 * core + 8 * half, 8)]
        return slab_z.at[(x + d) % NX]

    def last_copy(k):
        d, to = ends[k][2:]
        return pltpu.make_async_remote_copy(
            src_ref=piece(k), dst_ref=final.at[4 * d + slot], send_sem=final_sem.at[0],
            recv_sem=final_sem.at[1], device_id=to, device_id_type=MESH,
        )

    def here(k):
        core, half, _, _ = ends[k]
        return jnp.logical_and(c == core, y // 2 + 2 * half == y)

    def send_last(summed_x):
        for k, (core, half, d, _) in enumerate(ends):
            if along_x(core, half) != summed_x:
                continue
            if d > 0:
                last_copy(k).start()
                continue

            @pl.when(jnp.logical_not(here(k)))
            def _(k=k):
                last_copy(k).start()

            @pl.when(here(k))
            def _(k=k):
                final[slot] = piece(k)[...]

    await_bytes(xa, xa_sem.at[1])
    slab_x[...] = part_ref[x, :, 0:X_ROWS, :] + xa[0] + xa[1] + xa[2]
    send_last(True)
    await_bytes(za, za_sem.at[1])
    total = part_ref[:, z, X_ROWS:32, :]
    for k in range(NZ - 1):
        total = total + za[k]
    slab_z[...] = total
    send_last(False)
    meanwhile()
    await_bytes(xa, xa_sem.at[0])
    await_bytes(za, za_sem.at[0])
    own = jnp.logical_or(y == 0, y == NY - 1)

    def await_pieces(count, sem):
        pl.when(own)(functools.partial(await_bytes, final.at[pl.ds(0, count - 1)], sem))
        pl.when(jnp.logical_not(own))(functools.partial(await_bytes, final.at[pl.ds(0, count)], sem))

    for summed_x in (True, False):

        @pl.when(by_x(c, y) if summed_x else jnp.logical_not(by_x(c, y)))
        def _(summed_x=summed_x):
            count = NZ if summed_x else NX
            await_pieces(4 * count, final_sem.at[1])
            for at in range(4):
                total = final[at]
                for d in range(1, count):
                    total = total + final[4 * d + at]
                out_ref[at // 2 * 8 : at // 2 * 8 + 8, at % 2 * IDX_DIM : (at % 2 + 1) * IDX_DIM] = total

    await_pieces(3 * NZ + NX, final_sem.at[0])


def by_x(c, y):
    return jnp.logical_or(c == 0, y < 2)


def whole_kernel(
    order, order_row, lat_any, idx_any, hw_any, mq_any, iq_any, out_ref,
    table, first_row, first, lat_ref, idx_ref, hw_ref, w_other, p_ref, q_ref, slots, stage_out, stage_in, idx32, idx_stage_out, idx_stage_in, idxg, slots32, sorted32, idx_keys,
    vmq, queries, keys, scores, tgt_ref, vidx, idx_q, w_ref, inner_ref, logit_ref, stat_ref, stats_ref, arrive,
    grad_ref, part_ref, xa, za, slab_x, slab_z, final,
    load_sem, pair_send, pair_recv, ring_send, ring_recv, idx_sem,
    tgt_sem, stat_sem, xa_sem, za_sem, final_sem,
):
    x, z, c, y = coords()
    seq = lax.axis_index("seq")
    me = x * NZ + z
    barrier = pltpu.get_barrier_semaphore()
    partner = (seq_at(x, z, 1 - c), y)
    peers_y = [(seq, (y + d) % NY) for d in range(1, NY)]
    peers_x = [(seq_at((x + d) % NX, z, c), y) for d in range(1, NX)]
    peers_z = [(seq_at(x, (z + d) % NZ, c), y) for d in range(1, NZ)]
    ring = {("x", 1): peers_x[0], ("x", -1): peers_x[-1], ("z", 1): peers_z[0], ("z", -1): peers_z[-1]}

    def tell(to):
        pl.semaphore_signal(barrier, inc=1, device_id=to, device_id_type=MESH)

    for to in peers_x + peers_z + peers_y + [partner]:
        tell(to)
    loads = [
        pltpu.make_async_copy(src, dst, load_sem.at[k])
        for k, (src, dst) in enumerate(
            [
                (lat_any, lat_ref), (idx_any, idx_ref), (hw_any, hw_ref), (iq_any.at[c], vidx.at[0]),
                (mq_any.at[c], vmq.at[0]),
            ]
        )
    ]
    for d in loads:
        d.start()
    for summed_x in (True, False):

        @pl.when(by_x(c, y) if summed_x else jnp.logical_not(by_x(c, y)))
        def _(summed_x=summed_x):
            for d, _, source, core in final_sources(x, z, y, summed_x):
                if d == 0:
                    pl.when(jnp.logical_or(core != c, source[1] != y))(functools.partial(tell, source))
                else:
                    tell(source)

    fill_table(order, seq, table)
    first_row[...] = jnp.broadcast_to(slots_of(order_row[...]), (8, HALVES))
    to_scalars = pltpu.make_async_copy(first_row, first, load_sem.at[5])
    to_scalars.start()
    for d in loads[:3]:
        d.wait()
    weights = weight_rows(hw_ref[...])
    for half in range(2):
        w_other[half] = jnp.where(c == 0, weights[1][half], weights[0][half])
        w_ref[half] = jnp.where(c == 0, weights[0][half], weights[1][half])
    lat = lat_ref[...]
    stage_out[:, 0:KD] = jnp.where(c == 0, lat[:, KD:], lat[:, :KD])
    stage_out[:, KD:] = jnp.zeros((TOK, KPAD - KD), BF16)
    idx32[...] = idx_ref[...].astype(F32)
    rows = jnp.concatenate(
        [idx32[pl.ds(pl.multiple_of(y * 8, 8), 8), :], idx32[pl.ds(pl.multiple_of(HALF + y * 8, 8), 8), :]], axis=0
    )
    idx_stage_out[...] = jnp.where(c == 0, rows[:, IDX_DIM:], rows[:, :IDX_DIM]).astype(BF16)
    own = jnp.where(jnp.logical_or(y == 0, y == NY - 1), 1, 0)
    pl.semaphore_wait(barrier, NX - 1 + NZ - 1 + NY - 1 + 1 + 3 * NZ + NX - own)

    def remote(src, dst, send, recv, to):
        d = pltpu.make_async_remote_copy(
            src_ref=src, dst_ref=dst, send_sem=send, recv_sem=recv, device_id=to, device_id_type=MESH
        )
        d.start()
        return d

    def to_partner(k, src, dst):
        return remote(src, dst, pair_send.at[k], pair_recv.at[k], partner)

    pair_copies = [
        to_partner(0, stage_out, stage_in),
        to_partner(1, idx_stage_out, idx_stage_in),
        to_partner(2, w_other, w_ref.at[pl.ds(2, 2)]),
        to_partner(3, iq_any.at[1 - c], vidx.at[1]),
        to_partner(4, mq_any.at[1 - c], vmq.at[1]),
    ]
    mine = jnp.where(c == 0, lat[:, :KD], lat[:, KD:])
    idx_mine = jnp.where(c == 0, rows[:, :IDX_DIM], rows[:, IDX_DIM:]).astype(BF16)
    pair_copies[0].wait_recv()
    pair_copies[1].wait_recv()
    from_partner = stage_in[:, :KD]
    both = jnp.concatenate([jnp.where(c == 0, mine, from_partner), jnp.where(c == 0, from_partner, mine)], axis=1)
    p_ref[me] = both[:HALF, :P_LANES]
    q_ref[me] = jnp.concatenate([both[HALF:], both[:HALF, P_LANES:]], axis=1)
    idx_other = idx_stage_in[...]
    idxg[x, z, 0:16] = jnp.where(c == 0, idx_mine, idx_other)
    idxg[x, z, 16:32] = jnp.where(c == 0, idx_other, idx_mine)

    counter = [0]
    live, origin = {}, {}
    landed = [(0, me, 0, HALF), (1, me, 0, HALF)]

    def send(part, axis, way, dx, dz, lo, hi):
        k = counter[0]
        counter[0] += 1

        def block(ox, oz):
            ref = q_ref if part else p_ref
            return ref.at[(x + ox + 2 * NX) % NX * NZ + (z + oz + 2 * NZ) % NZ, pl.ds(lo, hi - lo)]

        gone_sem = ring_send.at[k if k < 4 else 4 + part]
        out = remote(block(dx, dz), block(dx, dz), gone_sem, ring_recv.at[k], ring[(axis, way)])
        here = block(dx - way, dz) if axis == "x" else block(dx, dz - way)
        arrival = pltpu.make_async_remote_copy(
            src_ref=here, dst_ref=here, send_sem=gone_sem, recv_sem=ring_recv.at[k],
            device_id=ring[(axis, way)], device_id_type=MESH,
        )
        live[k] = [out, arrival, False]
        ix, iz = (dx - way, dz) if axis == "x" else (dx, dz - way)
        origin[k] = (part, (x + ix + 2 * NX) % NX * NZ + (z + iz + 2 * NZ) % NZ, lo, hi)
        return k

    def arrived(k):
        if not live[k][2]:
            live[k][1].wait_recv()
            live[k][2] = True
            landed.append(origin[k])

    def left(ks):
        for k in ks:
            live[k][0].wait_send()

    last_x, last_z = NX // 2, NZ // 2

    def hop(part, axis, dx, dz, step, before):
        last = last_x if axis == "x" else last_z
        ks = []
        for way, half in ((1, (0, 16)), (-1, (16, 32))):
            if before is not None:
                arrived(before[0 if way == 1 else 1])
            away = -way * (step - 1)
            ox, oz = (away, dz) if axis == "x" else (dx, away)
            lo, hi = half if step == last else (0, 32)
            ks.append(send(part, axis, way, ox, oz, lo, hi))
        return ks

    zp, xq, zq = {}, {}, {}

    def start_p(dx):
        zp[dx] = {1: hop(0, "z", dx, 0, 1, None)}

    def advance_p(dx, step):
        zp[dx][step] = hop(0, "z", dx, 0, step, zp[dx][step - 1])

    def advance_q(step):
        before = zq[step - 1]
        if step <= last_z:
            zq[step] = hop(1, "z", 0, 0, step, before)
        else:
            arrived(before[0])
            arrived(before[1])
        for dz in (-(step - 1), step - 1) if step <= last_z else (last_z,):
            xq[dz] = {1: hop(1, "x", 0, dz, 1, None)}

    def finish_q(dz):
        xq[dz][2] = hop(1, "x", 0, dz, 2, xq[dz][1])

    def start_index():
        for d in range(1, NZ):
            ref = idxg.at[x, z]
            remote(ref, ref, idx_sem.at[0], idx_sem.at[1], peers_z[d - 1])

    def spread_index():
        await_bytes(idxg.at[x, pl.ds(0, NZ - 1)], idx_sem.at[1])
        for d in range(1, NX):
            remote(idxg.at[x], idxg.at[x], idx_sem.at[2], idx_sem.at[3], peers_x[d - 1])

    def have_index():
        await_bytes(idxg.at[pl.ds(0, NX - 1)], idx_sem.at[3])
        pair_copies[2].wait_recv()
        to_scalars.wait()
        sort_index_keys(first, idxg, slots32, sorted32, idx_keys)

    logit_tops = [(jnp.full((8, 128), NEG, F32),) * 2 for _ in range(2)]

    def logits(pair, first, last):
        logit_tops[pair] = lax.fori_loop(
            first, last,
            lambda i, t: logit_step(table, pair, i, y, idx_keys, idx_q, w_ref, inner_ref, logit_ref, t),
            logit_tops[pair],
        )
        if last == ENTRIES:
            logit_stats(table, pair, logit_ref, stat_ref, logit_tops[pair])

    def send_stats():
        for d in range(1, NY):
            remote(stat_ref, stats_ref.at[d], stat_sem.at[0], stat_sem.at[1], peers_y[d - 1])
        stats_ref[0] = stat_ref[...]

    def own_queries():
        loads[4].wait()
        split_heads(0, vmq, queries)

    def own_index_queries():
        loads[3].wait()
        split_index_heads(0, vidx, idx_q)

    def other_index_queries():
        pair_copies[3].wait_recv()
        split_index_heads(1, vidx, idx_q)

    def other_queries():
        pair_copies[4].wait_recv()
        split_heads(1, vmq, queries)

    work = [own_index_queries, spread_index, own_queries, have_index]
    work += [functools.partial(logits, 0, k, k + 3) for k in (0, 3, 6)]
    work += [other_index_queries]
    work += [functools.partial(logits, 1, k, k + 3) for k in (0, 3, 6)]
    work += [send_stats, other_queries]

    def between():
        if work:
            work.pop(0)()
        for _ in range(min(4, len(landed))):
            split_cores(p_ref, q_ref, slots, *landed.pop(0))

    zq[1] = hop(1, "z", 0, 0, 1, None)
    xp = hop(0, "x", 0, 0, 1, None)
    left(zq[1])
    start_p(0)
    left(xp)
    xq[0] = {1: hop(1, "x", 0, 0, 1, None)}
    start_index()
    between()
    advance_q(2)
    xp2 = hop(0, "x", 0, 0, 2, xp)
    start_p(-1)
    start_p(1)
    between()
    advance_p(0, 2)
    finish_q(0)
    advance_q(3)
    arrived(xp2[0])
    arrived(xp2[1])
    start_p(2)
    between()
    advance_p(-1, 2)
    advance_p(1, 2)
    between()
    advance_p(0, 3)
    advance_q(4)
    finish_q(-1)
    finish_q(1)
    between()
    advance_p(2, 2)
    between()
    advance_p(-1, 3)
    advance_p(1, 3)
    advance_q(5)
    between()
    finish_q(-2)
    finish_q(2)
    advance_p(0, 4)
    between()
    advance_p(2, 3)
    between()
    advance_p(-1, 4)
    advance_p(1, 4)
    finish_q(-3)
    finish_q(3)
    between()
    advance_p(2, 4)
    finish_q(last_z)
    while work:
        between()
    for k in live:
        arrived(k)
        while landed:
            split_cores(p_ref, q_ref, slots, *landed.pop(0))
    sort_keys(first, slots, keys)

    def send_targets(pair, at):
        cut = pl.ds(4 * at, 12)
        for d in range(1, NY):
            remote(
                tgt_ref.at[(y + d) % NY, pair, cut], arrive.at[d - 1, pair, cut], tgt_sem.at[0],
                tgt_sem.at[1 + pair * 3 + at // 3], peers_y[d - 1],
            )

    for pair in range(2):
        targets(table, pair, keys, queries, scores, tgt_ref, send_targets)
    await_bytes(stats_ref.at[pl.ds(1, NY - 1)], stat_sem.at[1])
    for pair in range(2):
        norms = [norms_of(stats_ref, 2 * pair + half) for half in range(2)]

        def step(i, carry):
            gradient_step(
                table, pair, i, y, idx_q, w_ref, inner_ref, logit_ref, tgt_ref, arrive, norms, grad_ref
            )
            return carry

        for at in range(0, ENTRIES, 3):
            await_bytes(arrive.at[:, pair, pl.ds(4 * at, 12)], tgt_sem.at[1 + pair * 3 + at // 3])
            lax.fori_loop(at, at + 3, step, 0)
    collect_gradients(table, order, grad_ref, sorted32, part_ref)

    def settle():
        blocks = NX * NZ - 1 - 2
        await_bytes(p_ref.at[pl.ds(0, blocks)], ring_send.at[4])
        await_bytes(q_ref.at[pl.ds(0, blocks)], ring_send.at[5])
        await_bytes(idxg.at[x, pl.ds(0, NZ - 1)], idx_sem.at[0])
        await_bytes(idxg.at[pl.ds(0, NX - 1)], idx_sem.at[2])
        await_bytes(stats_ref.at[pl.ds(1, NY - 1)], stat_sem.at[0])
        await_bytes(arrive, tgt_sem.at[0])
        for d in pair_copies:
            d.wait_send()

    scatter(
        x, z, c, y, peers_x, peers_z, remote, part_ref, out_ref, xa, za, slab_x, slab_z, final,
        xa_sem, za_sem, final_sem, settle,
    )


RING_COPIES = 76


def whole_call(order, order_row, lat, idx, hw, mq, iq):
    any_spec = pl.BlockSpec(memory_space=pl.ANY)
    vmem = pl.BlockSpec(memory_space=pltpu.VMEM)
    smem = pl.BlockSpec(memory_space=pltpu.SMEM)
    dma = pltpu.SemaphoreType.DMA
    return pl.pallas_call(
        whole_kernel,
        name="indexer_key_gradient",
        out_shape=jax.ShapeDtypeStruct((16, 2 * IDX_DIM), F32),
        in_specs=[smem, vmem] + [any_spec] * 5,
        out_specs=vmem,
        scratch_shapes=[
            pltpu.SMEM((8 * ENTRIES,), jnp.int32),
            pltpu.VMEM((8, HALVES), jnp.int32),
            pltpu.SMEM((8, HALVES), jnp.int32),
            pltpu.VMEM((TOK, 2 * KD), BF16),
            pltpu.VMEM((TOK, 2 * IDX_DIM), BF16),
            pltpu.VMEM((TOK, 2 * IDX_HEADS), F32),
            pltpu.VMEM((2, 16, 128), F32),
            pltpu.VMEM((NX * NZ, HALF, P_LANES), BF16),
            pltpu.VMEM((NX * NZ, HALF, Q_LANES), BF16),
            pltpu.VMEM((HALVES, HALF, KPAD), BF16),
            pltpu.VMEM((TOK, KPAD), BF16),
            pltpu.VMEM((TOK, KPAD), BF16),
            pltpu.VMEM((TOK, 2 * IDX_DIM), F32),
            pltpu.VMEM((16, IDX_DIM), BF16),
            pltpu.VMEM((16, IDX_DIM), BF16),
            pltpu.VMEM((NX, NZ, 32, IDX_DIM), BF16),
            pltpu.VMEM((HALVES, 8, IDX_DIM), F32),
            pltpu.VMEM((HALVES, 8, IDX_DIM), F32),
            pltpu.VMEM((8, 128, IDX_DIM), BF16),
            pltpu.VMEM((2, TOK, HEADS_DEV * KD), BF16),
            pltpu.VMEM((4, LANES, KPAD), BF16),
            pltpu.VMEM((8, 512, KPAD), BF16),
            pltpu.VMEM((ENTRIES, 512, LANES), F32),
            pltpu.VMEM((NY, 2, SLOTS, 8, 128), F32),
            pltpu.VMEM((2, TOK, IDX_HEADS * IDX_DIM), BF16),
            pltpu.VMEM((4, IDX_HEADS * HALF, IDX_DIM), BF16),
            pltpu.VMEM((4, 16, 128), F32),
            pltpu.VMEM((2, ENTRIES, 128, IDX_HEADS * HALF), BF16),
            pltpu.VMEM((2, ENTRIES, 128, 128), F32),
            pltpu.VMEM((8, 128), F32),
            pltpu.VMEM((NY, 8, 128), F32),
            pltpu.VMEM((NY - 1, 2, SLOTS, 8, 128), F32),
            pltpu.VMEM((2, ENTRIES, 128, IDX_DIM), F32),
            pltpu.VMEM((NX, NZ, 32, IDX_DIM), F32),
            pltpu.VMEM((NX - 1, NZ, X_ROWS, IDX_DIM), F32),
            pltpu.VMEM((NZ - 1, NX, 32 - X_ROWS, IDX_DIM), F32),
            pltpu.VMEM((NZ, X_ROWS, IDX_DIM), F32),
            pltpu.VMEM((NX, 32 - X_ROWS, IDX_DIM), F32),
            pltpu.VMEM((4 * NZ, 8, IDX_DIM), F32),
            dma((6,)),
            dma((5,)),
            dma((5,)),
            dma((6,)),
            dma((RING_COPIES,)),
            dma((4,)),
            dma((7,)),
            dma((2,)),
            dma((2,)),
            dma((2,)),
            dma((2,)),
        ],
        compiler_params=pltpu.CompilerParams(
            collective_id=0, has_side_effects=True, vmem_limit_bytes=VMEM_BYTES
        ),
    )(order, order_row, lat, idx, hw, mq, iq)


def per_device(mla_queries, latent_keys, index_queries, index_keys, head_weights, block_order):
    row = block_order.reshape(1, HALVES)
    return whole_call(block_order, row, latent_keys, index_keys, head_weights, mla_queries, index_queries)


def solution(mesh):
    return jax.shard_map(
        per_device,
        mesh=mesh,
        in_specs=(
            P(None, "seq", "head"),
            P("seq", None),
            P(None, "seq", None),
            P("seq", None),
            P("seq", None),
            P(),
        ),
        out_specs=P(("seq", "head"), None),
        check_vma=False,
    )
```

```python
import functools

import jax
import jax.numpy as jnp
from jax import lax
from jax.experimental import pallas as pl
from jax.experimental.pallas import tpu as pltpu
from jax.sharding import PartitionSpec as P

MESH = pl.DeviceIdType.MESH
NX, NZ, NY = 4, 8, 4
HEADS = 64
HEADS_DEV = 16
KD = 576
KPAD = 640
IDX_HEADS = 64
IDX_DIM = 128
TOK = 64
HALF = 32
HALVES = 128
SLOTS = 36
SCORE_SCALE = 192.0 ** (-0.5)
LOG2E = 1.4426950408889634
INDEX_NORM = (IDX_HEADS * IDX_DIM) ** (-0.5)
GRAD_COEF = 1024.0 * INDEX_NORM
NEG = -1e30
VMEM_BYTES = 60 * 1024 * 1024
F32 = jnp.float32
BF16 = jnp.bfloat16


def coords():
    s = lax.axis_index("seq")
    y = lax.axis_index("head")
    return s // (2 * NZ), (s // 2) % NZ, s % 2, y


def seq_at(x, z, c):
    return (x * NZ + z) * 2 + c


ENTRIES = 9


def fill_table(order, seq, table):
    for pair in range(2):
        device = seq if pair == 0 else seq + 1 - 2 * (seq % 2)
        early_place, late_place = order[2 * device], order[2 * device + 1]
        for i in range(ENTRIES):
            k = i - 5
            flip = jnp.where(early_place // 16 >= k, 1, 0)
            early = 1 if i == 0 else 0 if i < 6 else flip
            block = 0 if i == 0 else i - 1 if i < 6 else flip * k + (1 - flip) * (8 - k)
            place = early * early_place + (1 - early) * late_place
            fields = (early, 2 * pair + 1 - early, block, place * HALF - block * 512)
            for field, value in enumerate(fields):
                table[(field * 2 + pair) * ENTRIES + i] = jnp.int32(value)


def slots_of(row):
    slot = lax.broadcasted_iota(jnp.int32, (HALVES, HALVES), 0)
    lane = lax.broadcasted_iota(jnp.int32, (HALVES, HALVES), 1)
    column = jnp.sum(jnp.where(slot == lane, row, 0), axis=1, keepdims=True)
    return jnp.max(jnp.where(column == lane, slot - slot % 2, 0), axis=0, keepdims=True)


def entry(table, pair, i):
    return [table[(field * 2 + pair) * ENTRIES + i] for field in range(4)]


def mask_of(flag, shape):
    return jnp.zeros(shape, jnp.int32) + flag > 0


P_LANES = 7 * 128
Q_LANES = 4 * KD - P_LANES


def split_cores(p_ref, q_ref, slots, part, chip, lo, hi):
    pad = jnp.zeros((hi - lo, KPAD - KD), BF16)

    def padded(rows):
        return jnp.concatenate([rows, pad], axis=1)

    if part == 0:
        slots[4 * chip, lo:hi, :] = padded(p_ref[chip, lo:hi, :KD])
        slots[4 * chip + 2, lo:hi, : P_LANES - KD] = p_ref[chip, lo:hi, KD:]
    else:
        slots[4 * chip + 1, lo:hi, :] = padded(q_ref[chip, lo:hi, :KD])
        slots[4 * chip + 3, lo:hi, :] = padded(q_ref[chip, lo:hi, KD : 2 * KD])
        slots[4 * chip + 2, lo:hi, P_LANES - KD :] = padded(q_ref[chip, lo:hi, 2 * KD :])


def sort_keys(first, slots, keys):
    def step(p, carry):
        slot = first[0, p]
        low, high = p, HALVES - 1 - p
        keys[low // 16, pl.ds(pl.multiple_of(low % 16 * HALF, HALF), HALF), :] = slots[slot]
        keys[high // 16, pl.ds(pl.multiple_of(high % 16 * HALF, HALF), HALF), :] = slots[slot + 1]
        return carry

    lax.fori_loop(0, HALVES // 2, step, 0, unroll=4)


def sort_index_keys(first, idxg, slots32, sorted32, idx_keys):
    slots32[...] = idxg[...].astype(F32).reshape(HALVES, 8, IDX_DIM)

    def step(p, carry):
        slot = first[0, p]
        sorted32[p] = slots32[slot]
        sorted32[HALVES - 1 - p] = slots32[slot + 1]
        return carry

    lax.fori_loop(0, HALVES // 2, step, 0, unroll=4)
    idx_keys[...] = sorted32[...].reshape(8, 128, IDX_DIM).astype(BF16)


def split_heads(pair, vmq, queries):
    pad = jnp.zeros((HALF, KPAD - KD), BF16)
    for half in range(2):
        for h in range(HEADS_DEV):
            queries[2 * pair + half, h * HALF : (h + 1) * HALF, :] = jnp.concatenate(
                [vmq[pair, half * HALF : (half + 1) * HALF, h * KD : (h + 1) * KD], pad], axis=1
            )


LANES = HEADS_DEV * HALF
EXP_SCALE = SCORE_SCALE * LOG2E


def score_step(table, pair, i, keys, queries, scores, tops):
    early, g, block, limit = entry(table, pair, i)
    early = mask_of(early, (8, LANES))
    k = keys[block]
    s = lax.dot_general(k, queries[g], (((1,), (1,)), ((), ())), preferred_element_type=F32)
    row = lax.broadcasted_iota(jnp.int32, (512, LANES), 0)
    token = lax.broadcasted_iota(jnp.int32, (512, LANES), 1) % HALF
    s = jnp.where(row - token <= limit, s, NEG)
    scores[i] = s
    m = jnp.max(s.reshape(64, 8, LANES), axis=0)
    return (
        jnp.where(early, jnp.maximum(tops[0], m), tops[0]),
        jnp.where(early, tops[1], jnp.maximum(tops[1], m)),
    )


def exp_step(table, pair, i, scores, shifts, sums):
    early = entry(table, pair, i)[0]
    row = mask_of(early, (1, LANES))
    early = mask_of(early, (8, LANES))
    e = jnp.exp2(scores[i] * EXP_SCALE - jnp.where(row, shifts[0], shifts[1]))
    scores[i] = e
    m = jnp.sum(e.reshape(64, 8, LANES), axis=0)
    return (sums[0] + jnp.where(early, m, 0.0), sums[1] + jnp.where(early, 0.0, m))


def head_step(table, pair, i, scores, weights, tgt_ref):
    early = mask_of(entry(table, pair, i)[0], (1, LANES))
    group_of = lax.broadcasted_iota(jnp.int32, (8, 128), 1) // HALF
    weight = jnp.broadcast_to(jnp.where(early, weights[0], weights[1]), (8, LANES))
    low, even = group_of < 2, group_of % 2 == 0

    def heads(first):
        tiles = [slice(lt * 128, (lt + 1) * 128) for lt in range(LANES // 128)]
        terms = [scores[i, first : first + 8, cut] * weight[:, cut] for cut in tiles]
        return (terms[0] + terms[1]) + (terms[2] + terms[3])

    for part in range(4):
        for y in range(NY):
            v = [heads(part * 128 + 32 * a + 8 * y) for a in range(4)]
            t02 = jnp.where(low, v[0], v[2]) + pltpu.roll(jnp.where(low, v[2], v[0]), 64, 1)
            t13 = jnp.where(low, v[1], v[3]) + pltpu.roll(jnp.where(low, v[3], v[1]), 64, 1)
            swap = jnp.where(even, t13, t02)
            swap = jnp.where(even, pltpu.roll(swap, 96, 1), pltpu.roll(swap, 32, 1))
            tgt_ref[y, pair, 4 * i + part] = jnp.where(even, t02, t13) + swap


def start_tops():
    return (jnp.full((8, LANES), NEG, F32),) * 2


def start_sums():
    return (jnp.zeros((8, LANES), F32),) * 2


def shifts_of(tops):
    return tuple(jnp.max(t, axis=0, keepdims=True) * EXP_SCALE for t in tops)


def weights_of(sums):
    return tuple(1.0 / (HEADS * jnp.sum(t, axis=0, keepdims=True)) for t in sums)


def targets(table, pair, keys, queries, scores, tgt_ref, send):
    tops = lax.fori_loop(0, 9, lambda i, t: score_step(table, pair, i, keys, queries, scores, t), start_tops(), unroll=3)
    shifts = shifts_of(tops)
    sums = lax.fori_loop(0, 9, lambda i, t: exp_step(table, pair, i, scores, shifts, t), start_sums())
    weights = weights_of(sums)

    def last(i, carry):
        head_step(table, pair, i, scores, weights, tgt_ref)
        return carry

    for first in range(0, ENTRIES, 3):
        lax.fori_loop(first, first + 3, last, 0)
        send(pair, first)


def split_index_heads(pair, vidx, idx_q):
    for half in range(2):
        for j in range(IDX_HEADS):
            at = (j % 16 * 4 + j // 16) * HALF
            idx_q[2 * pair + half, at : at + HALF, :] = vidx[
                pair, half * HALF : (half + 1) * HALF, j * IDX_DIM : (j + 1) * IDX_DIM
            ]


def weight_rows(hw):
    turned = jnp.concatenate([hw, hw], axis=0).T
    return [
        [
            jnp.concatenate(
                [
                    turned[q * IDX_HEADS + a * 16 : q * IDX_HEADS + a * 16 + 16, half * HALF : (half + 1) * HALF]
                    for a in range(4)
                ],
                axis=1,
            )
            for half in range(2)
        ]
        for q in range(2)
    ]


def weight_cut(w_ref, g, ch):
    return jnp.concatenate([w_ref[g, 2 * ch : 2 * ch + 1, :], w_ref[g, 2 * ch + 1 : 2 * ch + 2, :]], axis=1)


def logit_step(table, pair, i, y, idx_keys, idx_q, w_ref, inner_ref, logit_ref, tops):
    early, g, block, limit = entry(table, pair, i)
    early = mask_of(early, (8, 128))
    k = idx_keys[block]
    acc = jnp.zeros((128, 128), F32)
    for ch in range(8):
        cut = slice(ch * 256, (ch + 1) * 256)
        inner = lax.dot_general(k, idx_q[g, cut, :], (((1,), (1,)), ((), ())), preferred_element_type=F32)
        inner_ref[pair, i, :, cut] = inner.astype(BF16)
        part = jnp.maximum(inner, 0.0) * weight_cut(w_ref, g, ch)
        acc = acc + part[:, :128] + part[:, 128:]
    acc = acc + pltpu.roll(acc, 64, 1)
    acc = acc + pltpu.roll(acc, 32, 1)
    row = lax.broadcasted_iota(jnp.int32, (128, 128), 0)
    token = lax.broadcasted_iota(jnp.int32, (128, 128), 1) % HALF
    offset = row // 8 * HALF + row % 8 - token
    acc = jnp.where(offset <= limit - 8 * y, acc * INDEX_NORM, NEG)
    logit_ref[pair, i] = acc
    m = jnp.max(acc.reshape(16, 8, 128), axis=0)
    return (
        jnp.where(early, jnp.maximum(tops[0], m), tops[0]),
        jnp.where(early, tops[1], jnp.maximum(tops[1], m)),
    )


def logit_stats(table, pair, logit_ref, stat_ref, tops):
    tops = [jnp.max(t, axis=0, keepdims=True) for t in tops]

    def step(i, sums):
        early = entry(table, pair, i)[0]
        row = mask_of(early, (1, 128))
        early = mask_of(early, (8, 128))
        e = jnp.exp(logit_ref[pair, i] - jnp.where(row, tops[0], tops[1]))
        e = jnp.sum(e.reshape(16, 8, 128), axis=0)
        return (sums[0] + jnp.where(early, e, 0.0), sums[1] + jnp.where(early, 0.0, e))

    sums = lax.fori_loop(0, 9, step, (jnp.zeros((8, 128), F32),) * 2, unroll=3)
    for half in range(2):
        g = 2 * pair + half
        stat_ref[g : g + 1, :] = tops[half]
        stat_ref[4 + g : 5 + g, :] = jnp.sum(sums[half], axis=0, keepdims=True)


def norms_of(stats_ref, g):
    tops = [stats_ref[d, g : g + 1, :] for d in range(NY)]
    top = jnp.maximum(jnp.maximum(tops[0], tops[1]), jnp.maximum(tops[2], tops[3]))
    norm = sum(stats_ref[d, 4 + g : 5 + g, :] * jnp.exp(tops[d] - top) for d in range(NY))
    return top, GRAD_COEF / norm


def gradient_step(table, pair, i, y, idx_q, w_ref, inner_ref, logit_ref, tgt_ref, arrive, norms, grad_ref):
    early, g, block, limit = entry(table, pair, i)
    early = mask_of(early, (1, 128))
    group_of = lax.broadcasted_iota(jnp.int32, (8, 128), 1) // HALF
    wide = []
    for part in range(4):
        at = 4 * i + part
        packed = tgt_ref[y, pair, at] + arrive[0, pair, at] + arrive[1, pair, at] + arrive[2, pair, at]
        for a in range(4):
            v = jnp.where(group_of == a, packed, 0.0)
            v = v + pltpu.roll(v, 64, 1)
            wide.append(v + pltpu.roll(v, 32, 1))
    target = jnp.concatenate(wide, axis=0)
    top = jnp.where(early, norms[0][0], norms[1][0])
    coef = jnp.where(early, norms[0][1], norms[1][1])
    row = lax.broadcasted_iota(jnp.int32, (128, 128), 0)
    token = lax.broadcasted_iota(jnp.int32, (128, 128), 1) % HALF
    offset = row // 8 * HALF + row % 8 - token
    seen = offset <= limit - 8 * y
    scaled = jnp.where(seen, jnp.exp(logit_ref[pair, i] - top) * coef - GRAD_COEF * target, 0.0)
    scaled = jnp.concatenate([scaled, scaled], axis=1)
    acc = jnp.zeros((128, IDX_DIM), F32)
    zero = jnp.zeros((), BF16)
    for ch in range(8):
        cut = slice(ch * 256, (ch + 1) * 256)
        signal = (scaled * weight_cut(w_ref, g, ch)).astype(BF16)
        signal = jnp.where(inner_ref[pair, i, :, cut] > zero, signal, zero)
        acc = acc + jnp.dot(signal, idx_q[g, cut, :], preferred_element_type=F32)
    grad_ref[pair, i] = acc


def collect_gradients(table, order, grad_ref, sorted_ref, part_ref):
    total = [grad_ref[0, 0] + grad_ref[1, 0] + grad_ref[0, 1] + grad_ref[1, 1]]
    total += [grad_ref[0, b + 1] + grad_ref[1, b + 1] for b in range(1, 5)] + [0.0] * 3
    for pair in range(2):
        for k in range(1, 4):
            flip = mask_of(entry(table, pair, k + 5)[0], (128, IDX_DIM))
            d = grad_ref[pair, k + 5]
            total[k] = total[k] + jnp.where(flip, d, 0.0)
            total[8 - k] = total[8 - k] + jnp.where(flip, 0.0, d)
    for b in range(8):
        sorted_ref[b * 16 : (b + 1) * 16] = total[b].reshape(16, 8, IDX_DIM)

    def store(chip, carry):
        for core in range(2):
            for half in range(2):
                place = order[4 * chip + 2 * core + half]
                rows = sorted_ref[place]
                part_ref[chip // NZ, chip % NZ, core * 16 + half * 8 : core * 16 + half * 8 + 8, :] = rows
        return carry

    lax.fori_loop(0, NX * NZ, store, 0, unroll=2)


X_ROWS = 24
PIECES = [(core, half) for core in range(2) for half in range(2)]


def along_x(core, half):
    return (core, half) != (1, 1)


def final_targets(x, z, y):
    return [
        (
            core, half, d,
            (seq_at(x, (z + d) % NZ, core) if along_x(core, half) else seq_at((x + d) % NX, z, core), y // 2 + 2 * half),
        )
        for core, half in PIECES
        for d in range(NZ if along_x(core, half) else NX)
    ]


def final_sources(x, z, y, summed_x):
    return [
        (
            d, 2 * odd + core,
            (seq_at(x, (z - d + NZ) % NZ, core) if summed_x else seq_at((x - d + NX) % NX, z, core), 2 * (y % 2) + odd),
            core,
        )
        for d in range(NZ if summed_x else NX)
        for odd in range(2)
        for core in range(2)
    ]


def await_bytes(ref, sem):
    pltpu.make_async_copy(ref, ref, sem).wait()


def scatter(
    x, z, c, y, peers_x, peers_z, remote, part_ref, out_ref, xa, za, slab_x, slab_z, final,
    xa_sem, za_sem, final_sem, meanwhile,
):
    for d in range(1, NX):
        remote(
            part_ref.at[(x + d) % NX, :, pl.ds(0, X_ROWS)], xa.at[d - 1], xa_sem.at[0], xa_sem.at[1], peers_x[d - 1],
        )
    for d in range(1, NZ):
        remote(
            part_ref.at[:, (z + d) % NZ, pl.ds(X_ROWS, 32 - X_ROWS)], za.at[d - 1], za_sem.at[0], za_sem.at[1],
            peers_z[d - 1],
        )
    slot = 2 * (y % 2) + c
    ends = final_targets(x, z, y)

    def piece(k):
        core, half, d, _ = ends[k]
        if along_x(core, half):
            return slab_x.at[(z + d) % NZ, pl.ds(16 * core + 8 * half, 8)]
        return slab_z.at[(x + d) % NX]

    def last_copy(k):
        d, to = ends[k][2:]
        return pltpu.make_async_remote_copy(
            src_ref=piece(k), dst_ref=final.at[4 * d + slot], send_sem=final_sem.at[0],
            recv_sem=final_sem.at[1], device_id=to, device_id_type=MESH,
        )

    def here(k):
        core, half, _, _ = ends[k]
        return jnp.logical_and(c == core, y // 2 + 2 * half == y)

    def send_last(summed_x):
        for k, (core, half, d, _) in enumerate(ends):
            if along_x(core, half) != summed_x:
                continue
            if d > 0:
                last_copy(k).start()
                continue

            @pl.when(jnp.logical_not(here(k)))
            def _(k=k):
                last_copy(k).start()

            @pl.when(here(k))
            def _(k=k):
                final[slot] = piece(k)[...]

    await_bytes(xa, xa_sem.at[1])
    slab_x[...] = part_ref[x, :, 0:X_ROWS, :] + xa[0] + xa[1] + xa[2]
    send_last(True)
    await_bytes(za, za_sem.at[1])
    total = part_ref[:, z, X_ROWS:32, :]
    for k in range(NZ - 1):
        total = total + za[k]
    slab_z[...] = total
    send_last(False)
    meanwhile()
    await_bytes(xa, xa_sem.at[0])
    await_bytes(za, za_sem.at[0])
    own = jnp.logical_or(y == 0, y == NY - 1)

    def await_pieces(count, sem):
        pl.when(own)(functools.partial(await_bytes, final.at[pl.ds(0, count - 1)], sem))
        pl.when(jnp.logical_not(own))(functools.partial(await_bytes, final.at[pl.ds(0, count)], sem))

    for summed_x in (True, False):

        @pl.when(by_x(c, y) if summed_x else jnp.logical_not(by_x(c, y)))
        def _(summed_x=summed_x):
            count = NZ if summed_x else NX
            await_pieces(4 * count, final_sem.at[1])
            for at in range(4):
                total = final[at]
                for d in range(1, count):
                    total = total + final[4 * d + at]
                out_ref[at // 2 * 8 : at // 2 * 8 + 8, at % 2 * IDX_DIM : (at % 2 + 1) * IDX_DIM] = total

    await_pieces(3 * NZ + NX, final_sem.at[0])


def by_x(c, y):
    return jnp.logical_or(c == 0, y < 2)


def whole_kernel(
    order, order_row, lat_any, idx_any, hw_any, mq_any, iq_any, out_ref,
    table, first_row, first, lat_ref, idx_ref, hw_ref, w_other, p_ref, q_ref, slots, stage_out, stage_in, idx32, idx_stage_out, idx_stage_in, idxg, slots32, sorted32, idx_keys,
    vmq, queries, keys, scores, tgt_ref, vidx, idx_q, w_ref, inner_ref, logit_ref, stat_ref, stats_ref, arrive,
    grad_ref, part_ref, xa, za, slab_x, slab_z, final,
    load_sem, pair_send, pair_recv, ring_send, ring_recv, idx_sem,
    tgt_sem, stat_sem, xa_sem, za_sem, final_sem,
):
    x, z, c, y = coords()
    seq = lax.axis_index("seq")
    me = x * NZ + z
    barrier = pltpu.get_barrier_semaphore()
    partner = (seq_at(x, z, 1 - c), y)
    peers_y = [(seq, (y + d) % NY) for d in range(1, NY)]
    peers_x = [(seq_at((x + d) % NX, z, c), y) for d in range(1, NX)]
    peers_z = [(seq_at(x, (z + d) % NZ, c), y) for d in range(1, NZ)]
    ring = {("x", 1): peers_x[0], ("x", -1): peers_x[-1], ("z", 1): peers_z[0], ("z", -1): peers_z[-1]}

    def tell(to):
        pl.semaphore_signal(barrier, inc=1, device_id=to, device_id_type=MESH)

    for to in peers_x + peers_z + peers_y + [partner]:
        tell(to)
    loads = [
        pltpu.make_async_copy(src, dst, load_sem.at[k])
        for k, (src, dst) in enumerate(
            [
                (lat_any, lat_ref), (idx_any, idx_ref), (hw_any, hw_ref), (iq_any.at[c], vidx.at[0]),
                (mq_any.at[c], vmq.at[0]),
            ]
        )
    ]
    for d in loads:
        d.start()
    for summed_x in (True, False):

        @pl.when(by_x(c, y) if summed_x else jnp.logical_not(by_x(c, y)))
        def _(summed_x=summed_x):
            for d, _, source, core in final_sources(x, z, y, summed_x):
                if d == 0:
                    pl.when(jnp.logical_or(core != c, source[1] != y))(functools.partial(tell, source))
                else:
                    tell(source)

    fill_table(order, seq, table)
    first_row[...] = jnp.broadcast_to(slots_of(order_row[...]), (8, HALVES))
    to_scalars = pltpu.make_async_copy(first_row, first, load_sem.at[5])
    to_scalars.start()
    for d in loads[:3]:
        d.wait()
    weights = weight_rows(hw_ref[...])
    for half in range(2):
        w_other[half] = jnp.where(c == 0, weights[1][half], weights[0][half])
        w_ref[half] = jnp.where(c == 0, weights[0][half], weights[1][half])
    lat = lat_ref[...]
    stage_out[:, 0:KD] = jnp.where(c == 0, lat[:, KD:], lat[:, :KD])
    stage_out[:, KD:] = jnp.zeros((TOK, KPAD - KD), BF16)
    idx32[...] = idx_ref[...].astype(F32)
    rows = jnp.concatenate(
        [idx32[pl.ds(pl.multiple_of(y * 8, 8), 8), :], idx32[pl.ds(pl.multiple_of(HALF + y * 8, 8), 8), :]], axis=0
    )
    idx_stage_out[...] = jnp.where(c == 0, rows[:, IDX_DIM:], rows[:, :IDX_DIM]).astype(BF16)
    own = jnp.where(jnp.logical_or(y == 0, y == NY - 1), 1, 0)
    pl.semaphore_wait(barrier, NX - 1 + NZ - 1 + NY - 1 + 1 + 3 * NZ + NX - own)

    def remote(src, dst, send, recv, to):
        d = pltpu.make_async_remote_copy(
            src_ref=src, dst_ref=dst, send_sem=send, recv_sem=recv, device_id=to, device_id_type=MESH
        )
        d.start()
        return d

    def to_partner(k, src, dst):
        return remote(src, dst, pair_send.at[k], pair_recv.at[k], partner)

    pair_copies = [
        to_partner(0, stage_out, stage_in),
        to_partner(1, idx_stage_out, idx_stage_in),
        to_partner(2, w_other, w_ref.at[pl.ds(2, 2)]),
    ]
    mine = jnp.where(c == 0, lat[:, :KD], lat[:, KD:])
    idx_mine = jnp.where(c == 0, rows[:, :IDX_DIM], rows[:, IDX_DIM:]).astype(BF16)
    pair_copies[0].wait_recv()
    pair_copies[1].wait_recv()
    from_partner = stage_in[:, :KD]
    both = jnp.concatenate([jnp.where(c == 0, mine, from_partner), jnp.where(c == 0, from_partner, mine)], axis=1)
    p_ref[me] = both[:HALF, :P_LANES]
    q_ref[me] = jnp.concatenate([both[HALF:], both[:HALF, P_LANES:]], axis=1)
    idx_other = idx_stage_in[...]
    idxg[x, z, 0:16] = jnp.where(c == 0, idx_mine, idx_other)
    idxg[x, z, 16:32] = jnp.where(c == 0, idx_other, idx_mine)

    counter = [0]
    live, origin = {}, {}
    landed = [(0, me, 0, HALF), (1, me, 0, HALF)]

    def send(part, axis, way, dx, dz, lo, hi):
        k = counter[0]
        counter[0] += 1

        def block(ox, oz):
            ref = q_ref if part else p_ref
            return ref.at[(x + ox + 2 * NX) % NX * NZ + (z + oz + 2 * NZ) % NZ, pl.ds(lo, hi - lo)]

        gone_sem = ring_send.at[k if k < 4 else 4 + part]
        out = remote(block(dx, dz), block(dx, dz), gone_sem, ring_recv.at[k], ring[(axis, way)])
        here = block(dx - way, dz) if axis == "x" else block(dx, dz - way)
        arrival = pltpu.make_async_remote_copy(
            src_ref=here, dst_ref=here, send_sem=gone_sem, recv_sem=ring_recv.at[k],
            device_id=ring[(axis, way)], device_id_type=MESH,
        )
        live[k] = [out, arrival, False]
        ix, iz = (dx - way, dz) if axis == "x" else (dx, dz - way)
        origin[k] = (part, (x + ix + 2 * NX) % NX * NZ + (z + iz + 2 * NZ) % NZ, lo, hi)
        return k

    def arrived(k):
        if not live[k][2]:
            live[k][1].wait_recv()
            live[k][2] = True
            landed.append(origin[k])

    def left(ks):
        for k in ks:
            live[k][0].wait_send()

    last_x, last_z = NX // 2, NZ // 2

    def hop(part, axis, dx, dz, step, before):
        last = last_x if axis == "x" else last_z
        ks = []
        for way, half in ((1, (0, 16)), (-1, (16, 32))):
            if before is not None:
                arrived(before[0 if way == 1 else 1])
            away = -way * (step - 1)
            ox, oz = (away, dz) if axis == "x" else (dx, away)
            lo, hi = half if step == last else (0, 32)
            ks.append(send(part, axis, way, ox, oz, lo, hi))
        return ks

    zp, xq, zq = {}, {}, {}

    def start_p(dx):
        zp[dx] = {1: hop(0, "z", dx, 0, 1, None)}

    def advance_p(dx, step):
        zp[dx][step] = hop(0, "z", dx, 0, step, zp[dx][step - 1])

    def advance_q(step):
        before = zq[step - 1]
        if step <= last_z:
            zq[step] = hop(1, "z", 0, 0, step, before)
        else:
            arrived(before[0])
            arrived(before[1])
        for dz in (-(step - 1), step - 1) if step <= last_z else (last_z,):
            xq[dz] = {1: hop(1, "x", 0, dz, 1, None)}

    def finish_q(dz):
        xq[dz][2] = hop(1, "x", 0, dz, 2, xq[dz][1])

    def start_index():
        for d in range(1, NZ):
            ref = idxg.at[x, z]
            remote(ref, ref, idx_sem.at[0], idx_sem.at[1], peers_z[d - 1])

    def spread_index():
        await_bytes(idxg.at[x, pl.ds(0, NZ - 1)], idx_sem.at[1])
        for d in range(1, NX):
            remote(idxg.at[x], idxg.at[x], idx_sem.at[2], idx_sem.at[3], peers_x[d - 1])

    def have_index():
        await_bytes(idxg.at[pl.ds(0, NX - 1)], idx_sem.at[3])
        pair_copies[2].wait_recv()
        to_scalars.wait()
        sort_index_keys(first, idxg, slots32, sorted32, idx_keys)

    logit_tops = [(jnp.full((8, 128), NEG, F32),) * 2 for _ in range(2)]

    def logits(pair, first, last):
        logit_tops[pair] = lax.fori_loop(
            first, last,
            lambda i, t: logit_step(table, pair, i, y, idx_keys, idx_q, w_ref, inner_ref, logit_ref, t),
            logit_tops[pair],
        )
        if last == ENTRIES:
            logit_stats(table, pair, logit_ref, stat_ref, logit_tops[pair])

    def send_stats():
        for d in range(1, NY):
            remote(stat_ref, stats_ref.at[d], stat_sem.at[0], stat_sem.at[1], peers_y[d - 1])
        stats_ref[0] = stat_ref[...]

    def own_queries():
        loads[4].wait()
        split_heads(0, vmq, queries)

    def own_index_queries():
        loads[3].wait()
        pair_copies.append(to_partner(3, iq_any.at[1 - c], vidx.at[1]))
        pair_copies.append(to_partner(4, mq_any.at[1 - c], vmq.at[1]))
        split_index_heads(0, vidx, idx_q)

    def other_index_queries():
        pair_copies[3].wait_recv()
        split_index_heads(1, vidx, idx_q)

    def other_queries():
        pair_copies[4].wait_recv()
        split_heads(1, vmq, queries)

    work = [own_index_queries, spread_index, own_queries, have_index]
    work += [functools.partial(logits, 0, k, k + 3) for k in (0, 3, 6)]
    work += [other_index_queries]
    work += [functools.partial(logits, 1, k, k + 3) for k in (0, 3, 6)]
    work += [send_stats, other_queries]

    def between():
        if work:
            work.pop(0)()
        for _ in range(min(4, len(landed))):
            split_cores(p_ref, q_ref, slots, *landed.pop(0))

    zq[1] = hop(1, "z", 0, 0, 1, None)
    xp = hop(0, "x", 0, 0, 1, None)
    left(zq[1])
    start_p(0)
    left(xp)
    xq[0] = {1: hop(1, "x", 0, 0, 1, None)}
    start_index()
    between()
    advance_q(2)
    xp2 = hop(0, "x", 0, 0, 2, xp)
    start_p(-1)
    start_p(1)
    between()
    advance_p(0, 2)
    finish_q(0)
    advance_q(3)
    arrived(xp2[0])
    arrived(xp2[1])
    start_p(2)
    between()
    advance_p(-1, 2)
    advance_p(1, 2)
    between()
    advance_p(0, 3)
    advance_q(4)
    finish_q(-1)
    finish_q(1)
    between()
    advance_p(2, 2)
    between()
    advance_p(-1, 3)
    advance_p(1, 3)
    advance_q(5)
    between()
    finish_q(-2)
    finish_q(2)
    advance_p(0, 4)
    between()
    advance_p(2, 3)
    between()
    advance_p(-1, 4)
    advance_p(1, 4)
    finish_q(-3)
    finish_q(3)
    between()
    advance_p(2, 4)
    finish_q(last_z)
    while work:
        between()
    for k in live:
        arrived(k)
        while landed:
            split_cores(p_ref, q_ref, slots, *landed.pop(0))
    sort_keys(first, slots, keys)

    def send_targets(pair, at):
        cut = pl.ds(4 * at, 12)
        for d in range(1, NY):
            remote(
                tgt_ref.at[(y + d) % NY, pair, cut], arrive.at[d - 1, pair, cut], tgt_sem.at[0],
                tgt_sem.at[1 + pair * 3 + at // 3], peers_y[d - 1],
            )

    for pair in range(2):
        targets(table, pair, keys, queries, scores, tgt_ref, send_targets)
    await_bytes(stats_ref.at[pl.ds(1, NY - 1)], stat_sem.at[1])
    for pair in range(2):
        norms = [norms_of(stats_ref, 2 * pair + half) for half in range(2)]

        def step(i, carry):
            gradient_step(
                table, pair, i, y, idx_q, w_ref, inner_ref, logit_ref, tgt_ref, arrive, norms, grad_ref
            )
            return carry

        for at in range(0, ENTRIES, 3):
            await_bytes(arrive.at[:, pair, pl.ds(4 * at, 12)], tgt_sem.at[1 + pair * 3 + at // 3])
            lax.fori_loop(at, at + 3, step, 0)
    collect_gradients(table, order, grad_ref, sorted32, part_ref)

    def settle():
        blocks = NX * NZ - 1 - 2
        await_bytes(p_ref.at[pl.ds(0, blocks)], ring_send.at[4])
        await_bytes(q_ref.at[pl.ds(0, blocks)], ring_send.at[5])
        await_bytes(idxg.at[x, pl.ds(0, NZ - 1)], idx_sem.at[0])
        await_bytes(idxg.at[pl.ds(0, NX - 1)], idx_sem.at[2])
        await_bytes(stats_ref.at[pl.ds(1, NY - 1)], stat_sem.at[0])
        await_bytes(arrive, tgt_sem.at[0])
        for d in pair_copies:
            d.wait_send()

    scatter(
        x, z, c, y, peers_x, peers_z, remote, part_ref, out_ref, xa, za, slab_x, slab_z, final,
        xa_sem, za_sem, final_sem, settle,
    )


RING_COPIES = 76


def whole_call(order, order_row, lat, idx, hw, mq, iq):
    any_spec = pl.BlockSpec(memory_space=pl.ANY)
    vmem = pl.BlockSpec(memory_space=pltpu.VMEM)
    smem = pl.BlockSpec(memory_space=pltpu.SMEM)
    dma = pltpu.SemaphoreType.DMA
    return pl.pallas_call(
        whole_kernel,
        name="indexer_key_gradient",
        out_shape=jax.ShapeDtypeStruct((16, 2 * IDX_DIM), F32),
        in_specs=[smem, vmem] + [any_spec] * 5,
        out_specs=vmem,
        scratch_shapes=[
            pltpu.SMEM((8 * ENTRIES,), jnp.int32),
            pltpu.VMEM((8, HALVES), jnp.int32),
            pltpu.SMEM((8, HALVES), jnp.int32),
            pltpu.VMEM((TOK, 2 * KD), BF16),
            pltpu.VMEM((TOK, 2 * IDX_DIM), BF16),
            pltpu.VMEM((TOK, 2 * IDX_HEADS), F32),
            pltpu.VMEM((2, 16, 128), F32),
            pltpu.VMEM((NX * NZ, HALF, P_LANES), BF16),
            pltpu.VMEM((NX * NZ, HALF, Q_LANES), BF16),
            pltpu.VMEM((HALVES, HALF, KPAD), BF16),
            pltpu.VMEM((TOK, KPAD), BF16),
            pltpu.VMEM((TOK, KPAD), BF16),
            pltpu.VMEM((TOK, 2 * IDX_DIM), F32),
            pltpu.VMEM((16, IDX_DIM), BF16),
            pltpu.VMEM((16, IDX_DIM), BF16),
            pltpu.VMEM((NX, NZ, 32, IDX_DIM), BF16),
            pltpu.VMEM((HALVES, 8, IDX_DIM), F32),
            pltpu.VMEM((HALVES, 8, IDX_DIM), F32),
            pltpu.VMEM((8, 128, IDX_DIM), BF16),
            pltpu.VMEM((2, TOK, HEADS_DEV * KD), BF16),
            pltpu.VMEM((4, LANES, KPAD), BF16),
            pltpu.VMEM((8, 512, KPAD), BF16),
            pltpu.VMEM((ENTRIES, 512, LANES), F32),
            pltpu.VMEM((NY, 2, SLOTS, 8, 128), F32),
            pltpu.VMEM((2, TOK, IDX_HEADS * IDX_DIM), BF16),
            pltpu.VMEM((4, IDX_HEADS * HALF, IDX_DIM), BF16),
            pltpu.VMEM((4, 16, 128), F32),
            pltpu.VMEM((2, ENTRIES, 128, IDX_HEADS * HALF), BF16),
            pltpu.VMEM((2, ENTRIES, 128, 128), F32),
            pltpu.VMEM((8, 128), F32),
            pltpu.VMEM((NY, 8, 128), F32),
            pltpu.VMEM((NY - 1, 2, SLOTS, 8, 128), F32),
            pltpu.VMEM((2, ENTRIES, 128, IDX_DIM), F32),
            pltpu.VMEM((NX, NZ, 32, IDX_DIM), F32),
            pltpu.VMEM((NX - 1, NZ, X_ROWS, IDX_DIM), F32),
            pltpu.VMEM((NZ - 1, NX, 32 - X_ROWS, IDX_DIM), F32),
            pltpu.VMEM((NZ, X_ROWS, IDX_DIM), F32),
            pltpu.VMEM((NX, 32 - X_ROWS, IDX_DIM), F32),
            pltpu.VMEM((4 * NZ, 8, IDX_DIM), F32),
            dma((6,)),
            dma((5,)),
            dma((5,)),
            dma((6,)),
            dma((RING_COPIES,)),
            dma((4,)),
            dma((7,)),
            dma((2,)),
            dma((2,)),
            dma((2,)),
            dma((2,)),
        ],
        compiler_params=pltpu.CompilerParams(
            collective_id=0, has_side_effects=True, vmem_limit_bytes=VMEM_BYTES
        ),
    )(order, order_row, lat, idx, hw, mq, iq)


def per_device(mla_queries, latent_keys, index_queries, index_keys, head_weights, block_order):
    row = block_order.reshape(1, HALVES)
    return whole_call(block_order, row, latent_keys, index_keys, head_weights, mla_queries, index_queries)


def solution(mesh):
    return jax.shard_map(
        per_device,
        mesh=mesh,
        in_specs=(
            P(None, "seq", "head"),
            P("seq", None),
            P(None, "seq", None),
            P("seq", None),
            P("seq", None),
            P(),
        ),
        out_specs=P(("seq", "head"), None),
        check_vma=False,
    )
```
